256 devices in a mesh: fsdp: 64 (over y, z_lo, x), dp: 4 (over z_hi, core).
Axes of the slice: x: 4, y: 4, z: 8 (z_hi: 2, z_lo: 4; z = z_hi * 4 + z_lo), core: 2. Of those that a mesh axis runs over, the one named last changes fastest.
Arguments:
- tokens: bfloat16 [32768, 2048], P(('fsdp', 'dp')), may hold values from -24 to 24
- cotangent: bfloat16 [32768, 2048], P(('fsdp', 'dp')), may hold values from -0.099121094 to 0.099121094
- saved_branch: bfloat16 [32768, 2048], P(('fsdp', 'dp')), may hold values from -6 to 6
- layer_gain: float32 [2048], replicated, may hold values from -3 to 3
- offsets: int32 [3], replicated, may hold values from 0 to 4225024, as said below
- master: float32 [4227072], P('fsdp'), may hold values from -0.006 to 0.006
- moment_one: float32 [4227072], P('fsdp'), may hold values from -6 to 6
- moment_two: float32 [4227072], P('fsdp'), may hold values from 0.5 to 20
- teacher: float32 [4227072], P('fsdp'), may hold values from -0.00012 to 0.00012
- teacher_tokens: bfloat16 [32768, 2048], P(('fsdp', 'dp')), may hold values from -6 to 6
Outputs:
- master_new: float32 [4227072], P('fsdp')
- moment_one_new: float32 [4227072], P('fsdp')
- moment_two_new: float32 [4227072], P('fsdp')
- teacher_new: float32 [4227072], P('fsdp')
- teacher_branch: bfloat16 [32768, 2048], P(('fsdp', 'dp'))
The draws below stay inside these ranges and needn't reach their ends.
Inputs may be any that keep to these rules, and one draw needn't show every extreme that they name: offsets[0] = 0; the projection (4194304 slots), the bias (2048) and the layer scale (2048) lie in that order without intersection, the layer scale at the bucket's end.
All inputs are finite; a program needn't handle non-finite values.
Results may differ from the reference program's by a relative error of at most 0.0056.
Values may be sent and summed in bfloat16 or wider, within the bound.
A program may use at most 128 MiB of HBM per device.

```python
import math
import jax
import jax.numpy as jnp
from jax import lax

WIN_IN = 2048
WIN_OUT = 2048
SLACK = 28672
STEP = 1000
ROWS = 32768
ROWS_T = 32768
BUCKET = 4227072


def draw_offsets(key, part):
    key = jax.random.fold_in(key, 7)
    units = jax.random.randint(key, (), 0, SLACK + 1)
    second = WIN_IN * WIN_OUT + units
    first = jnp.zeros((), jnp.int32)
    third = jnp.full((), BUCKET - WIN_OUT, jnp.int32)
    return jnp.stack([first, second.astype(jnp.int32), third]).astype(jnp.int32)


def raised(entries, stream_key, source, target, blocks, factor):
    def block_of(position):
        return (jnp.arange(entries.shape[position]) // (entries.shape[position] // blocks)).reshape((-1,) + (1,) * (entries.ndim - 1 - position))

    first = jax.random.permutation(stream_key, blocks)[block_of(target)]
    other_side = (block_of(target) + blocks // 2) % blocks
    return jnp.where((block_of(source) == first) | (block_of(source) == other_side), factor * entries, entries)


def steps_of(stream_key, extent, split, smallest, high):
    def one(position, blocks):
        heights = jax.random.uniform(jax.random.fold_in(jax.random.fold_in(stream_key, 6), position), (blocks,), jnp.float32, smallest / len(split), high / len(split))
        return jnp.repeat(jnp.exp(heights), extent[position] // blocks).reshape((-1,) + (1,) * (len(extent) - position - 1))

    loudness = one(*split[0])
    for cut in split[1:]:
        loudness = loudness * one(*cut)
    return loudness


def gaussian(stream_key, shape, spread, limit, split=(), kind=jnp.bfloat16):
    factor_of = steps_of(stream_key, shape, split, -0.22, 0.18) if split else 1.0
    drawn = jax.random.normal(stream_key, shape, jnp.float32) * spread * factor_of
    return jnp.minimum(jnp.maximum(drawn, -limit), limit).astype(kind)


def bell_draw_with(own_key, shape, width, reach, pieces, heavy, kind=jnp.bfloat16):
    drawn = width * jax.random.normal(own_key, shape, jnp.float32)
    if pieces:
        drawn = drawn * steps_of(own_key, shape, pieces, -0.22, 0.18)
    return jnp.clip(raised(drawn, jax.random.fold_in(own_key, 3), *heavy), -reach, reach).astype(kind)


def setup_inputs(seed: int = 0) -> dict:
    key_of = jax.random.split(jax.random.key(seed), 11)
    return {
        "tokens": bell_draw_with(key_of[0], (ROWS, WIN_IN), 1.0, 24.0, ((0, 256),), (0, 1, 256, 6.0)),
        "cotangent": gaussian(key_of[1], (ROWS, WIN_OUT), (3.0 / ROWS ** 0.5), 0.099121094, ((0, 256),)),
        "saved_branch": gaussian(key_of[2], (ROWS, WIN_OUT), 1.0, 6.0, ((0, 256),)),
        "layer_gain": gaussian(key_of[3], (WIN_OUT,), 1.0, 3.0, (), jnp.float32),
        "offsets": draw_offsets(jax.random.fold_in(key_of[10], 71), 0),
        "master": gaussian(key_of[5], (BUCKET,), 0.001, 0.006, ((0, 64),), jnp.float32),
        "moment_one": gaussian(key_of[6], (BUCKET,), 1.0, 6.0, ((0, 64),), jnp.float32),
        "moment_two": jnp.clip(jnp.exp(math.log(20.0) - 3.6888795 * jax.random.uniform(key_of[7], (BUCKET,), jnp.float32) ** steps_of(key_of[7], (BUCKET,), ((0, 64),), -0.2, 0.2)), 0.5, 20.0),
        "teacher": gaussian(key_of[8], (BUCKET,), 0.00002, 0.00012, ((0, 64),), jnp.float32),
        "teacher_tokens": gaussian(key_of[9], (ROWS_T, WIN_IN), 1.0, 6.0, ((0, 256),)),
    }


beta_one = 0.9
beta_two = 0.999
learn_rate = 0.001
decay_rate = 0.04
ema_rate = 0.994
epsilon = 1e-08

def reference(tokens, cotangent, saved_branch, layer_gain, offsets, master, moment_one, moment_two, teacher, teacher_tokens):
    cot_float = cotangent.astype(jnp.float32)
    weighted = (cot_float * layer_gain).astype(jnp.bfloat16)
    grad_proj = lax.dot_general(tokens, weighted, (((0,), (0,)), ((), ())), preferred_element_type=jnp.float32)
    grad_bias = lax.optimization_barrier(jnp.sum(cot_float * layer_gain, axis=0))
    grad_scale = lax.optimization_barrier(jnp.sum(cot_float * saved_branch.astype(jnp.float32), axis=0))
    grad = jnp.zeros((BUCKET,), jnp.float32)
    grad = lax.dynamic_update_slice(grad, grad_proj.reshape(-1), (offsets[0].astype(jnp.int32),))
    grad = lax.dynamic_update_slice(grad, grad_bias, (offsets[1].astype(jnp.int32),))
    grad = lax.dynamic_update_slice(grad, grad_scale, (offsets[2].astype(jnp.int32),))
    moment_one_new = beta_one * moment_one + (1.0 - beta_one) * grad
    moment_two_new = beta_two * moment_two + (1.0 - beta_two) * grad * grad
    first = moment_one_new / (1.0 - beta_one ** STEP)
    second = moment_two_new / (1.0 - beta_two ** STEP)
    places = jnp.arange(BUCKET, dtype=jnp.int32)
    start = offsets[0].astype(jnp.int32)
    inside = jnp.logical_and(places >= start, places < start + WIN_IN * WIN_OUT)
    mask = jnp.where(inside, 1.0, 0.0).astype(jnp.float32)
    master_new = master - learn_rate * (first / (jnp.sqrt(second) + epsilon) + decay_rate * mask * master)
    teacher_new = ema_rate * teacher + (1.0 - ema_rate) * master_new
    teacher_low = teacher_new.astype(jnp.bfloat16)
    proj_t = lax.dynamic_slice(teacher_low, (offsets[0].astype(jnp.int32),), (WIN_IN * WIN_OUT,)).reshape(WIN_IN, WIN_OUT)
    bias_t = lax.dynamic_slice(teacher_low, (offsets[1].astype(jnp.int32),), (WIN_OUT,)).astype(jnp.float32)
    scale_t = lax.dynamic_slice(teacher_low, (offsets[2].astype(jnp.int32),), (WIN_OUT,)).astype(jnp.float32)
    product = jnp.dot(teacher_tokens, proj_t, preferred_element_type=jnp.float32)
    teacher_branch = (scale_t * (product + bias_t)).astype(jnp.bfloat16)
    return (master_new, moment_one_new, moment_two_new, teacher_new, teacher_branch)
```

```python
import functools

import jax
import jax.numpy as jnp
from jax import lax
from jax.experimental import pallas as pl
from jax.experimental.pallas import tpu as pltpu
from jax.sharding import PartitionSpec as P

MESH = pl.DeviceIdType.MESH
F32 = jnp.float32
BF16 = jnp.bfloat16

STEP = 1000
beta_one = 0.9
beta_two = 0.999
learn_rate = 0.001
decay_rate = 0.04
ema_rate = 0.994
epsilon = 1e-08

WIDTH = 2048
WINDOW = 640
PROJ = WIDTH * WIDTH
SHARD = 66048
FLAT = SHARD // 128
TAIL_ROW = 260


def wrap(value, size):
    return lax.rem(value + size, size)


def device(x, y, z, c):
    return (y * 16 + lax.rem(z, 4) * 4 + x, lax.div(z, 4) * 2 + c)


def window_start(y):
    return pl.multiple_of(jnp.minimum(512 * y, WIDTH - WINDOW), 128)


def remote(src, dst, send, recv, to):
    return pltpu.make_async_remote_copy(
        src_ref=src, dst_ref=dst, send_sem=send, recv_sem=recv, device_id=to, device_id_type=MESH
    )


def bit_of(vector, bit):
    return lax.rem(lax.div(vector, 2**bit), 2) == 1


def roll_by(value, amount, axis, bits):
    for bit in bits:
        on = jnp.broadcast_to(bit_of(amount, bit), value.shape)
        value = jnp.where(on, pltpu.roll(value, 2 ** (bit - bits[0]), axis), value)
    return value


def shift_rows(value, amount):
    for bit in range(3):
        on = lax.rem(lax.div(amount, 2**bit), 2) == 1
        value = jnp.where(on, pltpu.roll(value, value.shape[0] - 2**bit, 0), value)
    return value


def rows_from(ref, start, count):
    base = pl.multiple_of(lax.div(start, 8) * 8, 8)
    return shift_rows(ref[pl.ds(base, count + 8), :], start - base)[:count]


def kernel(
    spot, gain, tokens, cot, saved, master, one, two, teacher,
    master_out, one_out, two_out, teacher_out,
    T, C, SL, SS, prod, zs, cr, zb, zr, xs, xr, pad, tg,
    own_sem, a1s, a1r, b1s, b1r, s1s, s1r, s2s, s2r, a2s, a2r, b2s, b2r, cs, crs, zss, zrs, xss, xrs,
):
    f = lax.axis_index("fsdp")
    p = lax.axis_index("dp")
    x = lax.rem(f, 4)
    zl = lax.rem(lax.div(f, 4), 4)
    y = lax.div(f, 16)
    c = lax.rem(p, 2)
    z = lax.div(p, 2) * 4 + zl

    def at(dx=0, dy=0, dz=0, dc=0):
        return device(wrap(x + dx, 4), wrap(y + dy, 4), wrap(z + dz, 8), wrap(c + dc, 2))

    partners = (
        [dict(dx=d) for d in (1, 2, 3)]
        + [dict(dy=d) for d in (1, 2, 3)]
        + [dict(dz=d) for d in range(1, 8)]
        + [dict(dx=d, dc=1) for d in range(4)]
    )
    barrier = pltpu.get_barrier_semaphore()
    for partner in partners:
        pl.semaphore_signal(barrier, inc=1, device_id=at(**partner), device_id_type=MESH)
    pl.semaphore_wait(barrier, len(partners))

    pending = []

    def send(copy):
        copy.start()
        pending.append(copy)

    mine = [
        pltpu.make_async_copy(tokens.at[:, pl.ds(window_start(y), WINDOW)], T.at[y, x], own_sem.at[0]),
        pltpu.make_async_copy(cot.at[:, pl.ds(pl.multiple_of(512 * x, 128), 512)], C.at[y, x], own_sem.at[1]),
    ]
    for copy in mine:
        copy.start()
    for d in (1, 2, 3):
        to_y = wrap(y + d, 4)
        send(remote(tokens.at[:, pl.ds(window_start(to_y), WINDOW)], T.at[y, x], a1s.at[d - 1], a1r.at[d - 1], at(dy=d)))
        to_x = wrap(x + d, 4)
        send(remote(cot.at[:, pl.ds(pl.multiple_of(512 * to_x, 128), 512)], C.at[y, x], b1s.at[d - 1], b1r.at[d - 1], at(dx=d)))
    for copy in mine:
        copy.wait()

    low, high = pl.ds(0, 64), pl.ds(64, 64)

    def spread_token(d):
        row = wrap(y - d, 4)
        for k, (half, dx) in enumerate([(low, 1), (high, 1), (high, -1), (low, -1)]):
            ref = T.at[row, x, half]
            send(remote(ref, ref, a2s.at[d, k], a2r.at[d, k], at(dx=dx)))

    def spread_cot(d):
        col = wrap(x - d, 4)
        for k, (half, dy) in enumerate([(low, 1), (high, 1), (high, -1), (low, -1)]):
            ref = C.at[y, col, half]
            send(remote(ref, ref, b2s.at[d, k], b2r.at[d, k], at(dy=dy)))

    def token_wait(d, k):
        half, dx = [(low, -1), (high, -1), (high, 1), (low, 1), (low, -2), (high, 2)][k]
        ref = T.at[wrap(y - d, 4), wrap(x + dx, 4), half]
        remote(ref, ref, a2s.at[d, k], a2r.at[d, k], at(dx=1)).wait_recv()
        return ref

    def cot_wait(d, k):
        half, dy = [(low, -1), (high, -1), (high, 1), (low, 1), (low, -2), (high, 2)][k]
        ref = C.at[wrap(y + dy, 4), wrap(x - d, 4), half]
        remote(ref, ref, b2s.at[d, k], b2r.at[d, k], at(dy=1)).wait_recv()
        return ref

    def relay(d):
        ref = token_wait(d, 0)
        send(remote(ref, ref, a2s.at[d, 4], a2r.at[d, 4], at(dx=1)))
        ref = cot_wait(d, 0)
        send(remote(ref, ref, b2s.at[d, 4], b2r.at[d, 4], at(dy=1)))
        ref = token_wait(d, 2)
        send(remote(ref, ref, a2s.at[d, 5], a2r.at[d, 5], at(dx=-1)))
        ref = cot_wait(d, 2)
        send(remote(ref, ref, b2s.at[d, 5], b2r.at[d, 5], at(dy=-1)))

    spread_token(0)
    spread_cot(0)

    total = jnp.zeros((1, WIDTH), F32)
    for r in range(0, 128, 16):
        total += jnp.sum(cot[r : r + 16].astype(F32) * saved[r : r + 16].astype(F32), axis=0, keepdims=True)
    top = total.astype(BF16)
    rest = (total - top.astype(F32)).astype(BF16)
    rows16 = lax.broadcasted_iota(jnp.int32, (16, WIDTH), 0)
    both = jnp.where(rows16 == 0, top.astype(F32), jnp.where(rows16 == 1, rest.astype(F32), 0.0)).astype(BF16)
    for q in range(4):
        SS[q] = both[:, 512 * q : 512 * q + 512]
    for d in (1, 2, 3):
        send(remote(SS.at[wrap(x + d, 4)], SL.at[y, x], s1s.at[d - 1], s1r.at[d - 1], at(dx=d)))
    SL[y, x] = SS[x]

    for d in (1, 2, 3):
        ref = T.at[wrap(y - d, 4), x]
        remote(ref, ref, a1s.at[d - 1], a1r.at[d - 1], at(dy=d)).wait_recv()
        spread_token(d)
        ref = C.at[y, wrap(x - d, 4)]
        remote(ref, ref, b1s.at[d - 1], b1r.at[d - 1], at(dx=d)).wait_recv()
        spread_cot(d)
        relay(d - 1)
    for d in (1, 2, 3):
        ref = SL.at[y, wrap(x - d, 4)]
        remote(ref, ref, s1s.at[d - 1], s1r.at[d - 1], at(dx=d)).wait_recv()
    for d in (1, 2, 3):
        send(remote(SL.at[y], SL.at[y], s2s.at[d - 1], s2r.at[d - 1], at(dy=d)))
    relay(3)
    for d in range(4):
        for k in (1, 3, 4, 5):
            token_wait(d, k)
            cot_wait(d, k)
    for d in (1, 2, 3):
        ref = SL.at[wrap(y - d, 4)]
        remote(ref, ref, s2s.at[d - 1], s2r.at[d - 1], at(dy=d)).wait_recv()

    prod[...] = jnp.zeros_like(prod)
    ones = jnp.ones((16, 512), BF16)

    def multiply(k, sums):
        left = T[k].reshape(512, WINDOW)
        right = C[k].reshape(512, 512)
        prod[0:WINDOW] += lax.dot_general(left, right, (((0,), (0,)), ((), ())), preferred_element_type=F32)
        return sums + jnp.dot(ones, right, preferred_element_type=F32)

    cot_sum = lax.fori_loop(0, 4, multiply, jnp.zeros((16, 512), F32))
    scale_sum = jnp.zeros((1, 512), F32)
    for i in range(4):
        for k in range(4):
            scale_sum += jnp.sum(SL[i, k].astype(F32), axis=0, keepdims=True)
    weight = gain[:, pl.ds(pl.multiple_of(512 * x, 128), 512)]
    first_row = 516 * y - window_start(y)
    rows = lax.broadcasted_iota(jnp.int32, (16, 512), 0)
    for k in range(4):
        for i in range(4):
            start = first_row + 129 * k + 32 * i + jnp.where(x < i, 1, 0)
            zs[k, 32 * i : 32 * i + 32] = (rows_from(prod, start, 32) * weight).astype(BF16)
        extra = rows_from(prod, first_row + 129 * k + 32 * x + 32, 8)[0:1] * weight
        block = jnp.where(
            rows == 0, extra, jnp.where(rows == 1, cot_sum * weight, jnp.where(rows == 2, scale_sum, 0.0))
        )
        zs[k, 128:144] = block.astype(BF16)

    keep = pl.ds(pl.multiple_of(256 * c, 128), 256)
    give = pl.ds(pl.multiple_of(256 * (1 - c), 128), 256)
    across = remote(zs.at[:, :, give], cr, cs.at[0], crs.at[0], at(dc=1))
    send(across)
    across.wait_recv()
    for k in range(4):
        zb[k] = (zs[k, :, keep].astype(F32) + cr[k].astype(F32)).astype(BF16)

    for d in range(1, 8):
        send(remote(zb.at[lax.rem(z + d, 4)], zr.at[z], zss.at[d - 1], zrs.at[d - 1], at(dz=d)))
    zr[z] = zb[zl]
    for d in range(1, 8):
        ref = zr.at[wrap(z - d, 8)]
        remote(ref, ref, zss.at[d - 1], zrs.at[d - 1], at(dz=d)).wait_recv()
    group = zr[0].astype(F32)
    for k in range(1, 8):
        group += zr[k].astype(F32)

    for i in range(4):
        xs[i, 0:32] = group[32 * i : 32 * i + 32]
        xs[i, 32:40] = group[128:136]
    slot = 2 * x + c
    n = 0
    for dx in range(4):
        for dc in range(2):
            if dx or dc:
                send(remote(xs.at[wrap(x + dx, 4)], xr.at[slot], xss.at[n], xrs.at[n], at(dx=dx, dc=dc)))
                n += 1
    xr[slot] = xs[x]
    n = 0
    for dx in range(4):
        for dc in range(2):
            if dx or dc:
                ref = xr.at[2 * wrap(x - dx, 4) + wrap(c - dc, 2)]
                remote(ref, ref, xss.at[n], xrs.at[n], at(dx=dx, dc=dc)).wait_recv()
                n += 1

    last = jnp.where(f == 63, 1.0, 0.0).astype(F32)
    place = spot[0:1]
    pad[...] = jnp.zeros_like(pad)
    tg[...] = jnp.zeros_like(tg)
    for q in range(4):
        for h in range(2):
            for t in range(2):
                k = 4 * q + 2 * h + t
                pad[k : k + 1] = xr[2 * q + h, 33:34, 128 * t : 128 * t + 128] * last
                tg[TAIL_ROW + 240 + k : TAIL_ROW + 241 + k] = xr[2 * q + h, 34:35, 128 * t : 128 * t + 128] * last
    rolled = roll_by(pad[0:24], place, 1, range(7))
    lanes = lax.broadcasted_iota(jnp.int32, (24, 128), 1)
    pad[0:24] = jnp.where(lanes >= lax.rem(place, 128), rolled, pltpu.roll(rolled, 1, 0))
    tg[TAIL_ROW : TAIL_ROW + 256] += roll_by(pad[...], place, 0, range(7, 15))

    limit = PROJ - SHARD * f
    lanes = lax.broadcasted_iota(jnp.int32, (8, 128), 1)
    subs = lax.broadcasted_iota(jnp.int32, (8, 128), 0)

    def update(where, grad, inside):
        old = master[where]
        new_one = beta_one * one[where] + (1.0 - beta_one) * grad
        new_two = beta_two * two[where] + (1.0 - beta_two) * grad * grad
        first = new_one / (1.0 - beta_one**STEP)
        second = new_two / (1.0 - beta_two**STEP)
        decay = jnp.where(inside, decay_rate, 0.0) * old
        new = old - learn_rate * (first / (jnp.sqrt(second) + epsilon) + decay)
        master_out[where] = new
        one_out[where] = new_one
        two_out[where] = new_two
        teacher_out[where] = ema_rate * teacher[where] + (1.0 - ema_rate) * new

    for b in range(4):
        for m in range(4):
            q = wrap(x + m, 4)
            for t in range(4):
                base = 128 * b + 4 * m + t
                where = (pl.ds(base, 8, stride=16), slice(None))
                grad = xr[2 * q + t // 2, 8 * b : 8 * b + 8, 128 * (t % 2) : 128 * (t % 2) + 128]
                slots = 128 * base + 2048 * subs + lanes
                update(where, grad + tg[where], slots < limit)
    for t in range(4):
        where = (slice(512 + t, 513 + t), slice(None))
        grad = xr[2 * x + t // 2, 32:33, 128 * (t % 2) : 128 * (t % 2) + 128]
        update(where, grad * (1.0 - last) + tg[where], jnp.full((1, 128), 65536, jnp.int32) < limit)

    for copy in pending:
        copy.wait_send()


def step_kernel(tokens, cot, saved, gain, offsets, master, one, two, teacher):
    vmem = pl.BlockSpec(memory_space=pltpu.VMEM)
    anyspace = pl.BlockSpec(memory_space=pl.ANY)
    dma = pltpu.SemaphoreType.DMA
    flat = jax.ShapeDtypeStruct((FLAT, 128), F32)
    return pl.pallas_call(
        kernel,
        out_shape=[flat] * 4,
        in_specs=[vmem, vmem, anyspace, vmem, vmem, vmem, vmem, vmem, vmem],
        out_specs=[vmem] * 4,
        scratch_shapes=[
            pltpu.VMEM((4, 4, 128, WINDOW), BF16),
            pltpu.VMEM((4, 4, 128, 512), BF16),
            pltpu.VMEM((4, 4, 16, 512), BF16),
            pltpu.VMEM((4, 16, 512), BF16),
            pltpu.VMEM((WINDOW + 32, 512), F32),
            pltpu.VMEM((4, 144, 512), BF16),
            pltpu.VMEM((4, 144, 256), BF16),
            pltpu.VMEM((4, 144, 256), BF16),
            pltpu.VMEM((8, 144, 256), BF16),
            pltpu.VMEM((4, 40, 256), F32),
            pltpu.VMEM((8, 40, 256), F32),
            pltpu.VMEM((256, 128), F32),
            pltpu.VMEM((520, 128), F32),
            dma((2,)), dma((3,)), dma((3,)), dma((3,)), dma((3,)), dma((3,)), dma((3,)), dma((3,)), dma((3,)),
            dma((4, 6)), dma((4, 6)), dma((4, 6)), dma((4, 6)),
            dma((1,)), dma((1,)), dma((7,)), dma((7,)), dma((7,)), dma((7,)),
        ],
        compiler_params=pltpu.CompilerParams(
            collective_id=0, has_side_effects=True, vmem_limit_bytes=40 << 20
        ),
        name="step",
    )(jnp.full((8, 128), offsets[1] - PROJ, jnp.int32), gain, tokens, cot, saved, master, one, two, teacher)


def per_device(
    tokens, cotangent, saved_branch, layer_gain, offsets, master, moment_one, moment_two, teacher, teacher_tokens
):
    width_in = width_out = WIDTH
    start_proj, start_bias, start_scale = offsets[0], offsets[1], offsets[2]
    flat = [a.reshape(FLAT, 128) for a in (master, moment_one, moment_two, teacher)]
    outs = step_kernel(tokens, cotangent, saved_branch, layer_gain.reshape(1, WIDTH), offsets, *flat)
    master_new, moment_one_new, moment_two_new, teacher_new = [a.reshape(SHARD) for a in outs]
    teacher_low = teacher_new.astype(BF16)
    gathered = lax.all_gather(teacher_low, "fsdp", axis=0, tiled=True)
    proj_t = lax.dynamic_slice(gathered, (start_proj,), (width_in * width_out,)).reshape(width_in, width_out)
    bias_t = lax.dynamic_slice(gathered, (start_bias,), (width_out,)).astype(F32)
    scale_t = lax.dynamic_slice(gathered, (start_scale,), (width_out,)).astype(F32)
    product = jnp.dot(teacher_tokens, proj_t, preferred_element_type=F32)
    teacher_branch = (scale_t * (product + bias_t)).astype(BF16)
    return (master_new, moment_one_new, moment_two_new, teacher_new, teacher_branch)


def solution(mesh):
    rows = P(("fsdp", "dp"), None)
    return jax.shard_map(
        per_device,
        mesh=mesh,
        in_specs=(rows, rows, rows, P(), P(), P("fsdp"), P("fsdp"), P("fsdp"), P("fsdp"), rows),
        out_specs=(P("fsdp"), P("fsdp"), P("fsdp"), P("fsdp"), rows),
        check_vma=False,
    )
```

```python
import functools

import jax
import jax.numpy as jnp
from jax import lax
from jax.experimental import pallas as pl
from jax.experimental.pallas import tpu as pltpu
from jax.sharding import PartitionSpec as P

MESH = pl.DeviceIdType.MESH
F32 = jnp.float32
BF16 = jnp.bfloat16

STEP = 1000
beta_one = 0.9
beta_two = 0.999
learn_rate = 0.001
decay_rate = 0.04
ema_rate = 0.994
epsilon = 1e-08

WIDTH = 2048
WINDOW = 640
PROJ = WIDTH * WIDTH
SHARD = 66048
FLAT = SHARD // 128
TAIL_ROW = 260


def wrap(value, size):
    return lax.rem(value + size, size)


def device(x, y, z, c):
    return (y * 16 + lax.rem(z, 4) * 4 + x, lax.div(z, 4) * 2 + c)


def window_start(y):
    return pl.multiple_of(jnp.minimum(512 * y, WIDTH - WINDOW), 128)


def remote(src, dst, send, recv, to):
    return pltpu.make_async_remote_copy(
        src_ref=src, dst_ref=dst, send_sem=send, recv_sem=recv, device_id=to, device_id_type=MESH
    )


def bit_of(vector, bit):
    return lax.rem(lax.div(vector, 2**bit), 2) == 1


def roll_by(value, amount, axis, bits):
    for bit in bits:
        on = jnp.broadcast_to(bit_of(amount, bit), value.shape)
        value = jnp.where(on, pltpu.roll(value, 2 ** (bit - bits[0]), axis), value)
    return value


def shift_rows(value, amount):
    for bit in range(3):
        on = lax.rem(lax.div(amount, 2**bit), 2) == 1
        value = jnp.where(on, pltpu.roll(value, value.shape[0] - 2**bit, 0), value)
    return value


def rows_from(ref, start, count):
    base = pl.multiple_of(lax.div(start, 8) * 8, 8)
    return shift_rows(ref[pl.ds(base, count + 8), :], start - base)[:count]


def kernel(
    spot_hbm, gain_hbm, tokens, cot_hbm, saved_hbm, master_hbm, one_hbm, two_hbm, teacher_hbm, tt_hbm,
    master_res, one_res, two_res, teacher_res, branch_res,
    spot, gain, cot, saved, master, one, two, teacher, master_out, one_out, two_out, teacher_out,
    T, C, SL, SS, prod, zs, cr, zb, zr, xs, xr, pad, tg, TT, S, TP, WF, WS, W, OUT,
    in_sem, res_sem, own_sem, a1s, a1r, b1s, b1r, s1s, s1r, s2s, s2r, a2s, a2r, b2s, b2r, cs, crs, zss, zrs, xss, xrs,
    ts, tr, w1s, w1r, w2s, w2r, w3s, w3r, os, orr,
):
    f = lax.axis_index("fsdp")
    p = lax.axis_index("dp")
    x = lax.rem(f, 4)
    zl = lax.rem(lax.div(f, 4), 4)
    y = lax.div(f, 16)
    c = lax.rem(p, 2)
    z = lax.div(p, 2) * 4 + zl

    def at(dx=0, dy=0, dz=0, dc=0):
        return device(wrap(x + dx, 4), wrap(y + dy, 4), wrap(z + dz, 8), wrap(c + dc, 2))

    partners = (
        [dict(dx=d) for d in (1, 2, 3)]
        + [dict(dy=d) for d in (1, 2, 3)]
        + [dict(dz=d) for d in range(1, 8)]
        + [dict(dx=d, dc=1) for d in range(4)]
        + [dict(dy=d, dc=1) for d in (1, 2, 3)]
    )
    loads = [
        pltpu.make_async_copy(src, dst, in_sem.at[k])
        for k, (src, dst) in enumerate(
            [
                (cot_hbm, cot), (saved_hbm, saved), (tt_hbm, TT.at[jnp.where(c == 0, x, y), c]), (gain_hbm, gain),
                (spot_hbm, spot), (master_hbm, master), (one_hbm, one), (two_hbm, two), (teacher_hbm, teacher),
            ]
        )
    ]
    for copy in loads:
        copy.start()
    barrier = pltpu.get_barrier_semaphore()
    for partner in partners:
        pl.semaphore_signal(barrier, inc=1, device_id=at(**partner), device_id_type=MESH)
    pl.semaphore_wait(barrier, len(partners))

    pending = []

    def send(copy):
        copy.start()
        pending.append(copy)

    mine = [
        pltpu.make_async_copy(tokens.at[:, pl.ds(window_start(y), WINDOW)], T.at[y, x], own_sem.at[0]),
        pltpu.make_async_copy(cot_hbm.at[:, pl.ds(pl.multiple_of(512 * x, 128), 512)], C.at[y, x], own_sem.at[1]),
    ]
    for copy in mine:
        copy.start()
    for d in (1, 2, 3):
        to_y = wrap(y + d, 4)
        send(remote(tokens.at[:, pl.ds(window_start(to_y), WINDOW)], T.at[y, x], a1s.at[d - 1], a1r.at[d - 1], at(dy=d)))
        to_x = wrap(x + d, 4)
        send(remote(cot_hbm.at[:, pl.ds(pl.multiple_of(512 * to_x, 128), 512)], C.at[y, x], b1s.at[d - 1], b1r.at[d - 1], at(dx=d)))
    for copy in mine:
        copy.wait()

    low, high = pl.ds(0, 64), pl.ds(64, 64)

    def spread_token(d):
        row = wrap(y - d, 4)
        for k, (half, dx) in enumerate([(low, 1), (high, 1), (high, -1), (low, -1)]):
            ref = T.at[row, x, half]
            send(remote(ref, ref, a2s.at[d, k], a2r.at[d, k], at(dx=dx)))

    def spread_cot(d):
        col = wrap(x - d, 4)
        for k, (half, dy) in enumerate([(low, 1), (high, 1), (high, -1), (low, -1)]):
            ref = C.at[y, col, half]
            send(remote(ref, ref, b2s.at[d, k], b2r.at[d, k], at(dy=dy)))

    def token_wait(d, k):
        half, dx = [(low, -1), (high, -1), (high, 1), (low, 1), (low, -2), (high, 2)][k]
        ref = T.at[wrap(y - d, 4), wrap(x + dx, 4), half]
        remote(ref, ref, a2s.at[d, k], a2r.at[d, k], at(dx=1)).wait_recv()
        return ref

    def cot_wait(d, k):
        half, dy = [(low, -1), (high, -1), (high, 1), (low, 1), (low, -2), (high, 2)][k]
        ref = C.at[wrap(y + dy, 4), wrap(x - d, 4), half]
        remote(ref, ref, b2s.at[d, k], b2r.at[d, k], at(dy=1)).wait_recv()
        return ref

    def relay(d):
        ref = token_wait(d, 0)
        send(remote(ref, ref, a2s.at[d, 4], a2r.at[d, 4], at(dx=1)))
        ref = cot_wait(d, 0)
        send(remote(ref, ref, b2s.at[d, 4], b2r.at[d, 4], at(dy=1)))
        ref = token_wait(d, 2)
        send(remote(ref, ref, a2s.at[d, 5], a2r.at[d, 5], at(dx=-1)))
        ref = cot_wait(d, 2)
        send(remote(ref, ref, b2s.at[d, 5], b2r.at[d, 5], at(dy=-1)))

    spread_token(0)
    spread_cot(0)

    a_own = jnp.where(c == 0, x, y)
    a_twin = jnp.where(c == 0, y, x)
    q = jnp.where(c == 0, lax.div(x, 2), 2 + lax.div(y, 2))

    def ring(d):
        return device(
            jnp.where(c == 0, wrap(x + d, 4), x), jnp.where(c == 0, y, wrap(y + d, 4)), z, c
        )

    def cross(d):
        return device(
            jnp.where(c == 0, x, wrap(x + d, 4)), jnp.where(c == 0, wrap(y + d, 4), y), z, c
        )

    loads[2].wait()
    send(remote(tt_hbm, TT.at[a_twin, c], ts.at[0, 6], tr.at[0, 6], at(dc=1)))

    HALVES = [(low, 1), (high, 1), (high, -1), (low, -1)]

    def spread_teacher(n, core):
        for k, (half, d) in enumerate(HALVES):
            ref = TT.at[a_own, core, half]
            send(remote(ref, ref, ts.at[n, k], tr.at[n, k], ring(d)))

    def teacher_wait(n, core, k):
        half, d = [(low, -1), (high, -1), (high, 1), (low, 1), (low, -2), (high, 2)][k]
        ref = TT.at[wrap(a_own + d, 4), core, half]
        remote(ref, ref, ts.at[n, k], tr.at[n, k], ring(1)).wait_recv()
        return ref

    def relay_teacher(n, core):
        for k, d in ((0, 1), (2, -1)):
            ref = teacher_wait(n, core, k)
            send(remote(ref, ref, ts.at[n, 4 + k // 2], tr.at[n, 4 + k // 2], ring(d)))

    def one_hot(g, carry):
        col = lax.broadcasted_iota(jnp.int32, (1, 384), 1)
        place = lax.rem(col, 192)
        i, r = lax.div(place, 48), lax.rem(place, 48)
        source = 129 * (2 * g + lax.div(col, 192)) + 32 * i + r - jnp.minimum(256 * g, WIDTH - 384)
        source = source + jnp.where(jnp.logical_and(r < 32, i > q), 1, 0)
        source = jnp.where(jnp.logical_or(r < 32, jnp.logical_and(r == 32, i == q)), source, -1)
        row = lax.broadcasted_iota(jnp.int32, (384, 384), 0)
        S[g] = jnp.where(row == source, 1.0, 0.0).astype(BF16)
        return carry

    lax.fori_loop(0, 8, one_hot, 0)

    def arrange(a):
        def group(g, carry):
            start = pl.multiple_of(jnp.minimum(256 * g, WIDTH - 384), 128)
            for core in range(2):
                part = jnp.dot(TT[a, core, :, pl.ds(start, 384)], S[g], preferred_element_type=F32)
                TP[g, a, core] = part.astype(BF16)
            return carry

        lax.fori_loop(0, 8, group, 0)

    loads[0].wait()
    loads[1].wait()
    total = jnp.zeros((1, WIDTH), F32)
    for r in range(0, 128, 16):
        total += jnp.sum(cot[r : r + 16].astype(F32) * saved[r : r + 16].astype(F32), axis=0, keepdims=True)
    top = total.astype(BF16)
    rest = (total - top.astype(F32)).astype(BF16)
    rows16 = lax.broadcasted_iota(jnp.int32, (16, WIDTH), 0)
    both = jnp.where(rows16 == 0, top.astype(F32), jnp.where(rows16 == 1, rest.astype(F32), 0.0)).astype(BF16)
    for q in range(4):
        SS[q] = both[:, 512 * q : 512 * q + 512]
    for d in (1, 2, 3):
        send(remote(SS.at[wrap(x + d, 4)], SL.at[y, x], s1s.at[d - 1], s1r.at[d - 1], at(dx=d)))
    SL[y, x] = SS[x]

    for d in (1, 2, 3):
        ref = T.at[wrap(y - d, 4), x]
        remote(ref, ref, a1s.at[d - 1], a1r.at[d - 1], at(dy=d)).wait_recv()
        spread_token(d)
        ref = C.at[y, wrap(x - d, 4)]
        remote(ref, ref, b1s.at[d - 1], b1r.at[d - 1], at(dx=d)).wait_recv()
        spread_cot(d)
        relay(d - 1)
    for d in (1, 2, 3):
        ref = SL.at[y, wrap(x - d, 4)]
        remote(ref, ref, s1s.at[d - 1], s1r.at[d - 1], at(dx=d)).wait_recv()
    for d in (1, 2, 3):
        send(remote(SL.at[y], SL.at[y], s2s.at[d - 1], s2r.at[d - 1], at(dy=d)))
    relay(3)
    spread_teacher(0, c)
    ref = TT.at[a_own, 1 - c]
    remote(ref, ref, ts.at[0, 6], tr.at[0, 6], at(dc=1)).wait_recv()
    spread_teacher(1, 1 - c)
    for d in range(4):
        for k in (1, 3, 4, 5):
            token_wait(d, k)
            cot_wait(d, k)
    for d in (1, 2, 3):
        ref = SL.at[wrap(y - d, 4)]
        remote(ref, ref, s2s.at[d - 1], s2r.at[d - 1], at(dy=d)).wait_recv()

    loads[3].wait()
    prod[...] = jnp.zeros_like(prod)
    ones = jnp.ones((16, 512), BF16)

    def multiply(k, sums):
        left = T[k].reshape(512, WINDOW)
        right = C[k].reshape(512, 512)
        prod[0:WINDOW] += lax.dot_general(left, right, (((0,), (0,)), ((), ())), preferred_element_type=F32)
        return sums + jnp.dot(ones, right, preferred_element_type=F32)

    cot_sum = lax.fori_loop(0, 4, multiply, jnp.zeros((16, 512), F32))
    scale_sum = jnp.zeros((1, 512), F32)
    for i in range(4):
        for k in range(4):
            scale_sum += jnp.sum(SL[i, k].astype(F32), axis=0, keepdims=True)
    weight = gain[:, pl.ds(pl.multiple_of(512 * x, 128), 512)]
    first_row = 516 * y - window_start(y)
    rows = lax.broadcasted_iota(jnp.int32, (16, 512), 0)
    for k in range(4):
        for i in range(4):
            start = first_row + 129 * k + 32 * i + jnp.where(x < i, 1, 0)
            zs[k, 32 * i : 32 * i + 32] = (rows_from(prod, start, 32) * weight).astype(BF16)
        extra = rows_from(prod, first_row + 129 * k + 32 * x + 32, 8)[0:1] * weight
        block = jnp.where(
            rows == 0, extra, jnp.where(rows == 1, cot_sum * weight, jnp.where(rows == 2, scale_sum, 0.0))
        )
        zs[k, 128:144] = block.astype(BF16)

    keep = pl.ds(pl.multiple_of(256 * c, 128), 256)
    give = pl.ds(pl.multiple_of(256 * (1 - c), 128), 256)
    across = remote(zs.at[:, :, give], cr, cs.at[0], crs.at[0], at(dc=1))
    send(across)
    relay_teacher(0, c)
    across.wait_recv()
    for k in range(4):
        zb[k] = (zs[k, :, keep].astype(F32) + cr[k].astype(F32)).astype(BF16)

    for d in range(1, 8):
        send(remote(zb.at[lax.rem(z + d, 4)], zr.at[z], zss.at[d - 1], zrs.at[d - 1], at(dz=d)))
    zr[z] = zb[zl]
    relay_teacher(1, 1 - c)
    arrange(a_own)
    for d in range(1, 8):
        ref = zr.at[wrap(z - d, 8)]
        remote(ref, ref, zss.at[d - 1], zrs.at[d - 1], at(dz=d)).wait_recv()
    group = zr[0].astype(F32)
    for k in range(1, 8):
        group += zr[k].astype(F32)

    for i in range(4):
        xs[i, 0:32] = group[32 * i : 32 * i + 32]
        xs[i, 32:40] = group[128:136]
    slot = 2 * x + c
    n = 0
    for dx in range(4):
        for dc in range(2):
            if dx or dc:
                send(remote(xs.at[wrap(x + dx, 4)], xr.at[slot], xss.at[n], xrs.at[n], at(dx=dx, dc=dc)))
                n += 1
    xr[slot] = xs[x]
    n = 0
    for dx in range(4):
        for dc in range(2):
            if dx or dc:
                ref = xr.at[2 * wrap(x - dx, 4) + wrap(c - dc, 2)]
                remote(ref, ref, xss.at[n], xrs.at[n], at(dx=dx, dc=dc)).wait_recv()
                n += 1

    for copy in loads[4:]:
        copy.wait()
    last = jnp.where(f == 63, 1.0, 0.0).astype(F32)
    place = spot[0:1]
    pad[...] = jnp.zeros_like(pad)
    tg[...] = jnp.zeros_like(tg)
    for e in range(8):
        for t in range(2):
            k = 2 * e + t
            pad[k : k + 1] = xr[e, 33:34, 128 * t : 128 * t + 128] * last
            tg[TAIL_ROW + 240 + k : TAIL_ROW + 241 + k] = xr[e, 34:35, 128 * t : 128 * t + 128] * last
    rolled = roll_by(pad[0:24], place, 1, range(7))
    lanes = lax.broadcasted_iota(jnp.int32, (24, 128), 1)
    pad[0:24] = jnp.where(lanes >= lax.rem(place, 128), rolled, pltpu.roll(rolled, 1, 0))
    tg[TAIL_ROW : TAIL_ROW + 256] += roll_by(pad[...], place, 0, range(7, 15))

    limit = PROJ - SHARD * f
    lanes = lax.broadcasted_iota(jnp.int32, (8, 128), 1)
    subs = lax.broadcasted_iota(jnp.int32, (8, 128), 0)

    def update(where, grad, inside):
        old = master[where]
        new_one = beta_one * one[where] + (1.0 - beta_one) * grad
        new_two = beta_two * two[where] + (1.0 - beta_two) * grad * grad
        first = new_one / (1.0 - beta_one**STEP)
        second = new_two / (1.0 - beta_two**STEP)
        decay = jnp.where(inside, decay_rate, 0.0) * old
        new = old - learn_rate * (first / (jnp.sqrt(second) + epsilon) + decay)
        master_out[where] = new
        one_out[where] = new_one
        two_out[where] = new_two
        new_teacher = ema_rate * teacher[where] + (1.0 - ema_rate) * new
        teacher_out[where] = new_teacher
        return new_teacher

    WF[:, 32:48] = jnp.zeros((8, 16, 256), F32)

    for b in range(4):
        for m in range(4):
            quarter = wrap(x + m, 4)
            for t in range(4):
                base = 128 * b + 4 * m + t
                where = (pl.ds(base, 8, stride=16), slice(None))
                e, side = 2 * quarter + t // 2, slice(128 * (t % 2), 128 * (t % 2) + 128)
                slots = 128 * base + 2048 * subs + lanes
                new = update(where, xr[e, 8 * b : 8 * b + 8, side] + tg[where], slots < limit)
                WF[e, 8 * b : 8 * b + 8, side] = new
    for t in range(4):
        where = (slice(512 + t, 513 + t), slice(None))
        e, side = 2 * x + t // 2, slice(128 * (t % 2), 128 * (t % 2) + 128)
        inside = jnp.full((1, 128), 65536, jnp.int32) < limit
        WF[e, 32:33, side] = update(where, xr[e, 32:33, side] * (1.0 - last) + tg[where], inside)

    tail = teacher_out[TAIL_ROW : TAIL_ROW + 256]
    back = lax.rem(32768 - lax.div(place, 128) * 128, 32768)
    moved = roll_by(tail, back, 0, range(7, 15))[0:24]
    lane = lax.rem(place, 128)
    rolled = roll_by(moved, lax.rem(128 - lane, 128), 1, range(7))
    lanes = lax.broadcasted_iota(jnp.int32, (24, 128), 1)
    bias = jnp.where(lanes < 128 - lane, rolled, pltpu.roll(rolled, 23, 0))
    for e in range(8):
        for t in range(2):
            k, side = 2 * e + t, slice(128 * t, 128 * t + 128)
            WF[e, 33:34, side] = bias[k : k + 1]
            WF[e, 34:35, side] = tail[240 + k : 241 + k]
    WS[...] = WF[...].astype(BF16)
    results = [
        pltpu.make_async_copy(src, dst, res_sem.at[k])
        for k, (src, dst) in enumerate(
            [(master_out, master_res), (one_out, one_res), (two_out, two_res), (teacher_out, teacher_res)]
        )
    ]

    first = 4 * c
    for d in (1, 2, 3):
        send(remote(WS.at[first + wrap(a_own + d, 4)], W.at[y, zl, x], w1s.at[d - 1], w1r.at[d - 1], ring(d)))
    W[y, zl, x] = WS[first + a_own]
    for copy in results:
        copy.start()

    def columns(core):
        def member(d):
            return W.at[y, zl, wrap(x + d, 4)] if core == 0 else W.at[wrap(y + d, 4), zl, x]

        def piece(layer, other, half=None):
            span = pl.ds(0, 4) if half is None else pl.ds(2 * half, 2)
            return W.at[other, layer, span] if core == 0 else W.at[span, layer, other]

        here = y if core == 0 else x
        started = []

        def go(copy):
            copy.start()
            started.append(copy)

        for d in (1, 2, 3):
            ref = member(-d)
            remote(ref, ref, w1s.at[d - 1], w1r.at[d - 1], ring(d)).wait_recv()
        mine = piece(zl, here)
        go(remote(mine, mine, w2s.at[0], w2r.at[0], at(dz=1)))
        go(remote(mine, mine, w2s.at[1], w2r.at[1], at(dz=-1)))
        ref = piece(zl, here, 0)
        go(remote(ref, ref, w2s.at[2], w2r.at[2], at(dz=2)))
        ref = piece(zl, here, 1)
        go(remote(ref, ref, w2s.at[3], w2r.at[3], at(dz=-2)))

        def spread(n, layer):
            for k, (half, d) in enumerate([(0, 1), (1, 1), (1, -1), (0, -1)]):
                ref = piece(layer, here, half)
                go(remote(ref, ref, w3s.at[n, k], w3r.at[n, k], cross(d)))

        def wait(n, layer, k):
            half, d = [(0, -1), (1, -1), (1, 1), (0, 1), (0, -2), (1, 2)][k]
            ref = piece(layer, wrap(here + d, 4), half)
            remote(ref, ref, w3s.at[n, k], w3r.at[n, k], cross(1)).wait_recv()
            return ref

        def pass_on(n, layer):
            for k, d in ((0, 1), (2, -1)):
                ref = wait(n, layer, k)
                go(remote(ref, ref, w3s.at[n, 4 + k // 2], w3r.at[n, 4 + k // 2], cross(d)))

        layers = [zl, wrap(zl - 1, 4), wrap(zl + 1, 4), wrap(zl + 2, 4)]
        spread(0, layers[0])
        arrange(wrap(a_own + 2, 4))
        for n, k in ((1, 0), (2, 1)):
            ref = piece(layers[n], here)
            remote(ref, ref, w2s.at[k], w2r.at[k], at(dz=1)).wait_recv()
            spread(n, layers[n])
        for k in (2, 3):
            ref = piece(layers[3], here, k - 2)
            remote(ref, ref, w2s.at[k], w2r.at[k], at(dz=1)).wait_recv()
        spread(3, layers[3])
        for n in range(4):
            pass_on(n, layers[n])
        for n in range(4):
            for k in (1, 3, 4, 5):
                wait(n, layers[n], k)
        for copy in started:
            copy.wait_send()

    for n, core in ((0, c), (1, 1 - c)):
        for k in (1, 3, 4, 5):
            teacher_wait(n, core, k)
    arrange(wrap(a_own + 1, 4))
    arrange(wrap(a_own + 3, 4))

    @pl.when(c == 0)
    def _():
        columns(0)

    @pl.when(c == 1)
    def _():
        columns(1)

    bias_t = W[3, 3, 3, 32:48].astype(F32)[1:2]
    scale_t = W[3, 3, 3, 32:48].astype(F32)[2:3]

    def finish(a, carry):
        total = jnp.zeros((256, 256), F32)
        for g in range(8):
            left = TP[g, a].reshape(256, 384)
            right = W[g // 2, 2 * (g % 2) : 2 * (g % 2) + 2].reshape(384, 256)
            total += jnp.dot(left, right, preferred_element_type=F32)
        OUT[a] = (scale_t * (total + bias_t)).astype(BF16).reshape(2, 128, 256)
        return carry

    lax.fori_loop(0, 4, finish, 0)
    e_own = first + a_own
    out_cols = branch_res.at[:, pl.ds(pl.multiple_of(256 * e_own, 128), 256)]
    n = 0
    for d in range(4):
        for dc in range(2):
            if d or dc:
                a = wrap(a_own + d, 4)
                core = wrap(c + dc, 2)
                to = device(jnp.where(c == 0, a, x), jnp.where(c == 0, y, a), z, core)
                send(remote(OUT.at[a, core], out_cols, os.at[n], orr.at[e_own], to))
                n += 1
    stay = pltpu.make_async_copy(OUT.at[a_own, c], out_cols, own_sem.at[2])
    stay.start()
    for e in range(8):

        @pl.when(e != e_own)
        def _():
            ref = branch_res.at[:, pl.ds(256 * e, 256)]
            remote(ref, ref, os.at[0], orr.at[e], at(dc=1)).wait_recv()

    stay.wait()
    for copy in results:
        copy.wait()
    for copy in pending:
        copy.wait_send()


def per_device(
    tokens, cotangent, saved_branch, layer_gain, offsets, master, moment_one, moment_two, teacher, teacher_tokens
):
    anyspace = pl.BlockSpec(memory_space=pl.ANY)
    dma = pltpu.SemaphoreType.DMA
    flat = jax.ShapeDtypeStruct((FLAT, 128), F32)
    shard = pltpu.VMEM((FLAT, 128), F32)
    spot = jnp.full((8, 128), offsets[1] - PROJ, jnp.int32)
    outs = pl.pallas_call(
        kernel,
        out_shape=[flat] * 4 + [jax.ShapeDtypeStruct((128, WIDTH), BF16)],
        in_specs=[anyspace] * 10,
        out_specs=[anyspace] * 5,
        scratch_shapes=[
            pltpu.VMEM((8, 128), jnp.int32),
            pltpu.VMEM((1, WIDTH), F32),
            pltpu.VMEM((128, WIDTH), BF16),
            pltpu.VMEM((128, WIDTH), BF16),
            shard, shard, shard, shard, shard, shard, shard, shard,
            pltpu.VMEM((4, 4, 128, WINDOW), BF16),
            pltpu.VMEM((4, 4, 128, 512), BF16),
            pltpu.VMEM((4, 4, 16, 512), BF16),
            pltpu.VMEM((4, 16, 512), BF16),
            pltpu.VMEM((WINDOW + 32, 512), F32),
            pltpu.VMEM((4, 144, 512), BF16),
            pltpu.VMEM((4, 144, 256), BF16),
            pltpu.VMEM((4, 144, 256), BF16),
            pltpu.VMEM((8, 144, 256), BF16),
            pltpu.VMEM((4, 40, 256), F32),
            pltpu.VMEM((8, 40, 256), F32),
            pltpu.VMEM((256, 128), F32),
            pltpu.VMEM((520, 128), F32),
            pltpu.VMEM((4, 2, 128, WIDTH), BF16),
            pltpu.VMEM((8, 384, 384), BF16),
            pltpu.VMEM((8, 4, 2, 128, 384), BF16),
            pltpu.VMEM((8, 48, 256), F32),
            pltpu.VMEM((8, 48, 256), BF16),
            pltpu.VMEM((4, 4, 4, 48, 256), BF16),
            pltpu.VMEM((4, 2, 128, 256), BF16),
            dma((9,)), dma((4,)), dma((3,)),
            dma((3,)), dma((3,)), dma((3,)), dma((3,)), dma((3,)), dma((3,)), dma((3,)), dma((3,)),
            dma((4, 6)), dma((4, 6)), dma((4, 6)), dma((4, 6)),
            dma((1,)), dma((1,)), dma((7,)), dma((7,)), dma((7,)), dma((7,)),
            dma((2, 7)), dma((2, 7)), dma((3,)), dma((3,)), dma((4,)), dma((4,)), dma((4, 6)), dma((4, 6)),
            dma((7,)), dma((8,)),
        ],
        compiler_params=pltpu.CompilerParams(collective_id=0, has_side_effects=True, vmem_limit_bytes=56 << 20),
        name="step",
    )(
        spot, layer_gain.reshape(1, WIDTH), tokens, cotangent, saved_branch,
        *[a.reshape(FLAT, 128) for a in (master, moment_one, moment_two, teacher)], teacher_tokens,
    )
    return tuple(a.reshape(SHARD) for a in outs[:4]) + (outs[4],)


def solution(mesh):
    rows = P(("fsdp", "dp"), None)
    return jax.shard_map(
        per_device,
        mesh=mesh,
        in_specs=(rows, rows, rows, P(), P(), P("fsdp"), P("fsdp"), P("fsdp"), P("fsdp"), rows),
        out_specs=(P("fsdp"), P("fsdp"), P("fsdp"), P("fsdp"), rows),
        check_vma=False,
    )
```

```python
import jax
import jax.numpy as jnp
from jax import lax
from jax.experimental import pallas as pl
from jax.experimental.pallas import tpu as pltpu
from jax.sharding import PartitionSpec as P

MESH = pl.DeviceIdType.MESH
F32 = jnp.float32
BF16 = jnp.bfloat16

STEP = 1000
beta_one = 0.9
beta_two = 0.999
learn_rate = 0.001
decay_rate = 0.04
ema_rate = 0.994
epsilon = 1e-08

WIDTH = 2048
PROJ = WIDTH * WIDTH
SHARD = 66048
FLAT = SHARD // 128
TAIL = 260
GROUP = 144


def wrap(value, size):
    return lax.rem(value + size, size)


def device(x, y, z, c):
    return (y * 16 + lax.rem(z, 4) * 4 + x, lax.div(z, 4) * 2 + c)


def remote(src, dst, send, recv, to):
    return pltpu.make_async_remote_copy(
        src_ref=src, dst_ref=dst, send_sem=send, recv_sem=recv, device_id=to, device_id_type=MESH
    )


def roll_by(value, amount, axis, bits):
    for bit in bits:
        on = jnp.broadcast_to(lax.rem(lax.div(amount, 2**bit), 2) == 1, value.shape)
        value = jnp.where(on, pltpu.roll(value, 2 ** (bit - bits[0]), axis), value)
    return value


def iota(shape, axis):
    return lax.broadcasted_iota(jnp.int32, shape, axis)


def kernel(
    offsets, gain_hbm, tokens_hbm, cot_hbm, saved_hbm, master_hbm, one_hbm, two_hbm, teacher_hbm, tt_hbm,
    master_res, one_res, two_res, teacher_res, branch_res,
    gain, tok, cot, saved, master, one, two, teacher, mix, master_out, one_out, two_out, teacher_out,
    TW, T, C, SL, SS, prod, zs, cr, zb, zr, PS, PR, xs, xr, pad, tg, TT, S, TP, TE, W, acc, OUT,
    in_sem, res_sem, own_sem, a1s, a1r, b1s, b1r, s1s, s1r, s2s, s2r, a2s, a2r, b2s, b2r, cs, crs, zss, zrs,
    ps, prs, xss, xrs, ts, tr, us, ur, w2s, w2r, w3s, w3r, os, orr,
):
    f = lax.axis_index("fsdp")
    p = lax.axis_index("dp")
    x = lax.rem(f, 4)
    zl = lax.rem(lax.div(f, 4), 4)
    y = lax.div(f, 16)
    c = lax.rem(p, 2)
    z = lax.div(p, 2) * 4 + zl

    def at(dx=0, dy=0, dz=0, dc=0):
        return device(wrap(x + dx, 4), wrap(y + dy, 4), wrap(z + dz, 8), wrap(c + dc, 2))

    partners = (
        [dict(dx=d) for d in (1, 2, 3)]
        + [dict(dy=d) for d in (1, 2, 3)]
        + [dict(dz=d) for d in range(1, 8)]
        + [dict(dx=d, dc=1) for d in range(4)]
    )
    loads = [
        pltpu.make_async_copy(src, dst, in_sem.at[k])
        for k, (src, dst) in enumerate(
            [
                (tokens_hbm, tok), (cot_hbm, cot), (saved_hbm, saved), (tt_hbm, TT.at[x, c]), (gain_hbm, gain),
                (master_hbm, master), (one_hbm, one), (two_hbm, two), (teacher_hbm, teacher),
            ]
        )
    ]
    for copy in loads:
        copy.start()
    barrier = pltpu.get_barrier_semaphore()
    for partner in partners:
        pl.semaphore_signal(barrier, inc=1, device_id=at(**partner), device_id_type=MESH)
    pl.semaphore_wait(barrier, len(partners))

    pending = []

    def send(copy):
        copy.start()
        pending.append(copy)

    def ring(view, halves, to, sends, recvs):
        def spread(n):
            for k, (half, d) in enumerate([(0, 1), (1, 1), (1, -1), (0, -1)]):
                ref = view(n, 0, halves[half])
                send(remote(ref, ref, sends.at[n, k], recvs.at[n, k], to(d)))

        def wait(n, k):
            half, d = [(0, -1), (1, -1), (1, 1), (0, 1), (0, -2), (1, 2)][k]
            ref = view(n, d, halves[half])
            remote(ref, ref, sends.at[n, k], recvs.at[n, k], to(1)).wait_recv()
            return ref

        def relay(n):
            for k, d in ((0, 1), (2, -1)):
                ref = wait(n, k)
                send(remote(ref, ref, sends.at[n, 4 + k // 2], recvs.at[n, 4 + k // 2], to(d)))

        return spread, wait, relay

    halves = [pl.ds(0, 64), pl.ds(64, 64)]
    along_x = lambda d: at(dx=d)
    along_y = lambda d: at(dy=d)
    spread_t, wait_t, relay_t = ring(
        lambda n, d, half: T.at[wrap(y - n, 4), wrap(x + d, 4), half], halves, along_x, a2s, a2r
    )
    spread_c, wait_c, relay_c = ring(
        lambda n, d, half: C.at[wrap(y + d, 4), wrap(x - n, 4), half], halves, along_y, b2s, b2r
    )
    spread_h, wait_h, relay_h = ring(
        lambda n, d, half: TT.at[wrap(x + d, 4), c, half], halves, along_x, ts, tr
    )

    def quarter(i):
        return cot_hbm.at[:, pl.ds(pl.multiple_of(512 * i, 128), 512)]

    mine = pltpu.make_async_copy(quarter(x), C.at[y, x], own_sem.at[0])
    mine.start()
    for d in (1, 2, 3):
        send(remote(quarter(wrap(x + d, 4)), C.at[y, x], b1s.at[d - 1], b1r.at[d - 1], at(dx=d)))
    loads[0].wait()
    for i in range(4):
        end = min(512 * i + 640, WIDTH)
        window = tok[:, 512 * i : end].astype(F32)
        if i:
            window = pltpu.roll(window, end - 512 * i - 4 * i, 1)[:, :512]
        else:
            window = window[:, :512]
        if i == 3:
            window = jnp.where(iota((128, 512), 1) < 500, window, 0.0)
        TW[i] = window.astype(BF16)
    for d in (1, 2, 3):
        send(remote(TW.at[wrap(y + d, 4)], T.at[y, x], a1s.at[d - 1], a1r.at[d - 1], at(dy=d)))
    T[y, x] = TW[y]
    spread_t(0)
    mine.wait()
    spread_c(0)
    loads[3].wait()
    send(remote(TT.at[x, c], TT.at[x, c], us.at[0], ur.at[0], at(dc=1)))
    for d in (1, 2, 3):
        ref = T.at[wrap(y - d, 4), x]
        remote(ref, ref, a1s.at[d - 1], a1r.at[d - 1], at(dy=d)).wait_recv()
        spread_t(d)
        ref = C.at[y, wrap(x - d, 4)]
        remote(ref, ref, b1s.at[d - 1], b1r.at[d - 1], at(dx=d)).wait_recv()
        spread_c(d)
        relay_t(d - 1)
        relay_c(d - 1)

    loads[1].wait()
    loads[2].wait()
    total = jnp.zeros((1, WIDTH), F32)
    for r in range(0, 128, 16):
        total += jnp.sum(cot[r : r + 16].astype(F32) * saved[r : r + 16].astype(F32), axis=0, keepdims=True)
    top = total.astype(BF16).astype(F32)
    lane = iota((128, 128), 1)
    left = jnp.zeros((128, 128), F32)
    for i in range(3):
        tile = tok[:, 512 * (i + 1) : 512 * (i + 1) + 128].astype(F32)
        left = jnp.where(jnp.logical_and(lane >= 4 * i, lane < 4 * i + 4), tile, left)
    rows = iota((16, 512), 0)
    for i in range(4):
        side = slice(512 * i, 512 * i + 512)
        part = lax.dot_general(
            left.astype(BF16), cot[:, side], (((0,), (0,)), ((), ())), preferred_element_type=F32
        )[:16]
        part = jnp.where(rows == 12, top[:, side], jnp.where(rows == 13, total[:, side] - top[:, side], part))
        SS[i] = part.astype(BF16)
    for d in (1, 2, 3):
        send(remote(SS.at[wrap(x + d, 4)], SL.at[y, x], s1s.at[d - 1], s1r.at[d - 1], at(dx=d)))
    SL[y, x] = SS[x]

    for copy in loads[4:]:
        copy.wait()
    limit = PROJ - SHARD * f
    spots = 128 * iota((FLAT, 128), 0) + iota((FLAT, 128), 1)
    keep = jnp.where(spots < limit, 1.0 - learn_rate * decay_rate, 1.0)
    mix[...] = ema_rate * teacher[...] + (1.0 - ema_rate) * keep * master[...]
    place = jnp.full((1, 128), offsets[1] - PROJ, jnp.int32)
    row_back = lax.rem(32768 - lax.div(place, 128) * 128, 32768)
    lane_at = lax.rem(place, 128)
    lane_back = lax.rem(128 - lane_at, 128)
    lanes24 = iota((24, 128), 1)
    low_core = c == 0
    for k, source in enumerate((mix, one, two)):
        for b in range(4):
            for m in range(4):
                for t in range(2):
                    low = source[pl.ds(128 * b + 4 * m + t, 8, stride=16), :]
                    high = source[pl.ds(128 * b + 4 * m + 2 + t, 8, stride=16), :]
                    PS[wrap(x + m, 4), k, 8 * b : 8 * b + 8, 128 * t : 128 * t + 128] = jnp.where(low_core, low, high)
        tail = source[TAIL : TAIL + 256]
        moved = roll_by(tail, row_back, 0, range(7, 15))[0:24]
        rolled = roll_by(moved, lane_back, 1, range(7))
        bias = jnp.where(lanes24 < 128 - lane_at, rolled, pltpu.roll(rolled, 23, 0))
        for m in range(4):
            for t in range(2):
                side = slice(128 * t, 128 * t + 128)
                n = 4 * m + t
                PS[m, k, 32:33, side] = jnp.where(low_core, source[512 + t : 513 + t], source[514 + t : 515 + t])
                PS[m, k, 33:34, side] = jnp.where(low_core, bias[n : n + 1], bias[n + 2 : n + 3])
                PS[m, k, 34:35, side] = jnp.where(low_core, tail[240 + n : 241 + n], tail[242 + n : 243 + n])
                PS[m, k, 35:40, side] = jnp.zeros((5, 128), F32)

    for d in (1, 2, 3):
        ref = SL.at[y, wrap(x - d, 4)]
        remote(ref, ref, s1s.at[d - 1], s1r.at[d - 1], at(dx=d)).wait_recv()
    for d in (1, 2, 3):
        send(remote(SL.at[y], SL.at[y], s2s.at[d - 1], s2r.at[d - 1], at(dy=d)))
    relay_t(3)
    relay_c(3)
    for d in (1, 2, 3):
        send(remote(PS.at[wrap(x + d, 4)], PR.at[x], ps.at[d - 1], prs.at[d - 1], at(dx=d)))
    PR[x] = PS[x]
    spread_h(0)

    def one_hot(g, carry):
        col = iota((1, 384), 1)
        i = lax.div(lax.rem(col, 128), 32)
        source = 258 * g + lax.div(col, 128) * 129 + lax.rem(col, 128) + jnp.where(i > x, 1, 0)
        slot = lax.rem(col, 128) - 32 * lax.rem(g, 4)
        extra = 258 * g + 32 * x + 32 + jnp.where(slot == 0, 0, 129)
        extra = jnp.where(jnp.logical_or(slot == 0, slot == 16), extra, -1)
        source = jnp.where(col < 256, source, extra) - jnp.minimum(256 * g, WIDTH - 384)
        S[g] = jnp.where(iota((384, 384), 0) == source, 1.0, 0.0).astype(BF16)
        return carry

    lax.fori_loop(0, 8, one_hot, 0)

    def arrange(a):
        def group(g, extra):
            start = pl.multiple_of(jnp.minimum(256 * g, WIDTH - 384), 128)
            block = TT[a, :, :, pl.ds(start, 384)].reshape(256, 384)
            part = jnp.dot(block, S[g], preferred_element_type=F32)
            TP[g, a] = part[:, :256].astype(BF16)
            return extra + part[:, 256:]

        for h in range(2):
            extra = lax.fori_loop(4 * h, 4 * h + 4, group, jnp.zeros((256, 128), F32))
            TE[a, :, 128 * h : 128 * h + 128] = extra.astype(BF16)

    for n in range(4):
        for k in (1, 3, 4, 5):
            wait_t(n, k)
            wait_c(n, k)
    for d in (1, 2, 3):
        ref = SL.at[wrap(y - d, 4)]
        remote(ref, ref, s2s.at[d - 1], s2r.at[d - 1], at(dy=d)).wait_recv()

    prod[0:512] = jnp.zeros((512, 512), F32)
    ones = jnp.ones((16, 512), BF16)

    def multiply(k, sums):
        right = C[k].reshape(512, 512)
        prod[0:512] += lax.dot_general(
            T[k].reshape(512, 512), right, (((0,), (0,)), ((), ())), preferred_element_type=F32
        )
        return sums + jnp.dot(ones, right, preferred_element_type=F32)

    cot_sum = lax.fori_loop(0, 4, multiply, jnp.zeros((16, 512), F32))
    small = jnp.zeros((16, 512), F32)
    for i in range(4):
        for k in range(4):
            small += SL[i, k].astype(F32)
    rest = jnp.where(y == 0, small, jnp.where(y == 1, pltpu.roll(small, 12, 0), pltpu.roll(small, 8, 0)))
    prod[512:528] = jnp.where(rows < jnp.where(y < 3, 4, 0), rest, 0.0)
    weight = gain[:, pl.ds(pl.multiple_of(512 * x, 128), 512)]
    for k in range(4):
        for i in range(4):
            start = 129 * k + 32 * i
            part = prod[start : start + 32]
            if i:
                part = jnp.where(x < i, prod[start + 1 : start + 33], part)
            zs[k, 32 * i : 32 * i + 32] = (part * weight).astype(BF16)
        extra = prod[129 * k + 32 : 129 * k + 33]
        for i in range(1, 4):
            extra = jnp.where(x == i, prod[129 * k + 32 * i + 32 : 129 * k + 32 * i + 33], extra)
        block = jnp.where(rows == 1, cot_sum * weight, jnp.where(rows == 2, small[12:13] + small[13:14], 0.0))
        zs[k, 128:144] = jnp.where(rows == 0, extra * weight, block).astype(BF16)

    keep_half = pl.ds(pl.multiple_of(256 * c, 128), 256)
    give_half = pl.ds(pl.multiple_of(256 * (1 - c), 128), 256)
    across = remote(zs.at[:, :, give_half], cr, cs.at[0], crs.at[0], at(dc=1))
    send(across)
    relay_h(0)
    across.wait_recv()
    for k in range(4):
        zb[k] = (zs[k, :, keep_half].astype(F32) + cr[k].astype(F32)).astype(BF16)

    for d in range(1, 8):
        send(remote(zb.at[lax.rem(z + d, 4)], zr.at[z], zss.at[d - 1], zrs.at[d - 1], at(dz=d)))
    zr[z] = zb[zl]
    ref = TT.at[x, 1 - c]
    remote(ref, ref, us.at[0], ur.at[0], at(dc=1)).wait_recv()
    arrange(x)
    for d in (1, 2, 3):
        ref = PR.at[wrap(x - d, 4)]
        remote(ref, ref, ps.at[d - 1], prs.at[d - 1], at(dx=d)).wait_recv()
    for d in range(1, 8):
        ref = zr.at[wrap(z - d, 8)]
        remote(ref, ref, zss.at[d - 1], zrs.at[d - 1], at(dz=d)).wait_recv()
    group = zr[0].astype(F32)
    for k in range(1, 8):
        group += zr[k].astype(F32)

    def low_teacher(grad, mixed, old_one, old_two):
        new_one = beta_one * old_one + (1.0 - beta_one) * grad
        new_two = beta_two * old_two + (1.0 - beta_two) * grad * grad
        first = new_one / (1.0 - beta_one**STEP)
        second = new_two / (1.0 - beta_two**STEP)
        return mixed - ((1.0 - ema_rate) * learn_rate) * (first / (jnp.sqrt(second) + epsilon))

    for i in range(4):
        span = slice(32 * i, 32 * i + 32)
        W[y, zl, span] = low_teacher(group[span], *[PR[i, k, 0:32] for k in range(3)]).astype(BF16)
    first_row = iota((8, 256), 0) == 0
    extras = [jnp.where(first_row, PR[x, k, 32:40], PR[3, k, 32:40]) for k in range(3)]
    block = low_teacher(group[128:136], *extras)
    block = jnp.where(iota((8, 256), 0) < 3, block, 0.0)
    W[y, zl, 128:144] = jnp.concatenate([block, jnp.zeros((8, 256), F32)], axis=0).astype(BF16)

    parts = [pl.ds(0, 80), pl.ds(80, 64)]
    layers = [zl, wrap(zl - 1, 4), wrap(zl + 1, 4), wrap(zl + 2, 4)]
    spread_w, wait_w, relay_w = ring(
        lambda n, d, half: W.at[wrap(y + d, 4), layers[n], half], parts, along_y, w3s, w3r
    )
    for k, (ref, d) in enumerate(
        [(W.at[y, zl], 1), (W.at[y, zl], -1), (W.at[y, zl, parts[0]], 2), (W.at[y, zl, parts[1]], -2)]
    ):
        send(remote(ref, ref, w2s.at[k], w2r.at[k], at(dz=d)))
    spread_w(0)

    for i in range(4):
        xs[i, 0:32] = group[32 * i : 32 * i + 32]
        xs[i, 32:40] = group[128:136]
    slot = 2 * x + c
    others = [(dx, dc) for dx in range(4) for dc in range(2) if dx or dc]
    for n, (dx, dc) in enumerate(others):
        send(remote(xs.at[wrap(x + dx, 4)], xr.at[slot], xss.at[n], xrs.at[n], at(dx=dx, dc=dc)))
    xr[slot] = xs[x]

    def share(n, d, arrivals):
        for k in arrivals:
            wait_h(0, k)
        ref = TT.at[wrap(x + d, 4), c]
        send(remote(ref, ref, us.at[n], ur.at[n], at(dc=1)))

    def shared(n, d):
        ref = TT.at[wrap(x + d, 4), 1 - c]
        remote(ref, ref, us.at[n], ur.at[n], at(dc=1)).wait_recv()

    share(1, -1, (1,))
    share(2, 1, (3,))
    for n, k in ((1, 0), (2, 1)):
        ref = W.at[y, layers[n]]
        remote(ref, ref, w2s.at[k], w2r.at[k], at(dz=1)).wait_recv()
        spread_w(n)
    for k in (2, 3):
        ref = W.at[y, layers[3], parts[k - 2]]
        remote(ref, ref, w2s.at[k], w2r.at[k], at(dz=1)).wait_recv()
    spread_w(3)
    relay_w(0)
    shared(1, -1)
    arrange(wrap(x - 1, 4))
    share(3, 2, (4, 5))
    relay_w(1)
    shared(2, 1)
    arrange(wrap(x + 1, 4))
    relay_w(2)

    def accumulate(i, a):
        total = jnp.zeros((256, 256), F32)
        for h in range(2):
            right = W[i, 2 * h : 2 * h + 2, 0:128].reshape(256, 256)
            total += jnp.dot(TP[2 * i + h, a], right, preferred_element_type=F32)
        return total

    relay_w(3)
    shared(3, 2)
    arrange(wrap(x + 2, 4))

    for n, (dx, dc) in enumerate(others):
        ref = xr.at[2 * wrap(x - dx, 4) + wrap(c - dc, 2)]
        remote(ref, ref, xss.at[n], xrs.at[n], at(dx=dx, dc=dc)).wait_recv()
    last = jnp.where(f == 63, 1.0, 0.0).astype(F32)
    pad[...] = jnp.zeros_like(pad)
    tg[...] = jnp.zeros_like(tg)
    for e in range(8):
        for t in range(2):
            n = 2 * e + t
            pad[n : n + 1] = xr[e, 33:34, 128 * t : 128 * t + 128] * last
            tg[TAIL + 240 + n : TAIL + 241 + n] = xr[e, 34:35, 128 * t : 128 * t + 128] * last
    rolled = roll_by(pad[0:24], place, 1, range(7))
    pad[0:24] = jnp.where(lanes24 >= lane_at, rolled, pltpu.roll(rolled, 1, 0))
    tg[TAIL : TAIL + 256] += roll_by(pad[...], place, 0, range(7, 15))
    lanes = iota((8, 128), 1)
    subs = iota((8, 128), 0)

    def update(where, grad, inside):
        old = master[where]
        new_one = beta_one * one[where] + (1.0 - beta_one) * grad
        new_two = beta_two * two[where] + (1.0 - beta_two) * grad * grad
        first = new_one / (1.0 - beta_one**STEP)
        second = new_two / (1.0 - beta_two**STEP)
        decay = jnp.where(inside, decay_rate, 0.0) * old
        new = old - learn_rate * (first / (jnp.sqrt(second) + epsilon) + decay)
        master_out[where] = new
        one_out[where] = new_one
        two_out[where] = new_two
        teacher_out[where] = ema_rate * teacher[where] + (1.0 - ema_rate) * new

    for b in range(4):
        for m in range(4):
            for t in range(4):
                base = 128 * b + 4 * m + t
                where = (pl.ds(base, 8, stride=16), slice(None))
                e, side = 2 * wrap(x + m, 4) + t // 2, slice(128 * (t % 2), 128 * (t % 2) + 128)
                slots = 128 * base + 2048 * subs + lanes
                update(where, xr[e, 8 * b : 8 * b + 8, side] + tg[where], slots < limit)
    for t in range(4):
        where = (slice(512 + t, 513 + t), slice(None))
        e, side = 2 * x + t // 2, slice(128 * (t % 2), 128 * (t % 2) + 128)
        inside = jnp.full((1, 128), 65536, jnp.int32) < limit
        update(where, xr[e, 32:33, side] * (1.0 - last) + tg[where], inside)
    results = [
        pltpu.make_async_copy(src, dst, res_sem.at[k])
        for k, (src, dst) in enumerate(
            [(master_out, master_res), (one_out, one_res), (two_out, two_res), (teacher_out, teacher_res)]
        )
    ]
    for copy in results:
        copy.start()

    def begin(a, carry):
        acc[a] = accumulate(y, a)
        return carry

    lax.fori_loop(0, 4, begin, 0)
    for d, arrivals in ((-1, (1,)), (1, (3,)), (2, (4, 5))):
        for n in range(4):
            for k in arrivals:
                wait_w(n, k)
        if d != 2:

            def more(a, carry):
                acc[a] += accumulate(wrap(y + d, 4), a)
                return carry

            lax.fori_loop(0, 4, more, 0)

    bias_t = W[3, 3, 128:144].astype(F32)[1:2]
    scale_t = W[3, 3, 128:144].astype(F32)[2:3]
    ends = W[:, :, 128:144].reshape(256, 256)
    out_cols = branch_res.at[:, pl.ds(pl.multiple_of(256 * slot, 128), 256)]
    n = 0
    for d in (2, 1, 3, 0):
        a = wrap(x + d, 4)
        total = acc[a] + accumulate(wrap(y + 2, 4), a) + jnp.dot(TE[a], ends, preferred_element_type=F32)
        OUT[a] = (scale_t * (total + bias_t)).astype(BF16).reshape(2, 128, 256)
        for dc in range(2):
            core = wrap(c + dc, 2)
            if d or dc:
                send(remote(OUT.at[a, core], out_cols, os.at[n], orr.at[slot], at(dx=d, dc=dc)))
                n += 1
    stay = pltpu.make_async_copy(OUT.at[x, c], out_cols, own_sem.at[1])
    stay.start()
    for n, (dx, dc) in enumerate(others):
        e = 2 * wrap(x - dx, 4) + wrap(c - dc, 2)
        ref = branch_res.at[:, pl.ds(pl.multiple_of(256 * e, 128), 256)]
        remote(ref, ref, os.at[n], orr.at[e], at(dc=1)).wait_recv()
    stay.wait()
    for copy in results:
        copy.wait()
    for copy in pending:
        copy.wait_send()


def copy_kernel(*refs):
    sems = refs[10]
    copies = [pltpu.make_async_copy(refs[k], refs[5 + k], sems.at[k]) for k in range(5)]
    for copy in copies:
        copy.start()
    for copy in copies:
        copy.wait()


def per_device(
    tokens, cotangent, saved_branch, layer_gain, offsets, master, moment_one, moment_two, teacher, teacher_tokens
):
    anyspace = pl.BlockSpec(memory_space=pl.ANY)
    dma = pltpu.SemaphoreType.DMA
    flat = jax.ShapeDtypeStruct((FLAT, 128), F32)
    shard = pltpu.VMEM((FLAT, 128), F32)
    rows = pltpu.VMEM((128, WIDTH), BF16)
    results = [flat] * 4 + [jax.ShapeDtypeStruct((128, WIDTH), BF16)]
    outs = pl.pallas_call(
        kernel,
        out_shape=results,
        in_specs=[pl.BlockSpec(memory_space=pltpu.SMEM)] + [anyspace] * 9,
        out_specs=[anyspace] * 5,
        scratch_shapes=[
            pltpu.VMEM((1, WIDTH), F32),
            rows, rows, rows,
            shard, shard, shard, shard, shard, shard, shard, shard, shard,
            pltpu.VMEM((4, 128, 512), BF16),
            pltpu.VMEM((4, 4, 128, 512), BF16),
            pltpu.VMEM((4, 4, 128, 512), BF16),
            pltpu.VMEM((4, 4, 16, 512), BF16),
            pltpu.VMEM((4, 16, 512), BF16),
            pltpu.VMEM((528, 512), F32),
            pltpu.VMEM((4, GROUP, 512), BF16),
            pltpu.VMEM((4, GROUP, 256), BF16),
            pltpu.VMEM((4, GROUP, 256), BF16),
            pltpu.VMEM((8, GROUP, 256), BF16),
            pltpu.VMEM((4, 3, 40, 256), F32),
            pltpu.VMEM((4, 3, 40, 256), F32),
            pltpu.VMEM((4, 40, 256), F32),
            pltpu.VMEM((8, 40, 256), F32),
            pltpu.VMEM((256, 128), F32),
            pltpu.VMEM((520, 128), F32),
            pltpu.VMEM((4, 2, 128, WIDTH), BF16),
            pltpu.VMEM((8, 384, 384), BF16),
            pltpu.VMEM((8, 4, 256, 256), BF16),
            pltpu.VMEM((4, 256, 256), BF16),
            pltpu.VMEM((4, 4, GROUP, 256), BF16),
            pltpu.VMEM((4, 256, 256), F32),
            pltpu.VMEM((4, 2, 128, 256), BF16),
            dma((9,)), dma((4,)), dma((2,)),
            dma((3,)), dma((3,)), dma((3,)), dma((3,)), dma((3,)), dma((3,)), dma((3,)), dma((3,)),
            dma((4, 6)), dma((4, 6)), dma((4, 6)), dma((4, 6)),
            dma((1,)), dma((1,)), dma((7,)), dma((7,)),
            dma((3,)), dma((3,)), dma((7,)), dma((7,)),
            dma((1, 6)), dma((1, 6)), dma((4,)), dma((4,)), dma((4,)), dma((4,)), dma((4, 6)), dma((4, 6)),
            dma((7,)), dma((8,)),
        ],
        compiler_params=pltpu.CompilerParams(collective_id=0, has_side_effects=True, vmem_limit_bytes=56 << 20),
        name="step",
    )(
        offsets, layer_gain.reshape(1, WIDTH), tokens, cotangent, saved_branch,
        *[a.reshape(FLAT, 128) for a in (master, moment_one, moment_two, teacher)], teacher_tokens,
    )
    outs = pl.pallas_call(
        copy_kernel,
        out_shape=results,
        in_specs=[anyspace] * 5,
        out_specs=[anyspace] * 5,
        scratch_shapes=[dma((5,))],
        name="place",
    )(*outs)
    return tuple(a.reshape(SHARD) for a in outs[:4]) + (outs[4],)


def solution(mesh):
    rows = P(("fsdp", "dp"), None)
    return jax.shard_map(
        per_device,
        mesh=mesh,
        in_specs=(rows, rows, rows, P(), P(), P("fsdp"), P("fsdp"), P("fsdp"), P("fsdp"), rows),
        out_specs=(P("fsdp"), P("fsdp"), P("fsdp"), P("fsdp"), rows),
        check_vma=False,
    )
```

```python
import jax
import jax.numpy as jnp
from jax import lax
from jax.experimental import pallas as pl
from jax.experimental.pallas import tpu as pltpu
from jax.sharding import PartitionSpec as P

MESH = pl.DeviceIdType.MESH
F32 = jnp.float32
BF16 = jnp.bfloat16

STEP = 1000
beta_one = 0.9
beta_two = 0.999
learn_rate = 0.001
decay_rate = 0.04
ema_rate = 0.994
epsilon = 1e-08

WIDTH = 2048
PROJ = WIDTH * WIDTH
SHARD = 66048
FLAT = SHARD // 128
TAIL = 260
GROUP = 144


def wrap(value, size):
    return lax.rem(value + size, size)


def device(x, y, z, c):
    return (y * 16 + lax.rem(z, 4) * 4 + x, lax.div(z, 4) * 2 + c)


def remote(src, dst, send, recv, to):
    return pltpu.make_async_remote_copy(
        src_ref=src, dst_ref=dst, send_sem=send, recv_sem=recv, device_id=to, device_id_type=MESH
    )


def roll_by(value, amount, axis, bits):
    for bit in bits:
        on = jnp.broadcast_to(lax.rem(lax.div(amount, 2**bit), 2) == 1, value.shape)
        value = jnp.where(on, pltpu.roll(value, 2 ** (bit - bits[0]), axis), value)
    return value


def iota(shape, axis):
    return lax.broadcasted_iota(jnp.int32, shape, axis)


def kernel(
    offsets, gain_hbm, tokens_hbm, cot_hbm, saved_hbm, master_hbm, one_hbm, two_hbm, teacher_hbm, tt_hbm,
    master_res, one_res, two_res, teacher_res, branch_res,
    gain, tok, cot, saved, master, one, two, teacher, mix, master_out, one_out, two_out, teacher_out,
    TW, T, C, SX, SL, SS, prod, zs, cr, zb, zr, PS, PR, xs, xr, pad, tg, TT, S, TP, TE, W, acc, OUT,
    in_sem, res_sem, own_sem, a1s, a1r, b1s, b1r, s1s, s1r, s2s, s2r, a2s, a2r, b2s, b2r, cs, crs, zss, zrs,
    ps, prs, xss, xrs, ts, tr, us, ur, w2s, w2r, w3s, w3r, os, orr,
):
    f = lax.axis_index("fsdp")
    p = lax.axis_index("dp")
    x = lax.rem(f, 4)
    zl = lax.rem(lax.div(f, 4), 4)
    y = lax.div(f, 16)
    c = lax.rem(p, 2)
    z = lax.div(p, 2) * 4 + zl

    def at(dx=0, dy=0, dz=0, dc=0):
        return device(wrap(x + dx, 4), wrap(y + dy, 4), wrap(z + dz, 8), wrap(c + dc, 2))

    partners = (
        [dict(dx=d) for d in (1, 2, 3)]
        + [dict(dy=d) for d in (1, 2, 3)]
        + [dict(dz=d) for d in range(1, 8)]
        + [dict(dx=d, dc=1) for d in range(4)]
    )
    loads = [
        pltpu.make_async_copy(src, dst, in_sem.at[k])
        for k, (src, dst) in enumerate(
            [
                (tokens_hbm, tok), (cot_hbm, cot), (saved_hbm, saved), (tt_hbm, TT.at[x, c]), (gain_hbm, gain),
                (master_hbm, master), (one_hbm, one), (two_hbm, two), (teacher_hbm, teacher),
            ]
        )
    ]
    for copy in loads:
        copy.start()
    barrier = pltpu.get_barrier_semaphore()
    for partner in partners:
        pl.semaphore_signal(barrier, inc=1, device_id=at(**partner), device_id_type=MESH)
    pl.semaphore_wait(barrier, len(partners))

    pending = []

    def send(copy):
        copy.start()
        pending.append(copy)

    def ring(view, halves, to, sends, recvs):
        def spread(n):
            for k, (half, d) in enumerate([(0, 1), (1, 1), (1, -1), (0, -1)]):
                ref = view(n, 0, halves[half])
                send(remote(ref, ref, sends.at[n, k], recvs.at[n, k], to(d)))

        def wait(n, k):
            half, d = [(0, -1), (1, -1), (1, 1), (0, 1), (0, -2), (1, 2)][k]
            ref = view(n, d, halves[half])
            remote(ref, ref, sends.at[n, k], recvs.at[n, k], to(1)).wait_recv()
            return ref

        def relay(n):
            for k, d in ((0, 1), (2, -1)):
                ref = wait(n, k)
                send(remote(ref, ref, sends.at[n, 4 + k // 2], recvs.at[n, 4 + k // 2], to(d)))

        return spread, wait, relay

    halves = [pl.ds(0, 64), pl.ds(64, 64)]
    along_x = lambda d: at(dx=d)
    along_y = lambda d: at(dy=d)
    spread_t, wait_t, relay_t = ring(
        lambda n, d, half: T.at[wrap(y - n, 4), wrap(x + d, 4), half], halves, along_x, a2s, a2r
    )
    spread_c, wait_c, relay_c = ring(
        lambda n, d, half: C.at[wrap(y + d, 4), wrap(x - n, 4), half], halves, along_y, b2s, b2r
    )
    spread_h, wait_h, relay_h = ring(
        lambda n, d, half: TT.at[wrap(x + d, 4), c, half], halves, along_x, ts, tr
    )

    def quarter(i):
        return cot_hbm.at[:, pl.ds(pl.multiple_of(512 * i, 128), 512)]

    mine = pltpu.make_async_copy(quarter(x), C.at[y, x], own_sem.at[0])
    mine.start()
    for d in (1, 2, 3):
        send(remote(quarter(wrap(x + d, 4)), C.at[y, x], b1s.at[d - 1], b1r.at[d - 1], at(dx=d)))
    loads[0].wait()
    for i in range(4):
        end = min(512 * i + 640, WIDTH)
        window = tok[:, 512 * i : end].astype(F32)
        if i:
            window = pltpu.roll(window, end - 512 * i - 4 * i, 1)[:, :512]
        else:
            window = window[:, :512]
        if i == 3:
            window = jnp.where(iota((128, 512), 1) < 500, window, 0.0)
        TW[i] = window.astype(BF16)
    for d in (1, 2, 3):
        send(remote(TW.at[wrap(y + d, 4)], T.at[y, x], a1s.at[d - 1], a1r.at[d - 1], at(dy=d)))
    T[y, x] = TW[y]
    spread_t(0)
    mine.wait()
    spread_c(0)
    loads[3].wait()
    send(remote(TT.at[x, c], TT.at[x, c], us.at[0], ur.at[0], at(dc=1)))
    loads[1].wait()
    loads[2].wait()
    total = jnp.zeros((1, WIDTH), F32)
    for r in range(0, 128, 16):
        total += jnp.sum(cot[r : r + 16].astype(F32) * saved[r : r + 16].astype(F32), axis=0, keepdims=True)
    top = total.astype(BF16).astype(F32)
    lane = iota((128, 128), 1)
    left = jnp.zeros((128, 128), F32)
    for i in range(3):
        tile = tok[:, 512 * (i + 1) : 512 * (i + 1) + 128].astype(F32)
        left = jnp.where(jnp.logical_and(lane >= 4 * i, lane < 4 * i + 4), tile, left)
    rows = iota((16, 512), 0)
    for i in range(4):
        side = slice(512 * i, 512 * i + 512)
        part = lax.dot_general(
            left.astype(BF16), cot[:, side], (((0,), (0,)), ((), ())), preferred_element_type=F32
        )[:16]
        part = jnp.where(rows == 12, top[:, side], jnp.where(rows == 13, total[:, side] - top[:, side], part))
        SS[i] = part.astype(BF16)
    for d in (1, 2, 3):
        send(remote(SS.at[wrap(x + d, 4)], SX.at[x], s1s.at[d - 1], s1r.at[d - 1], at(dx=d)))
    SX[x] = SS[x]

    for d, before in ((1, 0), (3, 1), (2, 3)):
        ref = T.at[wrap(y - d, 4), x]
        remote(ref, ref, a1s.at[d - 1], a1r.at[d - 1], at(dy=d)).wait_recv()
        spread_t(d)
        ref = C.at[y, wrap(x - d, 4)]
        remote(ref, ref, b1s.at[d - 1], b1r.at[d - 1], at(dx=d)).wait_recv()
        spread_c(d)
        relay_t(before)
        relay_c(before)

    for d in (1, 2, 3):
        ref = SX.at[wrap(x - d, 4)]
        remote(ref, ref, s1s.at[d - 1], s1r.at[d - 1], at(dx=d)).wait_recv()
    small = jnp.zeros((16, 512), F32)
    for i in range(4):
        small += SX[i].astype(F32)
    total = small[12:13] + small[13:14]
    top = total.astype(BF16).astype(F32)
    SL[y] = jnp.where(rows == 12, top, jnp.where(rows == 13, total - top, small)).astype(BF16)
    for d in (1, 2, 3):
        send(remote(SL.at[y], SL.at[y], s2s.at[d - 1], s2r.at[d - 1], at(dy=d)))

    for copy in loads[4:]:
        copy.wait()
    limit = PROJ - SHARD * f
    spots = 128 * iota((FLAT, 128), 0) + iota((FLAT, 128), 1)
    keep = jnp.where(spots < limit, 1.0 - learn_rate * decay_rate, 1.0)
    mix[...] = ema_rate * teacher[...] + (1.0 - ema_rate) * keep * master[...]
    place = jnp.full((1, 128), offsets[1] - PROJ, jnp.int32)
    row_back = lax.rem(32768 - lax.div(place, 128) * 128, 32768)
    lane_at = lax.rem(place, 128)
    lane_back = lax.rem(128 - lane_at, 128)
    lanes24 = iota((24, 128), 1)
    low_core = c == 0
    for k, source in enumerate((mix, one, two)):
        for b in range(4):
            for m in range(4):
                for t in range(2):
                    low = source[pl.ds(128 * b + 4 * m + t, 8, stride=16), :]
                    high = source[pl.ds(128 * b + 4 * m + 2 + t, 8, stride=16), :]
                    PS[wrap(x + m, 4), k, 8 * b : 8 * b + 8, 128 * t : 128 * t + 128] = jnp.where(low_core, low, high)
        tail = source[TAIL : TAIL + 256]
        moved = roll_by(tail, row_back, 0, range(7, 15))[0:24]
        rolled = roll_by(moved, lane_back, 1, range(7))
        bias = jnp.where(lanes24 < 128 - lane_at, rolled, pltpu.roll(rolled, 23, 0))
        for m in range(4):
            for t in range(2):
                side = slice(128 * t, 128 * t + 128)
                n = 4 * m + t
                PS[m, k, 32:33, side] = jnp.where(low_core, source[512 + t : 513 + t], source[514 + t : 515 + t])
                PS[m, k, 33:34, side] = jnp.where(low_core, bias[n : n + 1], bias[n + 2 : n + 3])
                PS[m, k, 34:35, side] = jnp.where(low_core, tail[240 + n : 241 + n], tail[242 + n : 243 + n])
                PS[m, k, 35:40, side] = jnp.zeros((5, 128), F32)

    relay_t(2)
    relay_c(2)
    for d in (1, 2, 3):
        send(remote(PS.at[wrap(x + d, 4)], PR.at[x], ps.at[d - 1], prs.at[d - 1], at(dx=d)))
    PR[x] = PS[x]
    spread_h(0)

    def one_hot(g, carry):
        col = iota((1, 384), 1)
        i = lax.div(lax.rem(col, 128), 32)
        source = 258 * g + lax.div(col, 128) * 129 + lax.rem(col, 128) + jnp.where(i > x, 1, 0)
        slot = lax.rem(col, 128) - 32 * lax.rem(g, 4)
        extra = 258 * g + 32 * x + 32 + jnp.where(slot == 0, 0, 129)
        extra = jnp.where(jnp.logical_or(slot == 0, slot == 16), extra, -1)
        source = jnp.where(col < 256, source, extra) - jnp.minimum(256 * g, WIDTH - 384)
        S[g] = jnp.where(iota((384, 384), 0) == source, 1.0, 0.0).astype(BF16)
        return carry

    lax.fori_loop(0, 8, one_hot, 0)

    def arrange(a):
        def group(g, extra):
            start = pl.multiple_of(jnp.minimum(256 * g, WIDTH - 384), 128)
            block = TT[a, :, :, pl.ds(start, 384)].reshape(256, 384)
            part = jnp.dot(block, S[g], preferred_element_type=F32)
            TP[g, a] = part[:, :256].astype(BF16)
            return extra + part[:, 256:]

        for h in range(2):
            extra = lax.fori_loop(4 * h, 4 * h + 4, group, jnp.zeros((256, 128), F32))
            TE[a, :, 128 * h : 128 * h + 128] = extra.astype(BF16)

    ones = jnp.ones((16, 512), BF16)
    cot_sum = jnp.zeros((16, 512), F32)
    for n, arrivals in ((0, ()), (1, (1,)), (3, (3,)), (2, (4, 5))):
        for k in (1, 3, 4, 5):
            wait_t(n, k)
        for k in arrivals:
            for i in range(4):
                wait_c(i, k)
        row = wrap(y - n, 4)
        right = C[row].reshape(512, 512)
        part = lax.dot_general(
            T[row].reshape(512, 512), right, (((0,), (0,)), ((), ())), preferred_element_type=F32
        )
        if n:
            prod[0:512] += part
        else:
            prod[0:512] = part
        cot_sum += jnp.dot(ones, right, preferred_element_type=F32)

    small = SL[y].astype(F32)
    for d in (1, 2, 3):
        ref = SL.at[wrap(y - d, 4)]
        remote(ref, ref, s2s.at[d - 1], s2r.at[d - 1], at(dy=d)).wait_recv()
        small += SL[wrap(y - d, 4)].astype(F32)
    rest = jnp.where(y == 0, small, jnp.where(y == 1, pltpu.roll(small, 12, 0), pltpu.roll(small, 8, 0)))
    prod[512:528] = jnp.where(rows < jnp.where(y < 3, 4, 0), rest, 0.0)
    weight = gain[:, pl.ds(pl.multiple_of(512 * x, 128), 512)]
    for k in range(4):
        for i in range(4):
            start = 129 * k + 32 * i
            part = prod[start : start + 32]
            if i:
                part = jnp.where(x < i, prod[start + 1 : start + 33], part)
            zs[k, 32 * i : 32 * i + 32] = (part * weight).astype(BF16)
        extra = prod[129 * k + 32 : 129 * k + 33]
        for i in range(1, 4):
            extra = jnp.where(x == i, prod[129 * k + 32 * i + 32 : 129 * k + 32 * i + 33], extra)
        block = jnp.where(rows == 1, cot_sum * weight, jnp.where(rows == 2, small[12:13] + small[13:14], 0.0))
        zs[k, 128:144] = jnp.where(rows == 0, extra * weight, block).astype(BF16)

    keep_half = pl.ds(pl.multiple_of(256 * c, 128), 256)
    give_half = pl.ds(pl.multiple_of(256 * (1 - c), 128), 256)
    across = remote(zs.at[:, :, give_half], cr, cs.at[0], crs.at[0], at(dc=1))
    send(across)
    relay_h(0)
    across.wait_recv()
    for k in range(4):
        zb[k] = (zs[k, :, keep_half].astype(F32) + cr[k].astype(F32)).astype(BF16)

    for d in range(1, 8):
        send(remote(zb.at[lax.rem(z + d, 4)], zr.at[z], zss.at[d - 1], zrs.at[d - 1], at(dz=d)))
    zr[z] = zb[zl]
    ref = TT.at[x, 1 - c]
    remote(ref, ref, us.at[0], ur.at[0], at(dc=1)).wait_recv()
    def share(n, d, arrivals):
        for k in arrivals:
            wait_h(0, k)
        ref = TT.at[wrap(x + d, 4), c]
        send(remote(ref, ref, us.at[n], ur.at[n], at(dc=1)))

    def shared(n, d):
        ref = TT.at[wrap(x + d, 4), 1 - c]
        remote(ref, ref, us.at[n], ur.at[n], at(dc=1)).wait_recv()

    arrange(x)
    share(1, -1, (1,))
    share(2, 1, (3,))
    shared(1, -1)
    arrange(wrap(x - 1, 4))
    shared(2, 1)
    arrange(wrap(x + 1, 4))
    for d in (1, 2, 3):
        ref = PR.at[wrap(x - d, 4)]
        remote(ref, ref, ps.at[d - 1], prs.at[d - 1], at(dx=d)).wait_recv()
    for d in range(1, 8):
        ref = zr.at[wrap(z - d, 8)]
        remote(ref, ref, zss.at[d - 1], zrs.at[d - 1], at(dz=d)).wait_recv()
    group = zr[0].astype(F32)
    for k in range(1, 8):
        group += zr[k].astype(F32)

    def low_teacher(grad, mixed, old_one, old_two):
        new_one = beta_one * old_one + (1.0 - beta_one) * grad
        new_two = beta_two * old_two + (1.0 - beta_two) * grad * grad
        first = new_one / (1.0 - beta_one**STEP)
        second = new_two / (1.0 - beta_two**STEP)
        return mixed - ((1.0 - ema_rate) * learn_rate) * (first / (jnp.sqrt(second) + epsilon))

    for i in range(4):
        span = slice(32 * i, 32 * i + 32)
        W[y, zl, span] = low_teacher(group[span], *[PR[i, k, 0:32] for k in range(3)]).astype(BF16)
    first_row = iota((8, 256), 0) == 0
    extras = [jnp.where(first_row, PR[x, k, 32:40], PR[3, k, 32:40]) for k in range(3)]
    block = low_teacher(group[128:136], *extras)
    block = jnp.where(iota((8, 256), 0) < 3, block, 0.0)
    W[y, zl, 128:144] = jnp.concatenate([block, jnp.zeros((8, 256), F32)], axis=0).astype(BF16)

    parts = [pl.ds(0, 80), pl.ds(80, 64)]
    layers = [zl, wrap(zl - 1, 4), wrap(zl + 1, 4), wrap(zl + 2, 4)]
    spread_w, wait_w, relay_w = ring(
        lambda n, d, half: W.at[wrap(y + d, 4), layers[n], half], parts, along_y, w3s, w3r
    )
    for k, (ref, d) in enumerate(
        [(W.at[y, zl], 1), (W.at[y, zl], -1), (W.at[y, zl, parts[0]], 2), (W.at[y, zl, parts[1]], -2)]
    ):
        send(remote(ref, ref, w2s.at[k], w2r.at[k], at(dz=d)))
    spread_w(0)

    for i in range(4):
        xs[i, 0:32] = group[32 * i : 32 * i + 32]
        xs[i, 32:40] = group[128:136]
    slot = 2 * x + c
    others = [(dx, dc) for dx in range(4) for dc in range(2) if dx or dc]
    for n, (dx, dc) in enumerate(others):
        send(remote(xs.at[wrap(x + dx, 4)], xr.at[slot], xss.at[n], xrs.at[n], at(dx=dx, dc=dc)))
    xr[slot] = xs[x]

    for n, k in ((1, 0), (2, 1)):
        ref = W.at[y, layers[n]]
        remote(ref, ref, w2s.at[k], w2r.at[k], at(dz=1)).wait_recv()
        spread_w(n)
    for k in (2, 3):
        ref = W.at[y, layers[3], parts[k - 2]]
        remote(ref, ref, w2s.at[k], w2r.at[k], at(dz=1)).wait_recv()
    spread_w(3)
    relay_w(0)
    share(3, 2, (4, 5))
    relay_w(1)
    relay_w(2)

    def accumulate(i, a):
        total = jnp.zeros((256, 256), F32)
        for h in range(2):
            right = W[i, 2 * h : 2 * h + 2, 0:128].reshape(256, 256)
            total += jnp.dot(TP[2 * i + h, a], right, preferred_element_type=F32)
        return total

    relay_w(3)
    shared(3, 2)
    arrange(wrap(x + 2, 4))

    for n, (dx, dc) in enumerate(others):
        ref = xr.at[2 * wrap(x - dx, 4) + wrap(c - dc, 2)]
        remote(ref, ref, xss.at[n], xrs.at[n], at(dx=dx, dc=dc)).wait_recv()
    last = jnp.where(f == 63, 1.0, 0.0).astype(F32)
    pad[...] = jnp.zeros_like(pad)
    tg[...] = jnp.zeros_like(tg)
    for e in range(8):
        for t in range(2):
            n = 2 * e + t
            pad[n : n + 1] = xr[e, 33:34, 128 * t : 128 * t + 128] * last
            tg[TAIL + 240 + n : TAIL + 241 + n] = xr[e, 34:35, 128 * t : 128 * t + 128] * last
    rolled = roll_by(pad[0:24], place, 1, range(7))
    pad[0:24] = jnp.where(lanes24 >= lane_at, rolled, pltpu.roll(rolled, 1, 0))
    tg[TAIL : TAIL + 256] += roll_by(pad[...], place, 0, range(7, 15))
    lanes = iota((8, 128), 1)
    subs = iota((8, 128), 0)

    def update(where, grad, inside):
        old = master[where]
        new_one = beta_one * one[where] + (1.0 - beta_one) * grad
        new_two = beta_two * two[where] + (1.0 - beta_two) * grad * grad
        first = new_one / (1.0 - beta_one**STEP)
        second = new_two / (1.0 - beta_two**STEP)
        decay = jnp.where(inside, decay_rate, 0.0) * old
        new = old - learn_rate * (first / (jnp.sqrt(second) + epsilon) + decay)
        master_out[where] = new
        one_out[where] = new_one
        two_out[where] = new_two
        teacher_out[where] = ema_rate * teacher[where] + (1.0 - ema_rate) * new

    for b in range(4):
        for m in range(4):
            for t in range(4):
                base = 128 * b + 4 * m + t
                where = (pl.ds(base, 8, stride=16), slice(None))
                e, side = 2 * wrap(x + m, 4) + t // 2, slice(128 * (t % 2), 128 * (t % 2) + 128)
                slots = 128 * base + 2048 * subs + lanes
                update(where, xr[e, 8 * b : 8 * b + 8, side] + tg[where], slots < limit)
    for t in range(4):
        where = (slice(512 + t, 513 + t), slice(None))
        e, side = 2 * x + t // 2, slice(128 * (t % 2), 128 * (t % 2) + 128)
        inside = jnp.full((1, 128), 65536, jnp.int32) < limit
        update(where, xr[e, 32:33, side] * (1.0 - last) + tg[where], inside)
    results = [
        pltpu.make_async_copy(src, dst, res_sem.at[k])
        for k, (src, dst) in enumerate(
            [(master_out, master_res), (one_out, one_res), (two_out, two_res), (teacher_out, teacher_res)]
        )
    ]
    for copy in results:
        copy.start()

    def begin(a, carry):
        acc[a] = accumulate(y, a)
        return carry

    lax.fori_loop(0, 4, begin, 0)
    for d, arrivals in ((-1, (1,)), (1, (3,)), (2, (4, 5))):
        for n in range(4):
            for k in arrivals:
                wait_w(n, k)
        if d != 2:

            def more(a, carry):
                acc[a] += accumulate(wrap(y + d, 4), a)
                return carry

            lax.fori_loop(0, 4, more, 0)

    bias_t = W[3, 3, 128:144].astype(F32)[1:2]
    scale_t = W[3, 3, 128:144].astype(F32)[2:3]
    ends = W[:, :, 128:144].reshape(256, 256)
    out_cols = branch_res.at[:, pl.ds(pl.multiple_of(256 * slot, 128), 256)]
    n = 0
    for d in (2, 1, 3, 0):
        a = wrap(x + d, 4)
        total = acc[a] + accumulate(wrap(y + 2, 4), a) + jnp.dot(TE[a], ends, preferred_element_type=F32)
        OUT[a] = (scale_t * (total + bias_t)).astype(BF16).reshape(2, 128, 256)
        for dc in range(2):
            core = wrap(c + dc, 2)
            if d or dc:
                send(remote(OUT.at[a, core], out_cols, os.at[n], orr.at[slot], at(dx=d, dc=dc)))
                n += 1
    stay = pltpu.make_async_copy(OUT.at[x, c], out_cols, own_sem.at[1])
    stay.start()
    for n, (dx, dc) in enumerate(others):
        e = 2 * wrap(x - dx, 4) + wrap(c - dc, 2)
        ref = branch_res.at[:, pl.ds(pl.multiple_of(256 * e, 128), 256)]
        remote(ref, ref, os.at[n], orr.at[e], at(dc=1)).wait_recv()
    stay.wait()
    for copy in results:
        copy.wait()
    for copy in pending:
        copy.wait_send()


def copy_kernel(*refs):
    sems = refs[15]
    loads = [pltpu.make_async_copy(refs[k], refs[10 + k], sems.at[k]) for k in range(5)]
    stores = [pltpu.make_async_copy(refs[10 + k], refs[5 + k], sems.at[5 + k]) for k in range(5)]
    for copy in loads:
        copy.start()
    for load, store in zip(loads, stores):
        load.wait()
        store.start()
    for copy in stores:
        copy.wait()


def per_device(
    tokens, cotangent, saved_branch, layer_gain, offsets, master, moment_one, moment_two, teacher, teacher_tokens
):
    anyspace = pl.BlockSpec(memory_space=pl.ANY)
    dma = pltpu.SemaphoreType.DMA
    flat = jax.ShapeDtypeStruct((FLAT, 128), F32)
    shard = pltpu.VMEM((FLAT, 128), F32)
    rows = pltpu.VMEM((128, WIDTH), BF16)
    results = [flat] * 4 + [jax.ShapeDtypeStruct((128, WIDTH), BF16)]
    outs = pl.pallas_call(
        kernel,
        out_shape=results,
        in_specs=[pl.BlockSpec(memory_space=pltpu.SMEM)] + [anyspace] * 9,
        out_specs=[anyspace] * 5,
        scratch_shapes=[
            pltpu.VMEM((1, WIDTH), F32),
            rows, rows, rows,
            shard, shard, shard, shard, shard, shard, shard, shard, shard,
            pltpu.VMEM((4, 128, 512), BF16),
            pltpu.VMEM((4, 4, 128, 512), BF16),
            pltpu.VMEM((4, 4, 128, 512), BF16),
            pltpu.VMEM((4, 16, 512), BF16),
            pltpu.VMEM((4, 16, 512), BF16),
            pltpu.VMEM((4, 16, 512), BF16),
            pltpu.VMEM((528, 512), F32),
            pltpu.VMEM((4, GROUP, 512), BF16),
            pltpu.VMEM((4, GROUP, 256), BF16),
            pltpu.VMEM((4, GROUP, 256), BF16),
            pltpu.VMEM((8, GROUP, 256), BF16),
            pltpu.VMEM((4, 3, 40, 256), F32),
            pltpu.VMEM((4, 3, 40, 256), F32),
            pltpu.VMEM((4, 40, 256), F32),
            pltpu.VMEM((8, 40, 256), F32),
            pltpu.VMEM((256, 128), F32),
            pltpu.VMEM((520, 128), F32),
            pltpu.VMEM((4, 2, 128, WIDTH), BF16),
            pltpu.VMEM((8, 384, 384), BF16),
            pltpu.VMEM((8, 4, 256, 256), BF16),
            pltpu.VMEM((4, 256, 256), BF16),
            pltpu.VMEM((4, 4, GROUP, 256), BF16),
            pltpu.VMEM((4, 256, 256), F32),
            pltpu.VMEM((4, 2, 128, 256), BF16),
            dma((9,)), dma((4,)), dma((2,)),
            dma((3,)), dma((3,)), dma((3,)), dma((3,)), dma((3,)), dma((3,)), dma((3,)), dma((3,)),
            dma((4, 6)), dma((4, 6)), dma((4, 6)), dma((4, 6)),
            dma((1,)), dma((1,)), dma((7,)), dma((7,)),
            dma((3,)), dma((3,)), dma((7,)), dma((7,)),
            dma((1, 6)), dma((1, 6)), dma((4,)), dma((4,)), dma((4,)), dma((4,)), dma((4, 6)), dma((4, 6)),
            dma((7,)), dma((8,)),
        ],
        compiler_params=pltpu.CompilerParams(collective_id=0, has_side_effects=True, vmem_limit_bytes=56 << 20),
        name="step",
    )(
        offsets, layer_gain.reshape(1, WIDTH), tokens, cotangent, saved_branch,
        *[a.reshape(FLAT, 128) for a in (master, moment_one, moment_two, teacher)], teacher_tokens,
    )
    outs = pl.pallas_call(
        copy_kernel,
        out_shape=results,
        in_specs=[anyspace] * 5,
        out_specs=[anyspace] * 5,
        scratch_shapes=[shard, shard, shard, shard, rows, dma((10,))],
        name="place",
    )(*outs)
    return tuple(a.reshape(SHARD) for a in outs[:4]) + (outs[4],)


def solution(mesh):
    rows = P(("fsdp", "dp"), None)
    return jax.shard_map(
        per_device,
        mesh=mesh,
        in_specs=(rows, rows, rows, P(), P(), P("fsdp"), P("fsdp"), P("fsdp"), P("fsdp"), rows),
        out_specs=(P("fsdp"), P("fsdp"), P("fsdp"), P("fsdp"), rows),
        check_vma=False,
    )
```

```python
import jax
import jax.numpy as jnp
from jax import lax
from jax.experimental import pallas as pl
from jax.experimental.pallas import tpu as pltpu
from jax.sharding import PartitionSpec as P

MESH = pl.DeviceIdType.MESH
F32 = jnp.float32
BF16 = jnp.bfloat16

STEP = 1000
beta_one = 0.9
beta_two = 0.999
learn_rate = 0.001
decay_rate = 0.04
ema_rate = 0.994
epsilon = 1e-08

WIDTH = 2048
PROJ = WIDTH * WIDTH
SHARD = 66048
FLAT = SHARD // 128
TAIL = 260
GROUP = 144


def wrap(value, size):
    return lax.rem(value + size, size)


def device(x, y, z, c):
    return (y * 16 + lax.rem(z, 4) * 4 + x, lax.div(z, 4) * 2 + c)


def remote(src, dst, send, recv, to):
    return pltpu.make_async_remote_copy(
        src_ref=src, dst_ref=dst, send_sem=send, recv_sem=recv, device_id=to, device_id_type=MESH
    )


def roll_by(value, amount, axis, bits):
    for bit in bits:
        on = jnp.broadcast_to(lax.rem(lax.div(amount, 2**bit), 2) == 1, value.shape)
        value = jnp.where(on, pltpu.roll(value, 2 ** (bit - bits[0]), axis), value)
    return value


def iota(shape, axis):
    return lax.broadcasted_iota(jnp.int32, shape, axis)


def kernel(
    offsets, gain_hbm, tokens_hbm, cot_hbm, saved_hbm, master_hbm, one_hbm, two_hbm, teacher_hbm, tt_hbm,
    master_res, one_res, two_res, teacher_res, branch_res,
    gain, tok, cot, saved, master, one, two, teacher, mix, master_out, one_out, two_out, teacher_out,
    TW, T, C, SX, SL, SS, prod, zs, cr, zb, zr, PS, PR, both, xs, xr, pad, tg, TT, S, TP, TE, W, acc, OUT,
    in_sem, res_sem, own_sem, a1s, a1r, b1s, b1r, s1s, s1r, s2s, s2r, a2s, a2r, b2s, b2r, cs, crs, zss, zrs,
    ps, prs, xss, xrs, ts, tr, us, ur, w2s, w2r, w3s, w3r, hs, hr, os, orr,
):
    f = lax.axis_index("fsdp")
    p = lax.axis_index("dp")
    x = lax.rem(f, 4)
    zl = lax.rem(lax.div(f, 4), 4)
    y = lax.div(f, 16)
    c = lax.rem(p, 2)
    z = lax.div(p, 2) * 4 + zl

    def at(dx=0, dy=0, dz=0, dc=0):
        return device(wrap(x + dx, 4), wrap(y + dy, 4), wrap(z + dz, 8), wrap(c + dc, 2))

    partners = (
        [dict(dx=d) for d in (1, 2, 3)]
        + [dict(dy=d) for d in (1, 2, 3)]
        + [dict(dz=d) for d in range(1, 8)]
        + [dict(dx=d, dc=1) for d in range(4)]
    )
    h = lax.div(z, 4)
    loads = [
        pltpu.make_async_copy(src, dst, in_sem.at[k])
        for k, (src, dst) in enumerate(
            [
                (tokens_hbm, tok), (cot_hbm, cot), (saved_hbm, saved), (tt_hbm, TT.at[x, c]), (gain_hbm, gain),
                (master_hbm, master), (one_hbm, one), (two_hbm, two), (teacher_hbm, teacher),
            ]
        )
    ]
    for copy in loads:
        copy.start()
    barrier = pltpu.get_barrier_semaphore()
    for partner in partners:
        pl.semaphore_signal(barrier, inc=1, device_id=at(**partner), device_id_type=MESH)
    pl.semaphore_wait(barrier, len(partners))

    pending = []

    def send(copy):
        copy.start()
        pending.append(copy)

    def ring(view, halves, to, sends, recvs):
        def spread(n):
            for k, (half, d) in enumerate([(0, 1), (1, 1), (1, -1), (0, -1)]):
                ref = view(n, 0, halves[half])
                send(remote(ref, ref, sends.at[n, k], recvs.at[n, k], to(d)))

        def wait(n, k):
            half, d = [(0, -1), (1, -1), (1, 1), (0, 1), (0, -2), (1, 2)][k]
            ref = view(n, d, halves[half])
            remote(ref, ref, sends.at[n, k], recvs.at[n, k], to(1)).wait_recv()
            return ref

        def relay(n):
            for k, d in ((0, 1), (2, -1)):
                ref = wait(n, k)
                send(remote(ref, ref, sends.at[n, 4 + k // 2], recvs.at[n, 4 + k // 2], to(d)))

        return spread, wait, relay

    halves = [pl.ds(0, 64), pl.ds(64, 64)]
    along_x = lambda d: at(dx=d)
    along_y = lambda d: at(dy=d)
    spread_t, wait_t, relay_t = ring(
        lambda n, d, half: T.at[wrap(y - n, 4), wrap(x + d, 4), half], halves, along_x, a2s, a2r
    )
    spread_c, wait_c, relay_c = ring(
        lambda n, d, half: C.at[wrap(y + d, 4), wrap(x - n, 4), half], halves, along_y, b2s, b2r
    )
    spread_h, wait_h, relay_h = ring(
        lambda n, d, half: TT.at[wrap(x + d, 4), c, half], halves, along_x, ts, tr
    )

    def quarter(i):
        return cot_hbm.at[:, pl.ds(pl.multiple_of(512 * i, 128), 512)]

    mine = pltpu.make_async_copy(quarter(x), C.at[y, x], own_sem.at[0])
    mine.start()
    for d in (1, 2, 3):
        send(remote(quarter(wrap(x + d, 4)), C.at[y, x], b1s.at[d - 1], b1r.at[d - 1], at(dx=d)))
    loads[0].wait()
    for i in range(4):
        end = min(512 * i + 640, WIDTH)
        window = tok[:, 512 * i : end].astype(F32)
        if i:
            window = pltpu.roll(window, end - 512 * i - 4 * i, 1)[:, :512]
        else:
            window = window[:, :512]
        if i == 3:
            window = jnp.where(iota((128, 512), 1) < 500, window, 0.0)
        TW[i] = window.astype(BF16)
    for d in (1, 2, 3):
        send(remote(TW.at[wrap(y + d, 4)], T.at[y, x], a1s.at[d - 1], a1r.at[d - 1], at(dy=d)))
    T[y, x] = TW[y]
    spread_t(0)
    mine.wait()
    spread_c(0)
    loads[3].wait()
    send(remote(TT.at[x, c], TT.at[x, c], us.at[0], ur.at[0], at(dc=1)))
    loads[1].wait()
    loads[2].wait()
    total = jnp.zeros((1, WIDTH), F32)
    for r in range(0, 128, 16):
        total += jnp.sum(cot[r : r + 16].astype(F32) * saved[r : r + 16].astype(F32), axis=0, keepdims=True)
    top = total.astype(BF16).astype(F32)
    lane = iota((128, 128), 1)
    left = jnp.zeros((128, 128), F32)
    for i in range(3):
        tile = tok[:, 512 * (i + 1) : 512 * (i + 1) + 128].astype(F32)
        left = jnp.where(jnp.logical_and(lane >= 4 * i, lane < 4 * i + 4), tile, left)
    rows = iota((16, 512), 0)
    for i in range(4):
        side = slice(512 * i, 512 * i + 512)
        part = lax.dot_general(
            left.astype(BF16), cot[:, side], (((0,), (0,)), ((), ())), preferred_element_type=F32
        )[:16]
        part = jnp.where(rows == 12, top[:, side], jnp.where(rows == 13, total[:, side] - top[:, side], part))
        SS[i] = part.astype(BF16)
    for d in (1, 2, 3):
        send(remote(SS.at[wrap(x + d, 4)], SX.at[x], s1s.at[d - 1], s1r.at[d - 1], at(dx=d)))
    SX[x] = SS[x]

    for d, before in ((1, 0), (3, 1), (2, 3)):
        ref = T.at[wrap(y - d, 4), x]
        remote(ref, ref, a1s.at[d - 1], a1r.at[d - 1], at(dy=d)).wait_recv()
        spread_t(d)
        ref = C.at[y, wrap(x - d, 4)]
        remote(ref, ref, b1s.at[d - 1], b1r.at[d - 1], at(dx=d)).wait_recv()
        spread_c(d)
        relay_t(before)
        relay_c(before)

    for d in (1, 2, 3):
        ref = SX.at[wrap(x - d, 4)]
        remote(ref, ref, s1s.at[d - 1], s1r.at[d - 1], at(dx=d)).wait_recv()
    small = jnp.zeros((16, 512), F32)
    for i in range(4):
        small += SX[i].astype(F32)
    total = small[12:13] + small[13:14]
    top = total.astype(BF16).astype(F32)
    SL[y] = jnp.where(rows == 12, top, jnp.where(rows == 13, total - top, small)).astype(BF16)
    for d in (1, 2, 3):
        send(remote(SL.at[y], SL.at[y], s2s.at[d - 1], s2r.at[d - 1], at(dy=d)))

    for copy in loads[4:]:
        copy.wait()
    limit = PROJ - SHARD * f
    spots = 128 * iota((FLAT, 128), 0) + iota((FLAT, 128), 1)
    keep = jnp.where(spots < limit, 1.0 - learn_rate * decay_rate, 1.0)
    mix[...] = ema_rate * teacher[...] + (1.0 - ema_rate) * keep * master[...]
    place = jnp.full((1, 128), offsets[1] - PROJ, jnp.int32)
    row_back = lax.rem(32768 - lax.div(place, 128) * 128, 32768)
    lane_at = lax.rem(place, 128)
    lane_back = lax.rem(128 - lane_at, 128)
    lanes24 = iota((24, 128), 1)
    mine_of = lambda four: jnp.where(
        c == 0, jnp.where(h == 0, four[0], four[1]), jnp.where(h == 0, four[2], four[3])
    )
    for k, source in enumerate((mix, one, two)):
        for b in range(4):
            for m in range(4):
                four = [source[pl.ds(128 * b + 4 * m + t, 8, stride=16), :] for t in range(4)]
                PS[wrap(x + m, 4), k, 8 * b : 8 * b + 8] = mine_of(four)
        tail = source[TAIL : TAIL + 256]
        moved = roll_by(tail, row_back, 0, range(7, 15))[0:24]
        rolled = roll_by(moved, lane_back, 1, range(7))
        bias = jnp.where(lanes24 < 128 - lane_at, rolled, pltpu.roll(rolled, 23, 0))
        for m in range(4):
            PS[m, k, 32:33] = mine_of([source[512 + t : 513 + t] for t in range(4)])
            PS[m, k, 33:34] = mine_of([bias[4 * m + t : 4 * m + t + 1] for t in range(4)])
            PS[m, k, 34:35] = mine_of([tail[240 + 4 * m + t : 241 + 4 * m + t] for t in range(4)])
            PS[m, k, 35:40] = jnp.zeros((5, 128), F32)

    relay_t(2)
    relay_c(2)
    for d in (1, 2, 3):
        send(remote(PS.at[wrap(x + d, 4)], PR.at[x], ps.at[d - 1], prs.at[d - 1], at(dx=d)))
    PR[x] = PS[x]
    spread_h(0)

    def one_hot(g, carry):
        col = iota((1, 384), 1)
        i = lax.div(lax.rem(col, 128), 32)
        source = 258 * g + lax.div(col, 128) * 129 + lax.rem(col, 128) + jnp.where(i > x, 1, 0)
        slot = lax.rem(col, 128) - 32 * lax.rem(g, 4)
        extra = 258 * g + 32 * x + 32 + jnp.where(slot == 0, 0, 129)
        extra = jnp.where(jnp.logical_or(slot == 0, slot == 16), extra, -1)
        source = jnp.where(col < 256, source, extra) - jnp.minimum(256 * g, WIDTH - 384)
        S[g] = jnp.where(iota((384, 384), 0) == source, 1.0, 0.0).astype(BF16)
        return carry

    lax.fori_loop(0, 8, one_hot, 0)

    def arrange(a):
        def group(g, extra):
            start = pl.multiple_of(jnp.minimum(256 * g, WIDTH - 384), 128)
            block = TT[a, :, :, pl.ds(start, 384)].reshape(256, 384)
            part = jnp.dot(block, S[g], preferred_element_type=F32)
            TP[g, a] = part[:, :256].astype(BF16)
            return extra + part[:, 256:]

        for h in range(2):
            extra = lax.fori_loop(4 * h, 4 * h + 4, group, jnp.zeros((256, 128), F32))
            TE[a, :, 128 * h : 128 * h + 128] = extra.astype(BF16)

    ones = jnp.ones((16, 512), BF16)
    cot_sum = jnp.zeros((16, 512), F32)
    for n, arrivals in ((0, ()), (1, (1,)), (3, (3,)), (2, (4, 5))):
        for k in (1, 3, 4, 5):
            wait_t(n, k)
        for k in arrivals:
            for i in range(4):
                wait_c(i, k)
        row = wrap(y - n, 4)
        right = C[row].reshape(512, 512)
        part = lax.dot_general(
            T[row].reshape(512, 512), right, (((0,), (0,)), ((), ())), preferred_element_type=F32
        )
        if n:
            prod[0:512] += part
        else:
            prod[0:512] = part
        cot_sum += jnp.dot(ones, right, preferred_element_type=F32)

    small = SL[y].astype(F32)
    for d in (1, 2, 3):
        ref = SL.at[wrap(y - d, 4)]
        remote(ref, ref, s2s.at[d - 1], s2r.at[d - 1], at(dy=d)).wait_recv()
        small += SL[wrap(y - d, 4)].astype(F32)
    rest = jnp.where(y == 0, small, jnp.where(y == 1, pltpu.roll(small, 12, 0), pltpu.roll(small, 8, 0)))
    prod[512:528] = jnp.where(rows < jnp.where(y < 3, 4, 0), rest, 0.0)
    keep_half = pl.ds(pl.multiple_of(256 * c, 128), 256)
    give_half = pl.ds(pl.multiple_of(256 * (1 - c), 128), 256)
    weight = gain[:, pl.ds(pl.multiple_of(512 * x, 128), 512)]
    for k in range(4):
        for i in range(4):
            start = 129 * k + 32 * i
            part = prod[start : start + 32]
            if i:
                part = jnp.where(x < i, prod[start + 1 : start + 33], part)
            zs[k, 32 * i : 32 * i + 32] = (part * weight).astype(BF16)
        extra = prod[129 * k + 32 : 129 * k + 33]
        for i in range(1, 4):
            extra = jnp.where(x == i, prod[129 * k + 32 * i + 32 : 129 * k + 32 * i + 33], extra)
        block = jnp.where(rows == 1, cot_sum * weight, jnp.where(rows == 2, small[12:13] + small[13:14], 0.0))
        zs[k, 128:144] = jnp.where(rows == 0, extra * weight, block).astype(BF16)
        send(remote(zs.at[k, :, give_half], cr.at[k], cs.at[k], crs.at[k], at(dc=1)))
    relay_h(0)

    for j in range(4):
        k = wrap(zl + j, 4)
        remote(zs.at[k, :, give_half], cr.at[k], cs.at[k], crs.at[k], at(dc=1)).wait_recv()
        chip = (zs[k, :, keep_half].astype(F32) + cr[k].astype(F32)).astype(BF16)
        zb[k] = chip[:, :128]
        zb[4 + k] = chip[:, 128:]
        for d in (j, j + 4):
            if d:
                to_z = wrap(z + d, 8)
                send(remote(zb.at[to_z], zr.at[z], zss.at[d - 1], zrs.at[d - 1], at(dz=d)))
    zr[z] = zb[z]

    def share(n, d, arrivals):
        for k in arrivals:
            wait_h(0, k)
        ref = TT.at[wrap(x + d, 4), c]
        send(remote(ref, ref, us.at[n], ur.at[n], at(dc=1)))

    def shared(n, d):
        ref = TT.at[wrap(x + d, 4), 1 - c]
        remote(ref, ref, us.at[n], ur.at[n], at(dc=1)).wait_recv()

    shared(0, 0)
    arrange(x)
    for d in (1, 2, 3):
        ref = PR.at[wrap(x - d, 4)]
        remote(ref, ref, ps.at[d - 1], prs.at[d - 1], at(dx=d)).wait_recv()
    for d in range(1, 8):
        ref = zr.at[wrap(z - d, 8)]
        remote(ref, ref, zss.at[d - 1], zrs.at[d - 1], at(dz=d)).wait_recv()
    group = zr[0].astype(F32)
    for k in range(1, 8):
        group += zr[k].astype(F32)

    def low_teacher(grad, mixed, old_one, old_two):
        new_one = beta_one * old_one + (1.0 - beta_one) * grad
        new_two = beta_two * old_two + (1.0 - beta_two) * grad * grad
        first = new_one / (1.0 - beta_one**STEP)
        second = new_two / (1.0 - beta_two**STEP)
        return mixed - ((1.0 - ema_rate) * learn_rate) * (first / (jnp.sqrt(second) + epsilon))

    for i in range(4):
        span = slice(32 * i, 32 * i + 32)
        W[h, y, zl, span] = low_teacher(group[span], *[PR[i, k, 0:32] for k in range(3)]).astype(BF16)
    first_row = iota((8, 128), 0) == 0
    extras = [jnp.where(first_row, PR[x, k, 32:40], PR[3, k, 32:40]) for k in range(3)]
    block = low_teacher(group[128:136], *extras)
    block = jnp.where(iota((8, 128), 0) < 3, block, 0.0)
    W[h, y, zl, 128:144] = jnp.concatenate([block, jnp.zeros((8, 128), F32)], axis=0).astype(BF16)

    parts = [pl.ds(0, 80), pl.ds(80, 64)]
    away = [0, -1, 1, -2, 2, -3, 3, 4]

    def block_of(n, d, half=None):
        owner = wrap(z + away[n], 8)
        ref = W.at[lax.div(owner, 4), wrap(y + d, 4), lax.rem(owner, 4)]
        return ref if half is None else ref.at[half]

    spread_w, wait_w, relay_w = ring(block_of, parts, along_y, w3s, w3r)
    own = block_of(0, 0)
    for n in range(1, 8):
        send(remote(own, own, w2s.at[n - 1], w2r.at[n - 1], at(dz=-away[n])))
    spread_w(0)

    both[h] = group[0:136]
    twin = remote(both.at[h], both.at[h], hs.at[0], hr.at[0], at(dz=4))
    send(twin)

    def follow(n):
        ref = block_of(n, 0)
        remote(ref, ref, w2s.at[n - 1], w2r.at[n - 1], at(dz=-away[n])).wait_recv()
        spread_w(n)
        relay_w(n - 1)

    share(1, -1, (1,))
    share(2, 1, (3,))
    follow(1)
    follow(2)
    follow(3)
    follow(4)
    shared(1, -1)
    arrange(wrap(x - 1, 4))
    follow(5)
    follow(6)
    follow(7)

    ref = both.at[1 - h]
    remote(ref, ref, hs.at[0], hr.at[0], at(dz=4)).wait_recv()
    for i in range(4):
        for k in range(2):
            side = slice(128 * k, 128 * k + 128)
            xs[i, 0:32, side] = both[k, 32 * i : 32 * i + 32]
            xs[i, 32:40, side] = both[k, 128:136]
    slot = 2 * x + c
    others = [(dx, dc) for dx in range(4) for dc in range(2) if dx or dc]
    for n, (dx, dc) in enumerate(others):
        send(remote(xs.at[wrap(x + dx, 4)], xr.at[slot], xss.at[n], xrs.at[n], at(dx=dx, dc=dc)))
    xr[slot] = xs[x]
    share(3, 2, (4, 5))
    relay_w(7)
    shared(2, 1)
    arrange(wrap(x + 1, 4))

    def accumulate(i, a):
        total = jnp.zeros((256, 256), F32)
        for k in range(2):
            sides = [W[n, i, 2 * k : 2 * k + 2, 0:128].reshape(256, 128) for n in range(2)]
            right = jnp.concatenate(sides, axis=1)
            total += jnp.dot(TP[2 * i + k, a], right, preferred_element_type=F32)
        return total


    for n, (dx, dc) in enumerate(others):
        ref = xr.at[2 * wrap(x - dx, 4) + wrap(c - dc, 2)]
        remote(ref, ref, xss.at[n], xrs.at[n], at(dx=dx, dc=dc)).wait_recv()
    last = jnp.where(f == 63, 1.0, 0.0).astype(F32)
    pad[...] = jnp.zeros_like(pad)
    tg[...] = jnp.zeros_like(tg)
    for e in range(8):
        for t in range(2):
            n = 2 * e + t
            pad[n : n + 1] = xr[e, 33:34, 128 * t : 128 * t + 128] * last
            tg[TAIL + 240 + n : TAIL + 241 + n] = xr[e, 34:35, 128 * t : 128 * t + 128] * last
    rolled = roll_by(pad[0:24], place, 1, range(7))
    pad[0:24] = jnp.where(lanes24 >= lane_at, rolled, pltpu.roll(rolled, 1, 0))
    tg[TAIL : TAIL + 256] += roll_by(pad[...], place, 0, range(7, 15))
    lanes = iota((8, 128), 1)
    subs = iota((8, 128), 0)

    def update(where, grad, inside):
        old = master[where]
        new_one = beta_one * one[where] + (1.0 - beta_one) * grad
        new_two = beta_two * two[where] + (1.0 - beta_two) * grad * grad
        first = new_one / (1.0 - beta_one**STEP)
        second = new_two / (1.0 - beta_two**STEP)
        decay = jnp.where(inside, decay_rate, 0.0) * old
        new = old - learn_rate * (first / (jnp.sqrt(second) + epsilon) + decay)
        master_out[where] = new
        one_out[where] = new_one
        two_out[where] = new_two
        teacher_out[where] = ema_rate * teacher[where] + (1.0 - ema_rate) * new

    for b in range(4):
        for m in range(4):
            for t in range(4):
                base = 128 * b + 4 * m + t
                where = (pl.ds(base, 8, stride=16), slice(None))
                e, side = 2 * wrap(x + m, 4) + t // 2, slice(128 * (t % 2), 128 * (t % 2) + 128)
                slots = 128 * base + 2048 * subs + lanes
                update(where, xr[e, 8 * b : 8 * b + 8, side] + tg[where], slots < limit)
    for t in range(4):
        where = (slice(512 + t, 513 + t), slice(None))
        e, side = 2 * x + t // 2, slice(128 * (t % 2), 128 * (t % 2) + 128)
        inside = jnp.full((1, 128), 65536, jnp.int32) < limit
        update(where, xr[e, 32:33, side] * (1.0 - last) + tg[where], inside)
    results = [
        pltpu.make_async_copy(src, dst, res_sem.at[k])
        for k, (src, dst) in enumerate(
            [(master_out, master_res), (one_out, one_res), (two_out, two_res), (teacher_out, teacher_res)]
        )
    ]
    for copy in results:
        copy.start()

    shared(3, 2)
    arrange(wrap(x + 2, 4))

    def begin(a, carry):
        acc[a] = accumulate(y, a)
        return carry

    lax.fori_loop(0, 4, begin, 0)
    for d, arrivals in ((-1, (1,)), (1, (3,)), (2, (4, 5))):
        for n in range(8):
            for k in arrivals:
                wait_w(n, k)
        if d != 2:

            def more(a, carry):
                acc[a] += accumulate(wrap(y + d, 4), a)
                return carry

            lax.fori_loop(0, 4, more, 0)

    ends = jnp.concatenate([W[n, :, :, 128:144].reshape(256, 128) for n in range(2)], axis=1)
    tail = ends[240:256].astype(F32)
    bias_t, scale_t = tail[1:2], tail[2:3]
    out_cols = branch_res.at[:, pl.ds(pl.multiple_of(256 * slot, 128), 256)]
    n = 0
    for d in (2, 1, 3, 0):
        a = wrap(x + d, 4)
        total = acc[a] + accumulate(wrap(y + 2, 4), a) + jnp.dot(TE[a], ends, preferred_element_type=F32)
        OUT[a] = (scale_t * (total + bias_t)).astype(BF16).reshape(2, 128, 256)
        for dc in range(2):
            core = wrap(c + dc, 2)
            if d or dc:
                send(remote(OUT.at[a, core], out_cols, os.at[n], orr.at[slot], at(dx=d, dc=dc)))
                n += 1
    stay = pltpu.make_async_copy(OUT.at[x, c], out_cols, own_sem.at[1])
    stay.start()
    for n, (dx, dc) in enumerate(others):
        e = 2 * wrap(x - dx, 4) + wrap(c - dc, 2)
        ref = branch_res.at[:, pl.ds(pl.multiple_of(256 * e, 128), 256)]
        remote(ref, ref, os.at[n], orr.at[e], at(dc=1)).wait_recv()
    stay.wait()
    for copy in results:
        copy.wait()
    for copy in pending:
        copy.wait_send()


def copy_kernel(*refs):
    sems = refs[15]
    loads = [pltpu.make_async_copy(refs[k], refs[10 + k], sems.at[k]) for k in range(5)]
    stores = [pltpu.make_async_copy(refs[10 + k], refs[5 + k], sems.at[5 + k]) for k in range(5)]
    for copy in loads:
        copy.start()
    for load, store in zip(loads, stores):
        load.wait()
        store.start()
    for copy in stores:
        copy.wait()


def per_device(
    tokens, cotangent, saved_branch, layer_gain, offsets, master, moment_one, moment_two, teacher, teacher_tokens
):
    anyspace = pl.BlockSpec(memory_space=pl.ANY)
    dma = pltpu.SemaphoreType.DMA
    flat = jax.ShapeDtypeStruct((FLAT, 128), F32)
    shard = pltpu.VMEM((FLAT, 128), F32)
    rows = pltpu.VMEM((128, WIDTH), BF16)
    results = [flat] * 4 + [jax.ShapeDtypeStruct((128, WIDTH), BF16)]
    outs = pl.pallas_call(
        kernel,
        out_shape=results,
        in_specs=[pl.BlockSpec(memory_space=pltpu.SMEM)] + [anyspace] * 9,
        out_specs=[anyspace] * 5,
        scratch_shapes=[
            pltpu.VMEM((1, WIDTH), F32),
            rows, rows, rows,
            shard, shard, shard, shard, shard, shard, shard, shard, shard,
            pltpu.VMEM((4, 128, 512), BF16),
            pltpu.VMEM((4, 4, 128, 512), BF16),
            pltpu.VMEM((4, 4, 128, 512), BF16),
            pltpu.VMEM((4, 16, 512), BF16),
            pltpu.VMEM((4, 16, 512), BF16),
            pltpu.VMEM((4, 16, 512), BF16),
            pltpu.VMEM((528, 512), F32),
            pltpu.VMEM((4, GROUP, 512), BF16),
            pltpu.VMEM((4, GROUP, 256), BF16),
            pltpu.VMEM((8, GROUP, 128), BF16),
            pltpu.VMEM((8, GROUP, 128), BF16),
            pltpu.VMEM((4, 3, 40, 128), F32),
            pltpu.VMEM((4, 3, 40, 128), F32),
            pltpu.VMEM((2, 136, 128), F32),
            pltpu.VMEM((4, 40, 256), F32),
            pltpu.VMEM((8, 40, 256), F32),
            pltpu.VMEM((256, 128), F32),
            pltpu.VMEM((520, 128), F32),
            pltpu.VMEM((4, 2, 128, WIDTH), BF16),
            pltpu.VMEM((8, 384, 384), BF16),
            pltpu.VMEM((8, 4, 256, 256), BF16),
            pltpu.VMEM((4, 256, 256), BF16),
            pltpu.VMEM((2, 4, 4, GROUP, 128), BF16),
            pltpu.VMEM((4, 256, 256), F32),
            pltpu.VMEM((4, 2, 128, 256), BF16),
            dma((9,)), dma((4,)), dma((2,)),
            dma((3,)), dma((3,)), dma((3,)), dma((3,)), dma((3,)), dma((3,)), dma((3,)), dma((3,)),
            dma((4, 6)), dma((4, 6)), dma((4, 6)), dma((4, 6)),
            dma((4,)), dma((4,)), dma((7,)), dma((7,)),
            dma((3,)), dma((3,)), dma((7,)), dma((7,)),
            dma((1, 6)), dma((1, 6)), dma((4,)), dma((4,)), dma((7,)), dma((7,)), dma((8, 6)), dma((8, 6)),
            dma((1,)), dma((1,)),
            dma((7,)), dma((8,)),
        ],
        compiler_params=pltpu.CompilerParams(collective_id=0, has_side_effects=True, vmem_limit_bytes=56 << 20),
        name="step",
    )(
        offsets, layer_gain.reshape(1, WIDTH), tokens, cotangent, saved_branch,
        *[a.reshape(FLAT, 128) for a in (master, moment_one, moment_two, teacher)], teacher_tokens,
    )
    outs = pl.pallas_call(
        copy_kernel,
        out_shape=results,
        in_specs=[anyspace] * 5,
        out_specs=[anyspace] * 5,
        scratch_shapes=[shard, shard, shard, shard, rows, dma((10,))],
        name="place",
    )(*outs)
    return tuple(a.reshape(SHARD) for a in outs[:4]) + (outs[4],)


def solution(mesh):
    rows = P(("fsdp", "dp"), None)
    return jax.shard_map(
        per_device,
        mesh=mesh,
        in_specs=(rows, rows, rows, P(), P(), P("fsdp"), P("fsdp"), P("fsdp"), P("fsdp"), rows),
        out_specs=(P("fsdp"), P("fsdp"), P("fsdp"), P("fsdp"), rows),
        check_vma=False,
    )
```

```python
import jax
import jax.numpy as jnp
from jax import lax
from jax.experimental import pallas as pl
from jax.experimental.pallas import tpu as pltpu
from jax.sharding import PartitionSpec as P

MESH = pl.DeviceIdType.MESH
F32 = jnp.float32
BF16 = jnp.bfloat16

STEP = 1000
beta_one = 0.9
beta_two = 0.999
learn_rate = 0.001
decay_rate = 0.04
ema_rate = 0.994
epsilon = 1e-08

WIDTH = 2048
PROJ = WIDTH * WIDTH
SHARD = 66048
FLAT = SHARD // 128
TAIL = 260
GROUP = 144


def wrap(value, size):
    return lax.rem(value + size, size)


def device(x, y, z, c):
    return (y * 16 + lax.rem(z, 4) * 4 + x, lax.div(z, 4) * 2 + c)


def remote(src, dst, send, recv, to):
    return pltpu.make_async_remote_copy(
        src_ref=src, dst_ref=dst, send_sem=send, recv_sem=recv, device_id=to, device_id_type=MESH
    )


def roll_by(value, amount, axis, bits):
    for bit in bits:
        on = jnp.broadcast_to(lax.rem(lax.div(amount, 2**bit), 2) == 1, value.shape)
        value = jnp.where(on, pltpu.roll(value, 2 ** (bit - bits[0]), axis), value)
    return value


def iota(shape, axis):
    return lax.broadcasted_iota(jnp.int32, shape, axis)


def kernel(
    offsets, gain_hbm, tokens_hbm, cot_hbm, saved_hbm, master_hbm, one_hbm, two_hbm, teacher_hbm, tt_hbm,
    master_res, one_res, two_res, teacher_res, branch_res,
    gain, tok, cot, saved, master, one, two, teacher, mix, master_out, one_out, two_out, teacher_out,
    TW, T, C, SX, SL, SS, prod, zs, cr, zb, zr, PS, PR, both, xs, xr, pad, tg, TT, S, TP, TE, W, acc, OUT,
    in_sem, res_sem, own_sem, a1s, a1r, b1s, b1r, s1s, s1r, s2s, s2r, a2s, a2r, b2s, b2r, cs, crs, zss, zrs,
    ps, prs, xss, xrs, ts, tr, us, ur, w2s, w2r, w3s, w3r, hs, hr, fs, fr, os, orr,
):
    f = lax.axis_index("fsdp")
    p = lax.axis_index("dp")
    x = lax.rem(f, 4)
    zl = lax.rem(lax.div(f, 4), 4)
    y = lax.div(f, 16)
    c = lax.rem(p, 2)
    z = lax.div(p, 2) * 4 + zl

    def at(dx=0, dy=0, dz=0, dc=0):
        return device(wrap(x + dx, 4), wrap(y + dy, 4), wrap(z + dz, 8), wrap(c + dc, 2))

    partners = (
        [dict(dx=d) for d in (1, 2, 3)]
        + [dict(dy=d) for d in (1, 2, 3)]
        + [dict(dz=d) for d in range(1, 8)]
        + [dict(dx=d, dc=1) for d in range(4)]
    )
    h = lax.div(z, 4)
    loads = [
        pltpu.make_async_copy(src, dst, in_sem.at[k])
        for k, (src, dst) in enumerate(
            [
                (tokens_hbm, tok), (cot_hbm, cot), (saved_hbm, saved), (tt_hbm, TT.at[0, c]), (gain_hbm, gain),
                (master_hbm, master), (one_hbm, one), (two_hbm, two), (teacher_hbm, teacher),
            ]
        )
    ]
    for copy in loads:
        copy.start()
    barrier = pltpu.get_barrier_semaphore()
    for partner in partners:
        pl.semaphore_signal(barrier, inc=1, device_id=at(**partner), device_id_type=MESH)
    pl.semaphore_wait(barrier, len(partners))

    pending = []

    def send(copy):
        copy.start()
        pending.append(copy)

    def settle(copies):
        for copy in copies:
            copy.wait_send()

    def ring(view, to, sends, recvs):
        def spread(n):
            for k, (half, d) in enumerate([(0, 1), (1, 1), (1, -1), (0, -1)]):
                send(remote(view(n, 0, half), view(n, -d % 4, half), sends.at[n, k], recvs.at[n, k], to(d)))

        def wait(n, k):
            half, d = [(0, 3), (1, 3), (1, 1), (0, 1), (0, 2), (1, 2)][k]
            ref = view(n, d, half)
            remote(ref, ref, sends.at[n, k], recvs.at[n, k], to(1)).wait_recv()

        def relay(n):
            for k, half, d in ((0, 0, 1), (2, 1, -1)):
                wait(n, k)
                j = 4 + k // 2
                send(remote(view(n, -d % 4, half), view(n, 2, half), sends.at[n, j], recvs.at[n, j], to(d)))

        return spread, wait, relay

    halves = [pl.ds(0, 64), pl.ds(64, 64)]
    groups = [pl.ds(0, 1), pl.ds(1, 3)]
    along_x = lambda d: at(dx=d)
    along_y = lambda d: at(dy=d)
    spread_t, wait_t, relay_t = ring(lambda n, d, k: T.at[d, groups[n], halves[k]], along_x, a2s, a2r)
    spread_c, wait_c, relay_c = ring(lambda n, d, k: C.at[groups[n], d, halves[k]], along_y, b2s, b2r)
    spread_h, wait_h, relay_h = ring(lambda n, d, k: TT.at[d, c, halves[k]], along_x, ts, tr)

    def quarter(i):
        return cot_hbm.at[:, pl.ds(pl.multiple_of(512 * i, 128), 512)]

    mine = pltpu.make_async_copy(quarter(x), C.at[0, 0], own_sem.at[0])
    mine.start()
    for d in (1, 2, 3):
        send(remote(quarter(wrap(x + d, 4)), C.at[4 - d, 0], b1s.at[d - 1], b1r.at[d - 1], at(dx=d)))
    loads[0].wait()
    for i in range(4):
        end = min(512 * i + 640, WIDTH)
        window = tok[:, 512 * i : end].astype(F32)
        if i:
            window = pltpu.roll(window, end - 512 * i - 4 * i, 1)[:, :512]
        else:
            window = window[:, :512]
        if i == 3:
            window = jnp.where(iota((128, 512), 1) < 500, window, 0.0)
        TW[i] = window.astype(BF16)
    for d in (1, 2, 3):
        send(remote(TW.at[wrap(y + d, 4)], T.at[0, 4 - d], a1s.at[d - 1], a1r.at[d - 1], at(dy=d)))
    T[0, 0] = TW[y]
    spread_t(0)
    mine.wait()
    spread_c(0)
    loads[3].wait()
    send(remote(TT.at[0, c], TT.at[0, c], us.at[0], ur.at[0], at(dc=1)))
    loads[1].wait()
    loads[2].wait()
    total = jnp.zeros((1, WIDTH), F32)
    for r in range(0, 128, 16):
        total += jnp.sum(cot[r : r + 16].astype(F32) * saved[r : r + 16].astype(F32), axis=0, keepdims=True)
    top = total.astype(BF16).astype(F32)
    lane = iota((128, 128), 1)
    left = jnp.zeros((128, 128), F32)
    for i in range(3):
        tile = tok[:, 512 * (i + 1) : 512 * (i + 1) + 128].astype(F32)
        left = jnp.where(jnp.logical_and(lane >= 4 * i, lane < 4 * i + 4), tile, left)
    rows = iota((16, 512), 0)
    for i in range(4):
        side = slice(512 * i, 512 * i + 512)
        part = lax.dot_general(
            left.astype(BF16), cot[:, side], (((0,), (0,)), ((), ())), preferred_element_type=F32
        )[:16]
        part = jnp.where(rows == 12, top[:, side], jnp.where(rows == 13, total[:, side] - top[:, side], part))
        SS[i] = part.astype(BF16)
    for d in (1, 2, 3):
        send(remote(SS.at[wrap(x + d, 4)], SX.at[x], s1s.at[d - 1], s1r.at[d - 1], at(dx=d)))
    SX[x] = SS[x]

    for d in (1, 2, 3):
        ref = T.at[0, 4 - d]
        remote(ref, ref, a1s.at[d - 1], a1r.at[d - 1], at(dy=d)).wait_recv()
    spread_t(1)
    for d in (1, 2, 3):
        ref = C.at[4 - d, 0]
        remote(ref, ref, b1s.at[d - 1], b1r.at[d - 1], at(dx=d)).wait_recv()
    spread_c(1)
    relay_t(0)
    relay_c(0)

    for d in (1, 2, 3):
        ref = SX.at[wrap(x - d, 4)]
        remote(ref, ref, s1s.at[d - 1], s1r.at[d - 1], at(dx=d)).wait_recv()
    small = jnp.zeros((16, 512), F32)
    for i in range(4):
        small += SX[i].astype(F32)
    total = small[12:13] + small[13:14]
    top = total.astype(BF16).astype(F32)
    SL[y] = jnp.where(rows == 12, top, jnp.where(rows == 13, total - top, small)).astype(BF16)
    for d in (1, 2, 3):
        send(remote(SL.at[y], SL.at[y], s2s.at[d - 1], s2r.at[d - 1], at(dy=d)))

    for copy in loads[4:]:
        copy.wait()
    limit = PROJ - SHARD * f
    spots = 128 * iota((FLAT, 128), 0) + iota((FLAT, 128), 1)
    keep = jnp.where(spots < limit, 1.0 - learn_rate * decay_rate, 1.0)
    mix[...] = ema_rate * teacher[...] + (1.0 - ema_rate) * keep * master[...]
    place = jnp.full((1, 128), offsets[1] - PROJ, jnp.int32)
    row_back = lax.rem(32768 - lax.div(place, 128) * 128, 32768)
    lane_at = lax.rem(place, 128)
    lane_back = lax.rem(128 - lane_at, 128)
    lanes24 = iota((24, 128), 1)
    mine_of = lambda four: jnp.where(
        c == 0, jnp.where(h == 0, four[0], four[1]), jnp.where(h == 0, four[2], four[3])
    )
    for k, source in enumerate((mix, one, two)):
        for b in range(4):
            for m in range(4):
                four = [source[pl.ds(128 * b + 4 * m + t, 8, stride=16), :] for t in range(4)]
                PS[m, k, 8 * b : 8 * b + 8] = mine_of(four)
        tail = source[TAIL : TAIL + 256]
        moved = roll_by(tail, row_back, 0, range(7, 15))[0:24]
        rolled = roll_by(moved, lane_back, 1, range(7))
        bias = jnp.where(lanes24 < 128 - lane_at, rolled, pltpu.roll(rolled, 23, 0))
        for m in range(4):
            to = wrap(m - x, 4)
            PS[to, k, 32:33] = mine_of([source[512 + t : 513 + t] for t in range(4)])
            PS[to, k, 33:34] = mine_of([bias[4 * m + t : 4 * m + t + 1] for t in range(4)])
            PS[to, k, 34:35] = mine_of([tail[240 + 4 * m + t : 241 + 4 * m + t] for t in range(4)])
            PS[to, k, 35:40] = jnp.zeros((5, 128), F32)

    relay_t(1)
    relay_c(1)
    plane = list(pending)
    pending.clear()
    for d in (1, 2, 3):
        send(remote(PS.at[d], PR.at[4 - d], ps.at[d - 1], prs.at[d - 1], at(dx=d)))
    PR[0] = PS[0]
    spread_h(0)

    def one_hot(g, carry):
        col = iota((1, 384), 1)
        i = lax.div(lax.rem(col, 128), 32)
        source = 258 * g + lax.div(col, 128) * 129 + lax.rem(col, 128) + jnp.where(i > x, 1, 0)
        slot = lax.rem(col, 128) - 32 * lax.rem(g, 4)
        extra = 258 * g + 32 * x + 32 + jnp.where(slot == 0, 0, 129)
        extra = jnp.where(jnp.logical_or(slot == 0, slot == 16), extra, -1)
        source = jnp.where(col < 256, source, extra) - jnp.minimum(256 * g, WIDTH - 384)
        S[g] = jnp.where(iota((384, 384), 0) == source, 1.0, 0.0).astype(BF16)
        return carry

    lax.fori_loop(0, 8, one_hot, 0)

    def arrange(a):
        def group(g, extra):
            start = pl.multiple_of(jnp.minimum(256 * g, WIDTH - 384), 128)
            block = TT[a, :, :, pl.ds(start, 384)].reshape(256, 384)
            part = jnp.dot(block, S[g], preferred_element_type=F32)
            TP[g, a] = part[:, :256].astype(BF16)
            return extra + part[:, 256:]

        for h in range(2):
            extra = lax.fori_loop(4 * h, 4 * h + 4, group, jnp.zeros((256, 128), F32))
            TE[a, :, 128 * h : 128 * h + 128] = extra.astype(BF16)

    ones = jnp.ones((16, 512), BF16)
    cot_sum = jnp.zeros((16, 512), F32)
    for step, (i, arrivals) in enumerate(((0, ()), (3, (1,)), (1, (3,)), (2, (4, 5)))):
        if not step:
            for n in range(2):
                for k in (1, 3, 4, 5):
                    wait_t(n, k)
        for k in arrivals:
            for n in range(2):
                wait_c(n, k)
        right = C[:, i].reshape(512, 512)
        left = T[:, i].reshape(512, 512)
        part = lax.dot_general(left, right, (((0,), (0,)), ((), ())), preferred_element_type=F32)
        if step:
            prod[0:512] += part
        else:
            prod[0:512] = part
        cot_sum += jnp.dot(ones, right, preferred_element_type=F32)

    small = SL[y].astype(F32)
    for d in (1, 2, 3):
        ref = SL.at[wrap(y - d, 4)]
        remote(ref, ref, s2s.at[d - 1], s2r.at[d - 1], at(dy=d)).wait_recv()
        small += SL[wrap(y - d, 4)].astype(F32)
    rest = jnp.where(y == 0, small, jnp.where(y == 1, pltpu.roll(small, 12, 0), pltpu.roll(small, 8, 0)))
    prod[512:528] = jnp.where(rows < jnp.where(y < 3, 4, 0), rest, 0.0)
    keep_half = pl.ds(pl.multiple_of(256 * c, 128), 256)
    give_half = pl.ds(pl.multiple_of(256 * (1 - c), 128), 256)
    weight = gain[:, pl.ds(pl.multiple_of(512 * x, 128), 512)]
    for k in range(4):
        for i in range(4):
            start = 129 * k + 32 * i
            part = prod[start : start + 32]
            if i:
                part = jnp.where(x < i, prod[start + 1 : start + 33], part)
            zs[k, 32 * i : 32 * i + 32] = (part * weight).astype(BF16)
        extra = prod[129 * k + 32 : 129 * k + 33]
        for i in range(1, 4):
            extra = jnp.where(x == i, prod[129 * k + 32 * i + 32 : 129 * k + 32 * i + 33], extra)
        block = jnp.where(rows == 1, cot_sum * weight, jnp.where(rows == 2, small[12:13] + small[13:14], 0.0))
        zs[k, 128:144] = jnp.where(rows == 0, extra * weight, block).astype(BF16)
        send(remote(zs.at[k, :, give_half], cr.at[k], cs.at[k], crs.at[k], at(dc=1)))
    relay_h(0)

    for j in range(4):
        k = wrap(zl + j, 4)
        remote(zs.at[k, :, give_half], cr.at[k], cs.at[k], crs.at[k], at(dc=1)).wait_recv()
        chip = (zs[k, :, keep_half].astype(F32) + cr[k].astype(F32)).astype(BF16)
        zb[k] = chip[:, :128]
        zb[4 + k] = chip[:, 128:]
        for d in (j, j + 4):
            if d:
                to_z = wrap(z + d, 8)
                send(remote(zb.at[to_z], zr.at[z], zss.at[d - 1], zrs.at[d - 1], at(dz=d)))
    zr[z] = zb[z]

    def share(n, d, arrivals):
        for k in arrivals:
            wait_h(0, k)
        ref = TT.at[d, c]
        send(remote(ref, ref, us.at[n], ur.at[n], at(dc=1)))

    def shared(n, d):
        ref = TT.at[d, 1 - c]
        remote(ref, ref, us.at[n], ur.at[n], at(dc=1)).wait_recv()

    shared(0, 0)
    arrange(0)
    settle(plane)
    for d in (1, 2, 3):
        ref = PR.at[4 - d]
        remote(ref, ref, ps.at[d - 1], prs.at[d - 1], at(dx=d)).wait_recv()
    for d in range(1, 8):
        ref = zr.at[wrap(z - d, 8)]
        remote(ref, ref, zss.at[d - 1], zrs.at[d - 1], at(dz=d)).wait_recv()
    group = zr[0].astype(F32)
    for k in range(1, 8):
        group += zr[k].astype(F32)

    def low_teacher(grad, mixed, old_one, old_two):
        new_one = beta_one * old_one + (1.0 - beta_one) * grad
        new_two = beta_two * old_two + (1.0 - beta_two) * grad * grad
        first = new_one / (1.0 - beta_one**STEP)
        second = new_two / (1.0 - beta_two**STEP)
        return mixed - ((1.0 - ema_rate) * learn_rate) * (first / (jnp.sqrt(second) + epsilon))

    for i in range(4):
        span = slice(32 * i, 32 * i + 32)
        W[0, 0, span] = low_teacher(group[span], *[PR[wrap(i - x, 4), k, 0:32] for k in range(3)]).astype(BF16)
    first_row = iota((8, 128), 0) == 0
    extras = [jnp.where(first_row, PR[0, k, 32:40], PR[wrap(3 - x, 4), k, 32:40]) for k in range(3)]
    block = low_teacher(group[128:136], *extras)
    block = jnp.where(iota((8, 128), 0) < 3, block, 0.0)
    W[0, 0, 128:144] = jnp.concatenate([block, jnp.zeros((8, 128), F32)], axis=0).astype(BF16)

    before_columns = list(pending)
    pending.clear()
    parts = [pl.ds(0, 80), pl.ds(80, 64)]

    def column_view(n, d, k):
        if n == 0:
            return W.at[d, 0, parts[k]]
        return W.at[d, (1 if n == 1 else 6) + k]

    spread_w, wait_w, relay_w = ring(column_view, along_y, w3s, w3r)
    for d in (4, 1, 7, 2, 6, 3, 5):
        send(remote(W.at[0, 0], W.at[0, 8 - d], w2s.at[d - 1], w2r.at[d - 1], at(dz=d)))
    spread_w(0)

    both[h] = group[0:136]
    twin = remote(both.at[h], both.at[h], hs.at[0], hr.at[0], at(dz=4))
    send(twin)

    def come(d):
        ref = W.at[0, 8 - d]
        remote(ref, ref, w2s.at[d - 1], w2r.at[d - 1], at(dz=d)).wait_recv()

    share(1, 3, (1,))
    share(2, 1, (3,))
    come(7)
    come(6)
    spread_w(1)
    come(1)
    come(2)
    spread_w(2)
    relay_w(0)
    for d in (3, 5, 4):
        come(d)
    far = W.at[0, pl.ds(3, 3)]
    for d in (1, 2, 3):
        send(remote(far, W.at[4 - d, pl.ds(3, 3)], fs.at[d - 1], fr.at[d - 1], at(dy=d)))
    relay_w(1)
    relay_w(2)
    shared(1, 3)
    arrange(3)

    ref = both.at[1 - h]
    remote(ref, ref, hs.at[0], hr.at[0], at(dz=4)).wait_recv()
    for i in range(4):
        for k in range(2):
            side = slice(128 * k, 128 * k + 128)
            xs[i, 0:32, side] = both[k, 32 * i : 32 * i + 32]
            xs[i, 32:40, side] = both[k, 128:136]
    slot = 2 * x + c
    others = [(dx, dc) for dx in range(4) for dc in range(2) if dx or dc]
    for n, (dx, dc) in enumerate(others):
        send(remote(xs.at[wrap(x + dx, 4)], xr.at[slot], xss.at[n], xrs.at[n], at(dx=dx, dc=dc)))
    xr[slot] = xs[x]
    share(3, 2, (4, 5))
    shared(2, 1)
    arrange(1)

    def block_at(i, j, n):
        return W.at[i, wrap(4 * n + j - z, 8)]

    def accumulate(i, a):
        total = jnp.zeros((256, 256), F32)
        for k in range(2):
            sides = [
                jnp.concatenate([block_at(i, 2 * k + j, n)[0:128] for j in range(2)], axis=0) for n in range(2)
            ]
            right = jnp.concatenate(sides, axis=1)
            total += jnp.dot(TP[2 * wrap(y + i, 4) + k, a], right, preferred_element_type=F32)
        return total

    shared(3, 2)
    arrange(2)
    settle(before_columns)

    def add(i, fresh):
        def body(a, carry):
            if fresh:
                acc[a] = accumulate(i, a)
            else:
                acc[a] += accumulate(i, a)
            return carry

        lax.fori_loop(0, 4, body, 0)

    add(0, True)
    for i, arrivals in ((3, (1,)), (1, (3,)), (2, (4, 5))):
        for n in range(3):
            for k in arrivals:
                wait_w(n, k)
        ref = W.at[i, pl.ds(3, 3)]
        remote(ref, ref, fs.at[0], fr.at[3 - i], at(dy=1)).wait_recv()
        if i != 2:
            add(i, False)

    ends = jnp.concatenate(
        [
            jnp.concatenate(
                [block_at(wrap(i - y, 4), j, n)[128:144] for i in range(4) for j in range(4)], axis=0
            )
            for n in range(2)
        ],
        axis=1,
    )
    tail = ends[240:256].astype(F32)
    bias_t, scale_t = tail[1:2], tail[2:3]
    columns = list(pending)
    pending.clear()
    out_cols = branch_res.at[:, pl.ds(pl.multiple_of(256 * slot, 128), 256)]
    n = 0
    for d in (2, 1, 3, 0):
        a = d
        total = acc[a] + accumulate(2, a) + jnp.dot(TE[a], ends, preferred_element_type=F32)
        OUT[a] = (scale_t * (total + bias_t)).astype(BF16).reshape(2, 128, 256)
        for dc in range(2):
            core = wrap(c + dc, 2)
            if d or dc:
                send(remote(OUT.at[a, core], out_cols, os.at[n], orr.at[slot], at(dx=d, dc=dc)))
                n += 1
    stay = pltpu.make_async_copy(OUT.at[0, c], out_cols, own_sem.at[1])
    stay.start()
    settle(columns)

    for n, (dx, dc) in enumerate(others):
        ref = xr.at[2 * wrap(x - dx, 4) + wrap(c - dc, 2)]
        remote(ref, ref, xss.at[n], xrs.at[n], at(dx=dx, dc=dc)).wait_recv()
    last = jnp.where(f == 63, 1.0, 0.0).astype(F32)
    pad[...] = jnp.zeros_like(pad)
    tg[...] = jnp.zeros_like(tg)
    for e in range(8):
        for t in range(2):
            n = 2 * e + t
            pad[n : n + 1] = xr[e, 33:34, 128 * t : 128 * t + 128] * last
            tg[TAIL + 240 + n : TAIL + 241 + n] = xr[e, 34:35, 128 * t : 128 * t + 128] * last
    rolled = roll_by(pad[0:24], place, 1, range(7))
    pad[0:24] = jnp.where(lanes24 >= lane_at, rolled, pltpu.roll(rolled, 1, 0))
    tg[TAIL : TAIL + 256] += roll_by(pad[...], place, 0, range(7, 15))
    lanes = iota((8, 128), 1)
    subs = iota((8, 128), 0)

    def update(where, grad, inside):
        old = master[where]
        new_one = beta_one * one[where] + (1.0 - beta_one) * grad
        new_two = beta_two * two[where] + (1.0 - beta_two) * grad * grad
        first = new_one / (1.0 - beta_one**STEP)
        second = new_two / (1.0 - beta_two**STEP)
        decay = jnp.where(inside, decay_rate, 0.0) * old
        new = old - learn_rate * (first / (jnp.sqrt(second) + epsilon) + decay)
        master_out[where] = new
        one_out[where] = new_one
        two_out[where] = new_two
        teacher_out[where] = ema_rate * teacher[where] + (1.0 - ema_rate) * new

    for b in range(4):
        for m in range(4):
            for t in range(4):
                base = 128 * b + 4 * m + t
                where = (pl.ds(base, 8, stride=16), slice(None))
                e, side = 2 * wrap(x + m, 4) + t // 2, slice(128 * (t % 2), 128 * (t % 2) + 128)
                slots = 128 * base + 2048 * subs + lanes
                update(where, xr[e, 8 * b : 8 * b + 8, side] + tg[where], slots < limit)
    for t in range(4):
        where = (slice(512 + t, 513 + t), slice(None))
        e, side = 2 * x + t // 2, slice(128 * (t % 2), 128 * (t % 2) + 128)
        inside = jnp.full((1, 128), 65536, jnp.int32) < limit
        update(where, xr[e, 32:33, side] * (1.0 - last) + tg[where], inside)
    results = [
        pltpu.make_async_copy(src, dst, res_sem.at[k])
        for k, (src, dst) in enumerate(
            [(master_out, master_res), (one_out, one_res), (two_out, two_res), (teacher_out, teacher_res)]
        )
    ]
    for copy in results:
        copy.start()

    for n, (dx, dc) in enumerate(others):
        e = 2 * wrap(x - dx, 4) + wrap(c - dc, 2)
        ref = branch_res.at[:, pl.ds(pl.multiple_of(256 * e, 128), 256)]
        remote(ref, ref, os.at[n], orr.at[e], at(dc=1)).wait_recv()
    stay.wait()
    for copy in results:
        copy.wait()
    settle(pending)


def copy_kernel(*refs):
    sems = refs[15]
    loads = [pltpu.make_async_copy(refs[k], refs[10 + k], sems.at[k]) for k in range(5)]
    stores = [pltpu.make_async_copy(refs[10 + k], refs[5 + k], sems.at[5 + k]) for k in range(5)]
    for copy in loads:
        copy.start()
    for load, store in zip(loads, stores):
        load.wait()
        store.start()
    for copy in stores:
        copy.wait()


def per_device(
    tokens, cotangent, saved_branch, layer_gain, offsets, master, moment_one, moment_two, teacher, teacher_tokens
):
    anyspace = pl.BlockSpec(memory_space=pl.ANY)
    dma = pltpu.SemaphoreType.DMA
    flat = jax.ShapeDtypeStruct((FLAT, 128), F32)
    shard = pltpu.VMEM((FLAT, 128), F32)
    rows = pltpu.VMEM((128, WIDTH), BF16)
    results = [flat] * 4 + [jax.ShapeDtypeStruct((128, WIDTH), BF16)]
    outs = pl.pallas_call(
        kernel,
        out_shape=results,
        in_specs=[pl.BlockSpec(memory_space=pltpu.SMEM)] + [anyspace] * 9,
        out_specs=[anyspace] * 5,
        scratch_shapes=[
            pltpu.VMEM((1, WIDTH), F32),
            rows, rows, rows,
            shard, shard, shard, shard, shard, shard, shard, shard, shard,
            pltpu.VMEM((4, 128, 512), BF16),
            pltpu.VMEM((4, 4, 128, 512), BF16),
            pltpu.VMEM((4, 4, 128, 512), BF16),
            pltpu.VMEM((4, 16, 512), BF16),
            pltpu.VMEM((4, 16, 512), BF16),
            pltpu.VMEM((4, 16, 512), BF16),
            pltpu.VMEM((528, 512), F32),
            pltpu.VMEM((4, GROUP, 512), BF16),
            pltpu.VMEM((4, GROUP, 256), BF16),
            pltpu.VMEM((8, GROUP, 128), BF16),
            pltpu.VMEM((8, GROUP, 128), BF16),
            pltpu.VMEM((4, 3, 40, 128), F32),
            pltpu.VMEM((4, 3, 40, 128), F32),
            pltpu.VMEM((2, 136, 128), F32),
            pltpu.VMEM((4, 40, 256), F32),
            pltpu.VMEM((8, 40, 256), F32),
            pltpu.VMEM((256, 128), F32),
            pltpu.VMEM((520, 128), F32),
            pltpu.VMEM((4, 2, 128, WIDTH), BF16),
            pltpu.VMEM((8, 384, 384), BF16),
            pltpu.VMEM((8, 4, 256, 256), BF16),
            pltpu.VMEM((4, 256, 256), BF16),
            pltpu.VMEM((4, 8, GROUP, 128), BF16),
            pltpu.VMEM((4, 256, 256), F32),
            pltpu.VMEM((4, 2, 128, 256), BF16),
            dma((9,)), dma((4,)), dma((2,)),
            dma((3,)), dma((3,)), dma((3,)), dma((3,)), dma((3,)), dma((3,)), dma((3,)), dma((3,)),
            dma((2, 6)), dma((2, 6)), dma((2, 6)), dma((2, 6)),
            dma((4,)), dma((4,)), dma((7,)), dma((7,)),
            dma((3,)), dma((3,)), dma((7,)), dma((7,)),
            dma((1, 6)), dma((1, 6)), dma((4,)), dma((4,)), dma((7,)), dma((7,)), dma((3, 6)), dma((3, 6)),
            dma((1,)), dma((1,)), dma((3,)), dma((3,)),
            dma((7,)), dma((8,)),
        ],
        compiler_params=pltpu.CompilerParams(collective_id=0, has_side_effects=True, vmem_limit_bytes=56 << 20),
        name="step",
    )(
        offsets, layer_gain.reshape(1, WIDTH), tokens, cotangent, saved_branch,
        *[a.reshape(FLAT, 128) for a in (master, moment_one, moment_two, teacher)], teacher_tokens,
    )
    outs = pl.pallas_call(
        copy_kernel,
        out_shape=results,
        in_specs=[anyspace] * 5,
        out_specs=[anyspace] * 5,
        scratch_shapes=[shard, shard, shard, shard, rows, dma((10,))],
        name="place",
    )(*outs)
    return tuple(a.reshape(SHARD) for a in outs[:4]) + (outs[4],)


def solution(mesh):
    rows = P(("fsdp", "dp"), None)
    return jax.shard_map(
        per_device,
        mesh=mesh,
        in_specs=(rows, rows, rows, P(), P(), P("fsdp"), P("fsdp"), P("fsdp"), P("fsdp"), rows),
        out_specs=(P("fsdp"), P("fsdp"), P("fsdp"), P("fsdp"), rows),
        check_vma=False,
    )
```

```python
import jax
import jax.numpy as jnp
from jax import lax
from jax.experimental import pallas as pl
from jax.experimental.pallas import tpu as pltpu
from jax.sharding import PartitionSpec as P

MESH = pl.DeviceIdType.MESH
F32 = jnp.float32
BF16 = jnp.bfloat16

STEP = 1000
beta_one = 0.9
beta_two = 0.999
learn_rate = 0.001
decay_rate = 0.04
ema_rate = 0.994
epsilon = 1e-08

WIDTH = 2048
PROJ = WIDTH * WIDTH
SHARD = 66048
FLAT = SHARD // 128
TAIL = 260
GROUP = 144


def wrap(value, size):
    return lax.rem(value + size, size)


def device(x, y, z, c):
    return (y * 16 + lax.rem(z, 4) * 4 + x, lax.div(z, 4) * 2 + c)


def remote(src, dst, send, recv, to):
    return pltpu.make_async_remote_copy(
        src_ref=src, dst_ref=dst, send_sem=send, recv_sem=recv, device_id=to, device_id_type=MESH
    )


def roll_by(value, amount, axis, bits):
    for bit in bits:
        on = jnp.broadcast_to(lax.rem(lax.div(amount, 2**bit), 2) == 1, value.shape)
        value = jnp.where(on, pltpu.roll(value, 2 ** (bit - bits[0]), axis), value)
    return value


def iota(shape, axis):
    return lax.broadcasted_iota(jnp.int32, shape, axis)


def kernel(
    offsets, gain_hbm, tokens_hbm, cot_hbm, saved_hbm, master_hbm, one_hbm, two_hbm, teacher_hbm, tt_hbm,
    master_res, one_res, two_res, teacher_res, branch_res,
    gain, tok, cot, saved, raw, master, one, two, teacher, mix, master_out, one_out, two_out, teacher_out,
    TW, T, C, SX, SL, SS, prod, zs, cr, zb, zr, PS, PR, both, xs, xr, pad, tg, TT, W, acc, OUT,
    in_sem, res_sem, own_sem, a1s, a1r, b1s, b1r, s1s, s1r, s2s, s2r, a2s, a2r, b2s, b2r, cs, crs, zss, zrs,
    ps, prs, xss, xrs, ts, tr, us, ur, w2s, w2r, w3s, w3r, hs, hr, fs, fr, os, orr,
):
    f = lax.axis_index("fsdp")
    p = lax.axis_index("dp")
    x = lax.rem(f, 4)
    zl = lax.rem(lax.div(f, 4), 4)
    y = lax.div(f, 16)
    c = lax.rem(p, 2)
    z = lax.div(p, 2) * 4 + zl

    def at(dx=0, dy=0, dz=0, dc=0):
        return device(wrap(x + dx, 4), wrap(y + dy, 4), wrap(z + dz, 8), wrap(c + dc, 2))

    partners = (
        [dict(dx=d) for d in (1, 2, 3)]
        + [dict(dy=d) for d in (1, 2, 3)]
        + [dict(dz=d) for d in range(1, 8)]
        + [dict(dx=d, dc=1) for d in range(4)]
    )
    h = lax.div(z, 4)
    loads = [
        pltpu.make_async_copy(src, dst, in_sem.at[k])
        for k, (src, dst) in enumerate(
            [
                (tokens_hbm, tok), (cot_hbm, cot), (saved_hbm, saved), (tt_hbm, raw), (gain_hbm, gain),
                (master_hbm, master), (one_hbm, one), (two_hbm, two), (teacher_hbm, teacher),
            ]
        )
    ]
    for copy in loads:
        copy.start()
    barrier = pltpu.get_barrier_semaphore()
    for partner in partners:
        pl.semaphore_signal(barrier, inc=1, device_id=at(**partner), device_id_type=MESH)
    pl.semaphore_wait(barrier, len(partners))

    pending = []

    def send(copy):
        copy.start()
        pending.append(copy)

    def settle(copies):
        for copy in copies:
            copy.wait_send()

    def ring(view, to, sends, recvs):
        def spread(n):
            for k, (half, d) in enumerate([(0, 1), (1, 1), (1, -1), (0, -1)]):
                send(remote(view(n, 0, half), view(n, -d % 4, half), sends.at[n, k], recvs.at[n, k], to(d)))

        def wait(n, k):
            half, d = [(0, 3), (1, 3), (1, 1), (0, 1), (0, 2), (1, 2)][k]
            ref = view(n, d, half)
            remote(ref, ref, sends.at[n, k], recvs.at[n, k], to(1)).wait_recv()

        def relay(n):
            for k, half, d in ((0, 0, 1), (2, 1, -1)):
                wait(n, k)
                j = 4 + k // 2
                send(remote(view(n, -d % 4, half), view(n, 2, half), sends.at[n, j], recvs.at[n, j], to(d)))

        return spread, wait, relay

    halves = [pl.ds(0, 64), pl.ds(64, 64)]
    groups = [pl.ds(0, 1), pl.ds(1, 3)]
    along_x = lambda d: at(dx=d)
    along_y = lambda d: at(dy=d)
    spread_t, wait_t, relay_t = ring(lambda n, d, k: T.at[d, groups[n], halves[k]], along_x, a2s, a2r)
    spread_c, wait_c, relay_c = ring(lambda n, d, k: C.at[groups[n], d, halves[k]], along_y, b2s, b2r)
    spread_h, wait_h, relay_h = ring(lambda n, d, k: TT.at[d, c, halves[k]], along_x, ts, tr)

    def quarter(i):
        return cot_hbm.at[:, pl.ds(pl.multiple_of(512 * i, 128), 512)]

    mine = pltpu.make_async_copy(quarter(x), C.at[0, 0], own_sem.at[0])
    mine.start()
    for d in (1, 2, 3):
        send(remote(quarter(wrap(x + d, 4)), C.at[4 - d, 0], b1s.at[d - 1], b1r.at[d - 1], at(dx=d)))
    mine.wait()
    spread_c(0)
    loads[0].wait()
    for i in range(4):
        end = min(512 * i + 640, WIDTH)
        window = tok[:, 512 * i : end].astype(F32)
        if i:
            window = pltpu.roll(window, end - 512 * i - 4 * i, 1)[:, :512]
        else:
            window = window[:, :512]
        if i == 3:
            window = jnp.where(iota((128, 512), 1) < 500, window, 0.0)
        TW[i] = window.astype(BF16)
    for d in (1, 2, 3):
        send(remote(TW.at[wrap(y + d, 4)], T.at[0, 4 - d], a1s.at[d - 1], a1r.at[d - 1], at(dy=d)))
    T[0, 0] = TW[y]
    spread_t(0)
    loads[1].wait()
    loads[2].wait()
    total = jnp.zeros((1, WIDTH), F32)
    for r in range(0, 128, 16):
        total += jnp.sum(cot[r : r + 16].astype(F32) * saved[r : r + 16].astype(F32), axis=0, keepdims=True)
    top = total.astype(BF16).astype(F32)
    lane = iota((128, 128), 1)
    left = jnp.zeros((128, 128), F32)
    for i in range(3):
        tile = tok[:, 512 * (i + 1) : 512 * (i + 1) + 128].astype(F32)
        left = jnp.where(jnp.logical_and(lane >= 4 * i, lane < 4 * i + 4), tile, left)
    rows = iota((16, 512), 0)
    for i in range(4):
        side = slice(512 * i, 512 * i + 512)
        part = lax.dot_general(
            left.astype(BF16), cot[:, side], (((0,), (0,)), ((), ())), preferred_element_type=F32
        )[:16]
        part = jnp.where(rows == 12, top[:, side], jnp.where(rows == 13, total[:, side] - top[:, side], part))
        SS[i] = part.astype(BF16)
    for d in (1, 2, 3):
        send(remote(SS.at[wrap(x + d, 4)], SX.at[x], s1s.at[d - 1], s1r.at[d - 1], at(dx=d)))
    SX[x] = SS[x]

    for d in (1, 2, 3):
        ref = T.at[0, 4 - d]
        remote(ref, ref, a1s.at[d - 1], a1r.at[d - 1], at(dy=d)).wait_recv()
    spread_t(1)
    for d in (1, 2, 3):
        ref = C.at[4 - d, 0]
        remote(ref, ref, b1s.at[d - 1], b1r.at[d - 1], at(dx=d)).wait_recv()
    spread_c(1)
    relay_t(0)
    relay_c(0)

    for d in (1, 2, 3):
        ref = SX.at[wrap(x - d, 4)]
        remote(ref, ref, s1s.at[d - 1], s1r.at[d - 1], at(dx=d)).wait_recv()
    small = jnp.zeros((16, 512), F32)
    for i in range(4):
        small += SX[i].astype(F32)
    total = small[12:13] + small[13:14]
    top = total.astype(BF16).astype(F32)
    SL[y] = jnp.where(rows == 12, top, jnp.where(rows == 13, total - top, small)).astype(BF16)
    for d in (1, 2, 3):
        send(remote(SL.at[y], SL.at[y], s2s.at[d - 1], s2r.at[d - 1], at(dy=d)))

    for copy in loads[4:]:
        copy.wait()
    limit = PROJ - SHARD * f
    spots = 128 * iota((FLAT, 128), 0) + iota((FLAT, 128), 1)
    keep = jnp.where(spots < limit, 1.0 - learn_rate * decay_rate, 1.0)
    mix[...] = ema_rate * teacher[...] + (1.0 - ema_rate) * keep * master[...]
    place = jnp.full((1, 128), offsets[1] - PROJ, jnp.int32)
    row_back = lax.rem(32768 - lax.div(place, 128) * 128, 32768)
    lane_at = lax.rem(place, 128)
    lane_back = lax.rem(128 - lane_at, 128)
    lanes24 = iota((24, 128), 1)
    mine_of = lambda four: jnp.where(
        c == 0, jnp.where(h == 0, four[0], four[1]), jnp.where(h == 0, four[2], four[3])
    )
    for k, source in enumerate((mix, one, two)):
        for b in range(4):
            for m in range(4):
                four = [source[pl.ds(128 * b + 4 * m + t, 8, stride=16), :] for t in range(4)]
                PS[m, k, 8 * b : 8 * b + 8] = mine_of(four)
        tail = source[TAIL : TAIL + 256]
        moved = roll_by(tail, row_back, 0, range(7, 15))[0:24]
        rolled = roll_by(moved, lane_back, 1, range(7))
        bias = jnp.where(lanes24 < 128 - lane_at, rolled, pltpu.roll(rolled, 23, 0))
        for m in range(4):
            to = wrap(m - x, 4)
            PS[to, k, 32:33] = mine_of([source[512 + t : 513 + t] for t in range(4)])
            PS[to, k, 33:34] = mine_of([bias[4 * m + t : 4 * m + t + 1] for t in range(4)])
            PS[to, k, 34:35] = mine_of([tail[240 + 4 * m + t : 241 + 4 * m + t] for t in range(4)])
            PS[to, k, 35:40] = jnp.zeros((5, 128), F32)

    loads[3].wait()

    def arrange(g, extra):
        for k in range(2):
            j = 2 * g + k
            start = pl.multiple_of(jnp.minimum(128 * j, WIDTH - 256), 128)
            col = iota((1, 256), 1)
            lane = lax.rem(col, 128)
            source = jnp.where(col < 128, 129 * j + lane, jnp.where(lane == 16 * lax.rem(j, 8), 129 * j + 128, -1))
            pick = jnp.where(iota((256, 256), 0) == source - start, 1.0, 0.0).astype(BF16)
            part = jnp.dot(raw[:, pl.ds(start, 256)], pick, preferred_element_type=F32)
            TT[0, c, :, pl.ds(pl.multiple_of(128 * j, 128), 128)] = part[:, :128].astype(BF16)
            extra += part[:, 128:]
        return extra

    for half in range(2):
        extra = lax.fori_loop(4 * half, 4 * half + 4, arrange, jnp.zeros((128, 128), F32))
        TT[0, c, :, WIDTH + 128 * half : WIDTH + 128 * half + 128] = extra.astype(BF16)
    send(remote(TT.at[0, c], TT.at[0, c], us.at[0], ur.at[0], at(dc=1)))

    relay_t(1)
    relay_c(1)
    plane = list(pending)
    pending.clear()
    for d in (1, 2, 3):
        send(remote(PS.at[d], PR.at[4 - d], ps.at[d - 1], prs.at[d - 1], at(dx=d)))
    PR[0] = PS[0]
    spread_h(0)

    def share(n, d, arrivals):
        for k in arrivals:
            wait_h(0, k)
        ref = TT.at[d, c]
        send(remote(ref, ref, us.at[n], ur.at[n], at(dc=1)))

    def shared(n, d):
        ref = TT.at[d, 1 - c]
        remote(ref, ref, us.at[n], ur.at[n], at(dc=1)).wait_recv()

    ones = jnp.ones((16, 512), BF16)
    cot_sum = jnp.zeros((16, 512), F32)
    for step, (i, arrivals) in enumerate(((0, ()), (3, (1,)), (1, (3,)), (2, (4, 5)))):
        if not step:
            for n in range(2):
                for k in (1, 3, 4, 5):
                    wait_t(n, k)
        for k in arrivals:
            for n in range(2):
                wait_c(n, k)
        right = C[:, i].reshape(512, 512)
        left = T[:, i].reshape(512, 512)
        part = lax.dot_general(left, right, (((0,), (0,)), ((), ())), preferred_element_type=F32)
        if step:
            prod[0:512] += part
        else:
            prod[0:512] = part
        cot_sum += jnp.dot(ones, right, preferred_element_type=F32)

    small = SL[y].astype(F32)
    for d in (1, 2, 3):
        ref = SL.at[wrap(y - d, 4)]
        remote(ref, ref, s2s.at[d - 1], s2r.at[d - 1], at(dy=d)).wait_recv()
        small += SL[wrap(y - d, 4)].astype(F32)
    rest = jnp.where(y == 0, small, jnp.where(y == 1, pltpu.roll(small, 12, 0), pltpu.roll(small, 8, 0)))
    prod[512:528] = jnp.where(rows < jnp.where(y < 3, 4, 0), rest, 0.0)
    keep_half = pl.ds(pl.multiple_of(256 * c, 128), 256)
    give_half = pl.ds(pl.multiple_of(256 * (1 - c), 128), 256)
    weight = gain[:, pl.ds(pl.multiple_of(512 * x, 128), 512)]
    for k in range(4):
        for i in range(4):
            start = 129 * k + 32 * i
            part = prod[start : start + 32]
            if i:
                part = jnp.where(x < i, prod[start + 1 : start + 33], part)
            zs[k, 32 * i : 32 * i + 32] = (part * weight).astype(BF16)
        extra = prod[129 * k + 32 : 129 * k + 33]
        for i in range(1, 4):
            extra = jnp.where(x == i, prod[129 * k + 32 * i + 32 : 129 * k + 32 * i + 33], extra)
        block = jnp.where(rows == 1, cot_sum * weight, jnp.where(rows == 2, small[12:13] + small[13:14], 0.0))
        zs[k, 128:144] = jnp.where(rows == 0, extra * weight, block).astype(BF16)
        send(remote(zs.at[k, :, give_half], cr.at[k], cs.at[k], crs.at[k], at(dc=1)))
    relay_h(0)

    for j in range(4):
        k = wrap(zl + j, 4)
        remote(zs.at[k, :, give_half], cr.at[k], cs.at[k], crs.at[k], at(dc=1)).wait_recv()
        chip = (zs[k, :, keep_half].astype(F32) + cr[k].astype(F32)).astype(BF16)
        zb[k] = chip[:, :128]
        zb[4 + k] = chip[:, 128:]
        for d in (j, j + 4):
            if d:
                to_z = wrap(z + d, 8)
                send(remote(zb.at[to_z], zr.at[z], zss.at[d - 1], zrs.at[d - 1], at(dz=d)))
    zr[z] = zb[z]

    settle(plane)
    for d in (1, 2, 3):
        ref = PR.at[4 - d]
        remote(ref, ref, ps.at[d - 1], prs.at[d - 1], at(dx=d)).wait_recv()
    for d in range(1, 8):
        ref = zr.at[wrap(z - d, 8)]
        remote(ref, ref, zss.at[d - 1], zrs.at[d - 1], at(dz=d)).wait_recv()
    group = zr[0].astype(F32)
    for k in range(1, 8):
        group += zr[k].astype(F32)

    def low_teacher(grad, mixed, old_one, old_two):
        new_one = beta_one * old_one + (1.0 - beta_one) * grad
        new_two = beta_two * old_two + (1.0 - beta_two) * grad * grad
        first = new_one / (1.0 - beta_one**STEP)
        second = new_two / (1.0 - beta_two**STEP)
        return mixed - ((1.0 - ema_rate) * learn_rate) * (first / (jnp.sqrt(second) + epsilon))

    main = [low_teacher(group[32 * i : 32 * i + 32], *[PR[wrap(i - x, 4), k, 0:32] for k in range(3)]) for i in range(4)]
    first_row = iota((8, 128), 0) == 0
    extras = [jnp.where(first_row, PR[0, k, 32:40], PR[wrap(3 - x, 4), k, 32:40]) for k in range(3)]
    block = low_teacher(group[128:136], *extras)
    nothing = jnp.zeros((8, 128), F32)
    plain = jnp.concatenate(main + [nothing, nothing], axis=0)
    moved = pltpu.roll(plain, 1, 0)
    at_row = iota((GROUP, 128), 0)
    place_row = 32 * x + 32
    plain = jnp.where(at_row < place_row, plain, jnp.where(at_row == place_row, block[0:1], moved))
    plain = jnp.where(at_row == 129, block[1:2], jnp.where(at_row == 130, block[2:3], plain))
    W[0, 0] = plain.astype(BF16)

    before_columns = list(pending)
    pending.clear()
    parts = [pl.ds(0, 80), pl.ds(80, 64)]

    def column_view(n, d, k):
        if n == 0:
            return W.at[d, 0, parts[k]]
        return W.at[d, (1 if n == 1 else 6) + k]

    spread_w, wait_w, relay_w = ring(column_view, along_y, w3s, w3r)
    for d in (4, 1, 7, 2, 6, 3, 5):
        send(remote(W.at[0, 0], W.at[0, 8 - d], w2s.at[d - 1], w2r.at[d - 1], at(dz=d)))
    spread_w(0)

    both[h] = group[0:136]
    twin = remote(both.at[h], both.at[h], hs.at[0], hr.at[0], at(dz=4))
    send(twin)

    def come(d):
        ref = W.at[0, 8 - d]
        remote(ref, ref, w2s.at[d - 1], w2r.at[d - 1], at(dz=d)).wait_recv()

    come(7)
    come(6)
    spread_w(1)
    come(1)
    come(2)
    spread_w(2)
    relay_w(0)
    share(1, 3, (1,))
    share(2, 1, (3,))
    for d in (3, 5, 4):
        come(d)
    far = W.at[0, pl.ds(3, 3)]
    for d in (1, 2, 3):
        send(remote(far, W.at[4 - d, pl.ds(3, 3)], fs.at[d - 1], fr.at[d - 1], at(dy=d)))
    relay_w(1)
    relay_w(2)

    ref = both.at[1 - h]
    remote(ref, ref, hs.at[0], hr.at[0], at(dz=4)).wait_recv()
    for i in range(4):
        for k in range(2):
            side = slice(128 * k, 128 * k + 128)
            xs[i, 0:32, side] = both[k, 32 * i : 32 * i + 32]
            xs[i, 32:40, side] = both[k, 128:136]
    slot = 2 * x + c
    others = [(dx, dc) for dx in range(4) for dc in range(2) if dx or dc]
    for n, (dx, dc) in enumerate(others):
        send(remote(xs.at[wrap(x + dx, 4)], xr.at[slot], xss.at[n], xrs.at[n], at(dx=dx, dc=dc)))
    xr[slot] = xs[x]
    share(3, 2, (4, 5))

    def block_at(i, j, n):
        return W.at[i, wrap(4 * n + j - z, 8)]

    def accumulate(i, a):
        total = jnp.zeros((256, 256), F32)
        for k in range(2):
            sides = [
                jnp.concatenate([block_at(i, 2 * k + j, n)[0:128] for j in range(2)], axis=0) for n in range(2)
            ]
            right = jnp.concatenate(sides, axis=1)
            start = pl.multiple_of(512 * wrap(y + i, 4) + 256 * k, 128)
            left = TT[a, :, :, pl.ds(start, 256)].reshape(256, 256)
            total += jnp.dot(left, right, preferred_element_type=F32)
        return total

    shared(0, 0)
    shared(1, 3)
    shared(2, 1)
    shared(3, 2)
    settle(before_columns)

    def add(i, fresh):
        def body(a, carry):
            if fresh:
                acc[a] = accumulate(i, a)
            else:
                acc[a] += accumulate(i, a)
            return carry

        lax.fori_loop(0, 4, body, 0)

    add(0, True)
    for i, arrivals in ((3, (1,)), (1, (3,)), (2, (4, 5))):
        for n in range(3):
            for k in arrivals:
                wait_w(n, k)
        ref = W.at[i, pl.ds(3, 3)]
        remote(ref, ref, fs.at[0], fr.at[3 - i], at(dy=1)).wait_recv()
        if i != 2:
            add(i, False)

    ends = jnp.concatenate(
        [
            jnp.concatenate(
                [block_at(wrap(i - y, 4), j, n)[128:144] for i in range(4) for j in range(4)], axis=0
            )
            for n in range(2)
        ],
        axis=1,
    )
    tail = ends[240:256].astype(F32)
    bias_t, scale_t = tail[1:2], tail[2:3]
    columns = list(pending)
    pending.clear()
    out_cols = branch_res.at[:, pl.ds(pl.multiple_of(256 * slot, 128), 256)]
    n = 0
    for d in (2, 1, 3, 0):
        a = d
        total = acc[a] + accumulate(2, a) + jnp.dot(
            TT[a, :, :, WIDTH:].reshape(256, 256), ends, preferred_element_type=F32
        )
        OUT[a] = (scale_t * (total + bias_t)).astype(BF16).reshape(2, 128, 256)
        for dc in range(2):
            core = wrap(c + dc, 2)
            if d or dc:
                send(remote(OUT.at[a, core], out_cols, os.at[n], orr.at[slot], at(dx=d, dc=dc)))
                n += 1
    stay = pltpu.make_async_copy(OUT.at[0, c], out_cols, own_sem.at[1])
    stay.start()
    settle(columns)

    for n, (dx, dc) in enumerate(others):
        ref = xr.at[2 * wrap(x - dx, 4) + wrap(c - dc, 2)]
        remote(ref, ref, xss.at[n], xrs.at[n], at(dx=dx, dc=dc)).wait_recv()
    last = jnp.where(f == 63, 1.0, 0.0).astype(F32)
    pad[...] = jnp.zeros_like(pad)
    tg[...] = jnp.zeros_like(tg)
    for e in range(8):
        for t in range(2):
            n = 2 * e + t
            pad[n : n + 1] = xr[e, 33:34, 128 * t : 128 * t + 128] * last
            tg[TAIL + 240 + n : TAIL + 241 + n] = xr[e, 34:35, 128 * t : 128 * t + 128] * last
    rolled = roll_by(pad[0:24], place, 1, range(7))
    pad[0:24] = jnp.where(lanes24 >= lane_at, rolled, pltpu.roll(rolled, 1, 0))
    tg[TAIL : TAIL + 256] += roll_by(pad[...], place, 0, range(7, 15))
    lanes = iota((8, 128), 1)
    subs = iota((8, 128), 0)

    def update(where, grad, inside):
        old = master[where]
        new_one = beta_one * one[where] + (1.0 - beta_one) * grad
        new_two = beta_two * two[where] + (1.0 - beta_two) * grad * grad
        first = new_one / (1.0 - beta_one**STEP)
        second = new_two / (1.0 - beta_two**STEP)
        decay = jnp.where(inside, decay_rate, 0.0) * old
        new = old - learn_rate * (first / (jnp.sqrt(second) + epsilon) + decay)
        master_out[where] = new
        one_out[where] = new_one
        two_out[where] = new_two
        teacher_out[where] = ema_rate * teacher[where] + (1.0 - ema_rate) * new

    for b in range(4):
        for m in range(4):
            for t in range(4):
                base = 128 * b + 4 * m + t
                where = (pl.ds(base, 8, stride=16), slice(None))
                e, side = 2 * wrap(x + m, 4) + t // 2, slice(128 * (t % 2), 128 * (t % 2) + 128)
                slots = 128 * base + 2048 * subs + lanes
                update(where, xr[e, 8 * b : 8 * b + 8, side] + tg[where], slots < limit)
    for t in range(4):
        where = (slice(512 + t, 513 + t), slice(None))
        e, side = 2 * x + t // 2, slice(128 * (t % 2), 128 * (t % 2) + 128)
        inside = jnp.full((1, 128), 65536, jnp.int32) < limit
        update(where, xr[e, 32:33, side] * (1.0 - last) + tg[where], inside)
    results = [
        pltpu.make_async_copy(src, dst, res_sem.at[k])
        for k, (src, dst) in enumerate(
            [(master_out, master_res), (one_out, one_res), (two_out, two_res), (teacher_out, teacher_res)]
        )
    ]
    for copy in results:
        copy.start()

    for n, (dx, dc) in enumerate(others):
        e = 2 * wrap(x - dx, 4) + wrap(c - dc, 2)
        ref = branch_res.at[:, pl.ds(pl.multiple_of(256 * e, 128), 256)]
        remote(ref, ref, os.at[n], orr.at[e], at(dc=1)).wait_recv()
    stay.wait()
    for copy in results:
        copy.wait()
    settle(pending)


def copy_kernel(*refs):
    sems = refs[15]
    loads = [pltpu.make_async_copy(refs[k], refs[10 + k], sems.at[k]) for k in range(5)]
    stores = [pltpu.make_async_copy(refs[10 + k], refs[5 + k], sems.at[5 + k]) for k in range(5)]
    for copy in loads:
        copy.start()
    for load, store in zip(loads, stores):
        load.wait()
        store.start()
    for copy in stores:
        copy.wait()


def per_device(
    tokens, cotangent, saved_branch, layer_gain, offsets, master, moment_one, moment_two, teacher, teacher_tokens
):
    anyspace = pl.BlockSpec(memory_space=pl.ANY)
    dma = pltpu.SemaphoreType.DMA
    flat = jax.ShapeDtypeStruct((FLAT, 128), F32)
    shard = pltpu.VMEM((FLAT, 128), F32)
    rows = pltpu.VMEM((128, WIDTH), BF16)
    results = [flat] * 4 + [jax.ShapeDtypeStruct((128, WIDTH), BF16)]
    outs = pl.pallas_call(
        kernel,
        out_shape=results,
        in_specs=[pl.BlockSpec(memory_space=pltpu.SMEM)] + [anyspace] * 9,
        out_specs=[anyspace] * 5,
        scratch_shapes=[
            pltpu.VMEM((1, WIDTH), F32),
            rows, rows, rows, rows,
            shard, shard, shard, shard, shard, shard, shard, shard, shard,
            pltpu.VMEM((4, 128, 512), BF16),
            pltpu.VMEM((4, 4, 128, 512), BF16),
            pltpu.VMEM((4, 4, 128, 512), BF16),
            pltpu.VMEM((4, 16, 512), BF16),
            pltpu.VMEM((4, 16, 512), BF16),
            pltpu.VMEM((4, 16, 512), BF16),
            pltpu.VMEM((528, 512), F32),
            pltpu.VMEM((4, GROUP, 512), BF16),
            pltpu.VMEM((4, GROUP, 256), BF16),
            pltpu.VMEM((8, GROUP, 128), BF16),
            pltpu.VMEM((8, GROUP, 128), BF16),
            pltpu.VMEM((4, 3, 40, 128), F32),
            pltpu.VMEM((4, 3, 40, 128), F32),
            pltpu.VMEM((2, 136, 128), F32),
            pltpu.VMEM((4, 40, 256), F32),
            pltpu.VMEM((8, 40, 256), F32),
            pltpu.VMEM((256, 128), F32),
            pltpu.VMEM((520, 128), F32),
            pltpu.VMEM((4, 2, 128, WIDTH + 256), BF16),
            pltpu.VMEM((4, 8, GROUP, 128), BF16),
            pltpu.VMEM((4, 256, 256), F32),
            pltpu.VMEM((4, 2, 128, 256), BF16),
            dma((9,)), dma((4,)), dma((2,)),
            dma((3,)), dma((3,)), dma((3,)), dma((3,)), dma((3,)), dma((3,)), dma((3,)), dma((3,)),
            dma((2, 6)), dma((2, 6)), dma((2, 6)), dma((2, 6)),
            dma((4,)), dma((4,)), dma((7,)), dma((7,)),
            dma((3,)), dma((3,)), dma((7,)), dma((7,)),
            dma((1, 6)), dma((1, 6)), dma((4,)), dma((4,)), dma((7,)), dma((7,)), dma((3, 6)), dma((3, 6)),
            dma((1,)), dma((1,)), dma((3,)), dma((3,)),
            dma((7,)), dma((8,)),
        ],
        compiler_params=pltpu.CompilerParams(collective_id=0, has_side_effects=True, vmem_limit_bytes=56 << 20),
        name="step",
    )(
        offsets, layer_gain.reshape(1, WIDTH), tokens, cotangent, saved_branch,
        *[a.reshape(FLAT, 128) for a in (master, moment_one, moment_two, teacher)], teacher_tokens,
    )
    outs = pl.pallas_call(
        copy_kernel,
        out_shape=results,
        in_specs=[anyspace] * 5,
        out_specs=[anyspace] * 5,
        scratch_shapes=[shard, shard, shard, shard, rows, dma((10,))],
        name="place",
    )(*outs)
    return tuple(a.reshape(SHARD) for a in outs[:4]) + (outs[4],)


def solution(mesh):
    rows = P(("fsdp", "dp"), None)
    return jax.shard_map(
        per_device,
        mesh=mesh,
        in_specs=(rows, rows, rows, P(), P(), P("fsdp"), P("fsdp"), P("fsdp"), P("fsdp"), rows),
        out_specs=(P("fsdp"), P("fsdp"), P("fsdp"), P("fsdp"), rows),
        check_vma=False,
    )
```

```python
import jax
import jax.numpy as jnp
from jax import lax
from jax.experimental import pallas as pl
from jax.experimental.pallas import tpu as pltpu
from jax.sharding import PartitionSpec as P

MESH = pl.DeviceIdType.MESH
F32 = jnp.float32
BF16 = jnp.bfloat16

STEP = 1000
beta_one = 0.9
beta_two = 0.999
learn_rate = 0.001
decay_rate = 0.04
ema_rate = 0.994
epsilon = 1e-08

WIDTH = 2048
PROJ = WIDTH * WIDTH
SHARD = 66048
FLAT = SHARD // 128
TAIL = 260
GROUP = 144


def wrap(value, size):
    return lax.rem(value + size, size)


def device(x, y, z, c):
    return (y * 16 + lax.rem(z, 4) * 4 + x, lax.div(z, 4) * 2 + c)


def remote(src, dst, send, recv, to):
    return pltpu.make_async_remote_copy(
        src_ref=src, dst_ref=dst, send_sem=send, recv_sem=recv, device_id=to, device_id_type=MESH
    )


def roll_by(value, amount, axis, bits):
    for bit in bits:
        on = jnp.broadcast_to(lax.rem(lax.div(amount, 2**bit), 2) == 1, value.shape)
        value = jnp.where(on, pltpu.roll(value, 2 ** (bit - bits[0]), axis), value)
    return value


def iota(shape, axis):
    return lax.broadcasted_iota(jnp.int32, shape, axis)


def kernel(
    offsets, gain_hbm, tokens_hbm, cot_hbm, saved_hbm, master_hbm, one_hbm, two_hbm, teacher_hbm, tt_hbm,
    master_res, one_res, two_res, teacher_res, branch_res,
    gain, tok, cot, saved, raw, master, one, two, teacher, mix, master_out, one_out, two_out, teacher_out,
    TW, T, C, SX, SL, SS, prod, zs, cr, zb, zr, PS, PR, both, xs, xr, pad, tg, TT, W, acc, OUT,
    in_sem, res_sem, own_sem, a1s, a1r, b1s, b1r, s1s, s1r, s2s, s2r, a2s, a2r, b2s, b2r, cs, crs, zss, zrs,
    ps, prs, xss, xrs, ts, tr, us, ur, w2s, w2r, w3s, w3r, hs, hr, fs, fr, os, orr,
):
    f = lax.axis_index("fsdp")
    p = lax.axis_index("dp")
    x = lax.rem(f, 4)
    zl = lax.rem(lax.div(f, 4), 4)
    y = lax.div(f, 16)
    c = lax.rem(p, 2)
    z = lax.div(p, 2) * 4 + zl

    def at(dx=0, dy=0, dz=0, dc=0):
        return device(wrap(x + dx, 4), wrap(y + dy, 4), wrap(z + dz, 8), wrap(c + dc, 2))

    partners = (
        [dict(dx=d) for d in (1, 2, 3)]
        + [dict(dy=d) for d in (1, 2, 3)]
        + [dict(dz=d) for d in range(1, 8)]
        + [dict(dx=d, dc=1) for d in range(4)]
    )
    h = lax.div(z, 4)
    loads = [
        pltpu.make_async_copy(src, dst, in_sem.at[k])
        for k, (src, dst) in enumerate(
            [
                (tokens_hbm, tok), (cot_hbm, cot), (saved_hbm, saved), (tt_hbm, raw), (gain_hbm, gain),
                (master_hbm, master), (one_hbm, one), (two_hbm, two), (teacher_hbm, teacher),
            ]
        )
    ]
    for copy in loads:
        copy.start()
    barrier = pltpu.get_barrier_semaphore()
    for partner in partners:
        pl.semaphore_signal(barrier, inc=1, device_id=at(**partner), device_id_type=MESH)
    pl.semaphore_wait(barrier, len(partners))

    pending = []

    def send(copy):
        copy.start()
        pending.append(copy)

    def settle(copies):
        for copy in copies:
            copy.wait_send()

    def ring(view, to, sends, recvs):
        def spread(n):
            for k, (half, d) in enumerate([(0, 1), (1, 1), (1, -1), (0, -1)]):
                send(remote(view(n, 0, half), view(n, -d % 4, half), sends.at[n, k], recvs.at[n, k], to(d)))

        def wait(n, k):
            half, d = [(0, 3), (1, 3), (1, 1), (0, 1), (0, 2), (1, 2)][k]
            ref = view(n, d, half)
            remote(ref, ref, sends.at[n, k], recvs.at[n, k], to(1)).wait_recv()

        def relay(n):
            for k, half, d in ((0, 0, 1), (2, 1, -1)):
                wait(n, k)
                j = 4 + k // 2
                send(remote(view(n, -d % 4, half), view(n, 2, half), sends.at[n, j], recvs.at[n, j], to(d)))

        return spread, wait, relay

    halves = [pl.ds(0, 64), pl.ds(64, 64)]
    groups = [pl.ds(0, 1), pl.ds(1, 3)]
    along_x = lambda d: at(dx=d)
    along_y = lambda d: at(dy=d)
    spread_t, wait_t, relay_t = ring(lambda n, d, k: T.at[d, groups[n], halves[k]], along_x, a2s, a2r)
    spread_c, wait_c, relay_c = ring(lambda n, d, k: C.at[groups[n], d, halves[k]], along_y, b2s, b2r)
    spread_h, wait_h, relay_h = ring(lambda n, d, k: TT.at[d, c, halves[k]], along_x, ts, tr)

    def quarter(i):
        return cot_hbm.at[:, pl.ds(pl.multiple_of(512 * i, 128), 512)]

    mine = pltpu.make_async_copy(quarter(x), C.at[0, 0], own_sem.at[0])
    mine.start()
    for d in (1, 2, 3):
        send(remote(quarter(wrap(x + d, 4)), C.at[4 - d, 0], b1s.at[d - 1], b1r.at[d - 1], at(dx=d)))
    mine.wait()
    spread_c(0)
    loads[0].wait()
    for i in range(4):
        end = min(512 * i + 640, WIDTH)
        window = tok[:, 512 * i : end].astype(F32)
        if i:
            window = pltpu.roll(window, end - 512 * i - 4 * i, 1)[:, :512]
        else:
            window = window[:, :512]
        if i == 3:
            window = jnp.where(iota((128, 512), 1) < 500, window, 0.0)
        TW[i] = window.astype(BF16)
    for d in (1, 2, 3):
        send(remote(TW.at[wrap(y + d, 4)], T.at[0, 4 - d], a1s.at[d - 1], a1r.at[d - 1], at(dy=d)))
    T[0, 0] = TW[y]
    spread_t(0)
    loads[1].wait()
    loads[2].wait()
    total = jnp.zeros((1, WIDTH), F32)
    for r in range(0, 128, 16):
        total += jnp.sum(cot[r : r + 16].astype(F32) * saved[r : r + 16].astype(F32), axis=0, keepdims=True)
    top = total.astype(BF16).astype(F32)
    lane = iota((128, 128), 1)
    left = jnp.zeros((128, 128), F32)
    for i in range(3):
        tile = tok[:, 512 * (i + 1) : 512 * (i + 1) + 128].astype(F32)
        left = jnp.where(jnp.logical_and(lane >= 4 * i, lane < 4 * i + 4), tile, left)
    rows = iota((16, 512), 0)
    for i in range(4):
        side = slice(512 * i, 512 * i + 512)
        part = lax.dot_general(
            left.astype(BF16), cot[:, side], (((0,), (0,)), ((), ())), preferred_element_type=F32
        )[:16]
        part = jnp.where(rows == 12, top[:, side], jnp.where(rows == 13, total[:, side] - top[:, side], part))
        SS[i] = part.astype(BF16)
    for d in (1, 2, 3):
        send(remote(SS.at[wrap(x + d, 4)], SX.at[x], s1s.at[d - 1], s1r.at[d - 1], at(dx=d)))
    SX[x] = SS[x]

    for d in (1, 2, 3):
        ref = T.at[0, 4 - d]
        remote(ref, ref, a1s.at[d - 1], a1r.at[d - 1], at(dy=d)).wait_recv()
    spread_t(1)
    for d in (1, 2, 3):
        ref = C.at[4 - d, 0]
        remote(ref, ref, b1s.at[d - 1], b1r.at[d - 1], at(dx=d)).wait_recv()
    spread_c(1)
    relay_t(0)
    relay_c(0)

    for d in (1, 2, 3):
        ref = SX.at[wrap(x - d, 4)]
        remote(ref, ref, s1s.at[d - 1], s1r.at[d - 1], at(dx=d)).wait_recv()
    small = jnp.zeros((16, 512), F32)
    for i in range(4):
        small += SX[i].astype(F32)
    total = small[12:13] + small[13:14]
    top = total.astype(BF16).astype(F32)
    SL[y] = jnp.where(rows == 12, top, jnp.where(rows == 13, total - top, small)).astype(BF16)
    for d in (1, 2, 3):
        send(remote(SL.at[y], SL.at[y], s2s.at[d - 1], s2r.at[d - 1], at(dy=d)))

    for copy in loads[4:]:
        copy.wait()
    limit = PROJ - SHARD * f
    spots = 128 * iota((FLAT, 128), 0) + iota((FLAT, 128), 1)
    keep = jnp.where(spots < limit, 1.0 - learn_rate * decay_rate, 1.0)
    mix[...] = ema_rate * teacher[...] + (1.0 - ema_rate) * keep * master[...]
    place = jnp.full((1, 128), offsets[1] - PROJ, jnp.int32)
    row_back = lax.rem(32768 - lax.div(place, 128) * 128, 32768)
    lane_at = lax.rem(place, 128)
    lane_back = lax.rem(128 - lane_at, 128)
    lanes24 = iota((24, 128), 1)
    mine_of = lambda four: jnp.where(
        c == 0, jnp.where(h == 0, four[0], four[1]), jnp.where(h == 0, four[2], four[3])
    )
    for k, source in enumerate((mix, one, two)):
        for b in range(4):
            for m in range(4):
                four = [source[pl.ds(128 * b + 4 * m + t, 8, stride=16), :] for t in range(4)]
                PS[m, k, 8 * b : 8 * b + 8] = mine_of(four)
        tail = source[TAIL : TAIL + 256]
        moved = roll_by(tail, row_back, 0, range(7, 15))[0:24]
        rolled = roll_by(moved, lane_back, 1, range(7))
        bias = jnp.where(lanes24 < 128 - lane_at, rolled, pltpu.roll(rolled, 23, 0))
        for m in range(4):
            to = wrap(m - x, 4)
            PS[to, k, 32:33] = mine_of([source[512 + t : 513 + t] for t in range(4)])
            PS[to, k, 33:34] = mine_of([bias[4 * m + t : 4 * m + t + 1] for t in range(4)])
            PS[to, k, 34:35] = mine_of([tail[240 + 4 * m + t : 241 + 4 * m + t] for t in range(4)])
            PS[to, k, 35:40] = jnp.zeros((5, 128), F32)

    loads[3].wait()

    def arrange(g, extra):
        for k in range(2):
            j = 2 * g + k
            start = pl.multiple_of(jnp.minimum(128 * j, WIDTH - 256), 128)
            col = iota((1, 256), 1)
            lane = lax.rem(col, 128)
            source = jnp.where(col < 128, 129 * j + lane, jnp.where(lane == 16 * lax.rem(j, 8), 129 * j + 128, -1))
            pick = jnp.where(iota((256, 256), 0) == source - start, 1.0, 0.0).astype(BF16)
            part = jnp.dot(raw[:, pl.ds(start, 256)], pick, preferred_element_type=F32)
            TT[0, c, :, pl.ds(pl.multiple_of(128 * j, 128), 128)] = part[:, :128].astype(BF16)
            extra += part[:, 128:]
        return extra

    for half in range(2):
        extra = lax.fori_loop(4 * half, 4 * half + 4, arrange, jnp.zeros((128, 128), F32))
        TT[0, c, :, WIDTH + 128 * half : WIDTH + 128 * half + 128] = extra.astype(BF16)
    send(remote(TT.at[0, c], TT.at[0, c], us.at[0], ur.at[0], at(dc=1)))

    relay_t(1)
    relay_c(1)
    plane = list(pending)
    pending.clear()
    for d in (1, 2, 3):
        send(remote(PS.at[d], PR.at[4 - d], ps.at[d - 1], prs.at[d - 1], at(dx=d)))
    PR[0] = PS[0]
    spread_h(0)

    def share(n, d, arrivals):
        for k in arrivals:
            wait_h(0, k)
        ref = TT.at[d, c]
        send(remote(ref, ref, us.at[n], ur.at[n], at(dc=1)))

    def shared(n, d):
        ref = TT.at[d, 1 - c]
        remote(ref, ref, us.at[n], ur.at[n], at(dc=1)).wait_recv()

    ones = jnp.ones((16, 512), BF16)
    cot_sum = jnp.zeros((16, 512), F32)
    for step, (i, arrivals) in enumerate(((0, ()), (3, (1,)), (1, (3,)), (2, (4, 5)))):
        if not step:
            for n in range(2):
                for k in (1, 3, 4, 5):
                    wait_t(n, k)
        for k in arrivals:
            for n in range(2):
                wait_c(n, k)
        right = C[:, i].reshape(512, 512)
        left = T[:, i].reshape(512, 512)
        part = lax.dot_general(left, right, (((0,), (0,)), ((), ())), preferred_element_type=F32)
        if step:
            prod[0:512] += part
        else:
            prod[0:512] = part
        cot_sum += jnp.dot(ones, right, preferred_element_type=F32)

    small = SL[y].astype(F32)
    for d in (1, 2, 3):
        ref = SL.at[wrap(y - d, 4)]
        remote(ref, ref, s2s.at[d - 1], s2r.at[d - 1], at(dy=d)).wait_recv()
        small += SL[wrap(y - d, 4)].astype(F32)
    rest = jnp.where(y == 0, small, jnp.where(y == 1, pltpu.roll(small, 12, 0), pltpu.roll(small, 8, 0)))
    prod[512:528] = jnp.where(rows < jnp.where(y < 3, 4, 0), rest, 0.0)
    keep_half = pl.ds(pl.multiple_of(256 * c, 128), 256)
    give_half = pl.ds(pl.multiple_of(256 * (1 - c), 128), 256)
    weight = gain[:, pl.ds(pl.multiple_of(512 * x, 128), 512)]
    for k in range(4):
        for i in range(4):
            start = 129 * k + 32 * i
            part = prod[start : start + 32]
            if i:
                part = jnp.where(x < i, prod[start + 1 : start + 33], part)
            zs[k, 32 * i : 32 * i + 32] = (part * weight).astype(BF16)
        extra = prod[129 * k + 32 : 129 * k + 33]
        for i in range(1, 4):
            extra = jnp.where(x == i, prod[129 * k + 32 * i + 32 : 129 * k + 32 * i + 33], extra)
        block = jnp.where(rows == 1, cot_sum * weight, jnp.where(rows == 2, small[12:13] + small[13:14], 0.0))
        zs[k, 128:144] = jnp.where(rows == 0, extra * weight, block).astype(BF16)
        send(remote(zs.at[k, :, give_half], cr.at[k], cs.at[k], crs.at[k], at(dc=1)))
    relay_h(0)

    for j in range(4):
        k = wrap(zl + j, 4)
        remote(zs.at[k, :, give_half], cr.at[k], cs.at[k], crs.at[k], at(dc=1)).wait_recv()
        chip = (zs[k, :, keep_half].astype(F32) + cr[k].astype(F32)).astype(BF16)
        zb[k] = chip[:, :128]
        zb[4 + k] = chip[:, 128:]
        for d in (j, j + 4):
            if d:
                to_z = wrap(z + d, 8)
                send(remote(zb.at[to_z], zr.at[z], zss.at[d - 1], zrs.at[d - 1], at(dz=d)))
    zr[z] = zb[z]

    settle(plane)
    for d in (1, 2, 3):
        ref = PR.at[4 - d]
        remote(ref, ref, ps.at[d - 1], prs.at[d - 1], at(dx=d)).wait_recv()
    for d in range(1, 8):
        ref = zr.at[wrap(z - d, 8)]
        remote(ref, ref, zss.at[d - 1], zrs.at[d - 1], at(dz=d)).wait_recv()
    group = zr[0].astype(F32)
    for k in range(1, 8):
        group += zr[k].astype(F32)

    def low_teacher(grad, mixed, old_one, old_two):
        new_one = beta_one * old_one + (1.0 - beta_one) * grad
        new_two = beta_two * old_two + (1.0 - beta_two) * grad * grad
        first = new_one / (1.0 - beta_one**STEP)
        second = new_two / (1.0 - beta_two**STEP)
        return mixed - ((1.0 - ema_rate) * learn_rate) * (first / (jnp.sqrt(second) + epsilon))

    main = [low_teacher(group[32 * i : 32 * i + 32], *[PR[wrap(i - x, 4), k, 0:32] for k in range(3)]) for i in range(4)]
    first_row = iota((8, 128), 0) == 0
    extras = [jnp.where(first_row, PR[0, k, 32:40], PR[wrap(3 - x, 4), k, 32:40]) for k in range(3)]
    block = low_teacher(group[128:136], *extras)
    nothing = jnp.zeros((8, 128), F32)
    plain = jnp.concatenate(main + [nothing, nothing], axis=0)
    moved = pltpu.roll(plain, 1, 0)
    at_row = iota((GROUP, 128), 0)
    place_row = 32 * x + 32
    plain = jnp.where(at_row < place_row, plain, jnp.where(at_row == place_row, block[0:1], moved))
    plain = jnp.where(at_row == 129, block[1:2], jnp.where(at_row == 130, block[2:3], plain))
    W[0, 0] = plain.astype(BF16)

    before_columns = list(pending)
    pending.clear()
    parts = [pl.ds(0, 80), pl.ds(80, 64)]

    def column_view(n, d, k):
        if n == 0:
            return W.at[d, 0, parts[k]]
        return W.at[d, (1 if n == 1 else 6) + k]

    spread_w, wait_w, relay_w = ring(column_view, along_y, w3s, w3r)
    for d in (4, 1, 7, 2, 6, 3, 5):
        send(remote(W.at[0, 0], W.at[0, 8 - d], w2s.at[d - 1], w2r.at[d - 1], at(dz=d)))
    spread_w(0)

    both[h] = group[0:136]
    twin = remote(both.at[h], both.at[h], hs.at[0], hr.at[0], at(dz=4))
    send(twin)

    def come(d):
        ref = W.at[0, 8 - d]
        remote(ref, ref, w2s.at[d - 1], w2r.at[d - 1], at(dz=d)).wait_recv()

    come(7)
    come(6)
    spread_w(1)
    come(1)
    come(2)
    spread_w(2)
    relay_w(0)
    share(1, 3, (1,))
    share(2, 1, (3,))
    for d in (3, 5, 4):
        come(d)
    far = W.at[0, pl.ds(3, 3)]
    for d in (1, 2, 3):
        send(remote(far, W.at[4 - d, pl.ds(3, 3)], fs.at[d - 1], fr.at[d - 1], at(dy=d)))
    relay_w(1)
    relay_w(2)

    ref = both.at[1 - h]
    remote(ref, ref, hs.at[0], hr.at[0], at(dz=4)).wait_recv()
    for i in range(4):
        for k in range(2):
            side = slice(128 * k, 128 * k + 128)
            xs[i, 0:32, side] = both[k, 32 * i : 32 * i + 32]
            xs[i, 32:40, side] = both[k, 128:136]
    slot = 2 * x + c
    others = [(dx, dc) for dx in range(4) for dc in range(2) if dx or dc]
    for n, (dx, dc) in enumerate(others):
        send(remote(xs.at[wrap(x + dx, 4)], xr.at[slot], xss.at[n], xrs.at[n], at(dx=dx, dc=dc)))
    xr[slot] = xs[x]
    share(3, 2, (4, 5))

    def block_at(i, j, n):
        return W.at[i, wrap(4 * n + j - z, 8)]

    def accumulate(i, a):
        total = jnp.zeros((256, 256), F32)
        for k in range(2):
            sides = [
                jnp.concatenate([block_at(i, 2 * k + j, n)[0:128] for j in range(2)], axis=0) for n in range(2)
            ]
            right = jnp.concatenate(sides, axis=1)
            start = pl.multiple_of(512 * wrap(y + i, 4) + 256 * k, 128)
            left = TT[a, :, :, pl.ds(start, 256)].reshape(256, 256)
            total += jnp.dot(left, right, preferred_element_type=F32)
        return total

    shared(0, 0)
    shared(1, 3)
    shared(2, 1)
    shared(3, 2)
    settle(before_columns)

    def begin(a, carry):
        acc[a] = accumulate(0, a)
        return carry

    lax.fori_loop(0, 4, begin, 0)
    for i, arrivals in ((3, (1,)), (1, (3,)), (2, (4, 5))):
        for n in range(3):
            for k in arrivals:
                wait_w(n, k)
        ref = W.at[i, pl.ds(3, 3)]
        remote(ref, ref, fs.at[0], fr.at[3 - i], at(dy=1)).wait_recv()

    ends = jnp.concatenate(
        [
            jnp.concatenate(
                [block_at(wrap(i - y, 4), j, n)[128:144] for i in range(4) for j in range(4)], axis=0
            )
            for n in range(2)
        ],
        axis=1,
    )
    tail = ends[240:256].astype(F32)
    bias_t, scale_t = tail[1:2], tail[2:3]
    columns = list(pending)
    pending.clear()
    out_cols = branch_res.at[:, pl.ds(pl.multiple_of(256 * slot, 128), 256)]
    n = 0
    for d in (2, 1, 3, 0):
        a = d
        total = acc[a] + accumulate(3, a) + accumulate(1, a) + accumulate(2, a) + jnp.dot(
            TT[a, :, :, WIDTH:].reshape(256, 256), ends, preferred_element_type=F32
        )
        OUT[a] = (scale_t * (total + bias_t)).astype(BF16).reshape(2, 128, 256)
        for dc in range(2):
            core = wrap(c + dc, 2)
            if d or dc:
                send(remote(OUT.at[a, core], out_cols, os.at[n], orr.at[slot], at(dx=d, dc=dc)))
                n += 1
    stay = pltpu.make_async_copy(OUT.at[0, c], out_cols, own_sem.at[1])
    stay.start()
    settle(columns)

    for n, (dx, dc) in enumerate(others):
        ref = xr.at[2 * wrap(x - dx, 4) + wrap(c - dc, 2)]
        remote(ref, ref, xss.at[n], xrs.at[n], at(dx=dx, dc=dc)).wait_recv()
    last = jnp.where(f == 63, 1.0, 0.0).astype(F32)
    pad[...] = jnp.zeros_like(pad)
    tg[...] = jnp.zeros_like(tg)
    for e in range(8):
        for t in range(2):
            n = 2 * e + t
            pad[n : n + 1] = xr[e, 33:34, 128 * t : 128 * t + 128] * last
            tg[TAIL + 240 + n : TAIL + 241 + n] = xr[e, 34:35, 128 * t : 128 * t + 128] * last
    rolled = roll_by(pad[0:24], place, 1, range(7))
    pad[0:24] = jnp.where(lanes24 >= lane_at, rolled, pltpu.roll(rolled, 1, 0))
    tg[TAIL : TAIL + 256] += roll_by(pad[...], place, 0, range(7, 15))
    lanes = iota((8, 128), 1)
    subs = iota((8, 128), 0)

    def update(where, grad, inside):
        old = master[where]
        new_one = beta_one * one[where] + (1.0 - beta_one) * grad
        new_two = beta_two * two[where] + (1.0 - beta_two) * grad * grad
        first = new_one / (1.0 - beta_one**STEP)
        second = new_two / (1.0 - beta_two**STEP)
        decay = jnp.where(inside, decay_rate, 0.0) * old
        new = old - learn_rate * (first / (jnp.sqrt(second) + epsilon) + decay)
        master_out[where] = new
        one_out[where] = new_one
        two_out[where] = new_two
        teacher_out[where] = ema_rate * teacher[where] + (1.0 - ema_rate) * new

    for b in range(4):
        for m in range(4):
            for t in range(4):
                base = 128 * b + 4 * m + t
                where = (pl.ds(base, 8, stride=16), slice(None))
                e, side = 2 * wrap(x + m, 4) + t // 2, slice(128 * (t % 2), 128 * (t % 2) + 128)
                slots = 128 * base + 2048 * subs + lanes
                update(where, xr[e, 8 * b : 8 * b + 8, side] + tg[where], slots < limit)
    for t in range(4):
        where = (slice(512 + t, 513 + t), slice(None))
        e, side = 2 * x + t // 2, slice(128 * (t % 2), 128 * (t % 2) + 128)
        inside = jnp.full((1, 128), 65536, jnp.int32) < limit
        update(where, xr[e, 32:33, side] * (1.0 - last) + tg[where], inside)
    results = [
        pltpu.make_async_copy(src, dst, res_sem.at[k])
        for k, (src, dst) in enumerate(
            [(master_out, master_res), (one_out, one_res), (two_out, two_res), (teacher_out, teacher_res)]
        )
    ]
    for copy in results:
        copy.start()

    for n, (dx, dc) in enumerate(others):
        e = 2 * wrap(x - dx, 4) + wrap(c - dc, 2)
        ref = branch_res.at[:, pl.ds(pl.multiple_of(256 * e, 128), 256)]
        remote(ref, ref, os.at[n], orr.at[e], at(dc=1)).wait_recv()
    stay.wait()
    for copy in results:
        copy.wait()
    settle(pending)


def copy_kernel(*refs):
    sems = refs[15]
    loads = [pltpu.make_async_copy(refs[k], refs[10 + k], sems.at[k]) for k in range(5)]
    stores = [pltpu.make_async_copy(refs[10 + k], refs[5 + k], sems.at[5 + k]) for k in range(5)]
    for copy in loads:
        copy.start()
    for load, store in zip(loads, stores):
        load.wait()
        store.start()
    for copy in stores:
        copy.wait()


def per_device(
    tokens, cotangent, saved_branch, layer_gain, offsets, master, moment_one, moment_two, teacher, teacher_tokens
):
    anyspace = pl.BlockSpec(memory_space=pl.ANY)
    dma = pltpu.SemaphoreType.DMA
    flat = jax.ShapeDtypeStruct((FLAT, 128), F32)
    shard = pltpu.VMEM((FLAT, 128), F32)
    rows = pltpu.VMEM((128, WIDTH), BF16)
    results = [flat] * 4 + [jax.ShapeDtypeStruct((128, WIDTH), BF16)]
    outs = pl.pallas_call(
        kernel,
        out_shape=results,
        in_specs=[pl.BlockSpec(memory_space=pltpu.SMEM)] + [anyspace] * 9,
        out_specs=[anyspace] * 5,
        scratch_shapes=[
            pltpu.VMEM((1, WIDTH), F32),
            rows, rows, rows, rows,
            shard, shard, shard, shard, shard, shard, shard, shard, shard,
            pltpu.VMEM((4, 128, 512), BF16),
            pltpu.VMEM((4, 4, 128, 512), BF16),
            pltpu.VMEM((4, 4, 128, 512), BF16),
            pltpu.VMEM((4, 16, 512), BF16),
            pltpu.VMEM((4, 16, 512), BF16),
            pltpu.VMEM((4, 16, 512), BF16),
            pltpu.VMEM((528, 512), F32),
            pltpu.VMEM((4, GROUP, 512), BF16),
            pltpu.VMEM((4, GROUP, 256), BF16),
            pltpu.VMEM((8, GROUP, 128), BF16),
            pltpu.VMEM((8, GROUP, 128), BF16),
            pltpu.VMEM((4, 3, 40, 128), F32),
            pltpu.VMEM((4, 3, 40, 128), F32),
            pltpu.VMEM((2, 136, 128), F32),
            pltpu.VMEM((4, 40, 256), F32),
            pltpu.VMEM((8, 40, 256), F32),
            pltpu.VMEM((256, 128), F32),
            pltpu.VMEM((520, 128), F32),
            pltpu.VMEM((4, 2, 128, WIDTH + 256), BF16),
            pltpu.VMEM((4, 8, GROUP, 128), BF16),
            pltpu.VMEM((4, 256, 256), F32),
            pltpu.VMEM((4, 2, 128, 256), BF16),
            dma((9,)), dma((4,)), dma((2,)),
            dma((3,)), dma((3,)), dma((3,)), dma((3,)), dma((3,)), dma((3,)), dma((3,)), dma((3,)),
            dma((2, 6)), dma((2, 6)), dma((2, 6)), dma((2, 6)),
            dma((4,)), dma((4,)), dma((7,)), dma((7,)),
            dma((3,)), dma((3,)), dma((7,)), dma((7,)),
            dma((1, 6)), dma((1, 6)), dma((4,)), dma((4,)), dma((7,)), dma((7,)), dma((3, 6)), dma((3, 6)),
            dma((1,)), dma((1,)), dma((3,)), dma((3,)),
            dma((7,)), dma((8,)),
        ],
        compiler_params=pltpu.CompilerParams(collective_id=0, has_side_effects=True, vmem_limit_bytes=56 << 20),
        name="step",
    )(
        offsets, layer_gain.reshape(1, WIDTH), tokens, cotangent, saved_branch,
        *[a.reshape(FLAT, 128) for a in (master, moment_one, moment_two, teacher)], teacher_tokens,
    )
    outs = pl.pallas_call(
        copy_kernel,
        out_shape=results,
        in_specs=[anyspace] * 5,
        out_specs=[anyspace] * 5,
        scratch_shapes=[shard, shard, shard, shard, rows, dma((10,))],
        name="place",
    )(*outs)
    return tuple(a.reshape(SHARD) for a in outs[:4]) + (outs[4],)


def solution(mesh):
    rows = P(("fsdp", "dp"), None)
    return jax.shard_map(
        per_device,
        mesh=mesh,
        in_specs=(rows, rows, rows, P(), P(), P("fsdp"), P("fsdp"), P("fsdp"), P("fsdp"), rows),
        out_specs=(P("fsdp"), P("fsdp"), P("fsdp"), P("fsdp"), rows),
        check_vma=False,
    )
```

```python
import jax
import jax.numpy as jnp
from jax import lax
from jax.experimental import pallas as pl
from jax.experimental.pallas import tpu as pltpu
from jax.sharding import PartitionSpec as P

MESH = pl.DeviceIdType.MESH
F32 = jnp.float32
BF16 = jnp.bfloat16

STEP = 1000
beta_one = 0.9
beta_two = 0.999
learn_rate = 0.001
decay_rate = 0.04
ema_rate = 0.994
epsilon = 1e-08

WIDTH = 2048
PROJ = WIDTH * WIDTH
SHARD = 66048
FLAT = SHARD // 128
TAIL = 260
GROUP = 144


def wrap(value, size):
    return lax.rem(value + size, size)


def device(x, y, z, c):
    return (y * 16 + lax.rem(z, 4) * 4 + x, lax.div(z, 4) * 2 + c)


def remote(src, dst, send, recv, to):
    return pltpu.make_async_remote_copy(
        src_ref=src, dst_ref=dst, send_sem=send, recv_sem=recv, device_id=to, device_id_type=MESH
    )


def roll_by(value, amount, axis, bits):
    for bit in bits:
        on = jnp.broadcast_to(lax.rem(lax.div(amount, 2**bit), 2) == 1, value.shape)
        value = jnp.where(on, pltpu.roll(value, 2 ** (bit - bits[0]), axis), value)
    return value


def iota(shape, axis):
    return lax.broadcasted_iota(jnp.int32, shape, axis)


def kernel(
    offsets, gain_hbm, tokens_hbm, cot_hbm, saved_hbm, master_hbm, one_hbm, two_hbm, teacher_hbm, tt_hbm,
    master_res, one_res, two_res, teacher_res, branch_res,
    gain, tok, cot, saved, raw, master, one, two, teacher, mix, master_out, one_out, two_out, teacher_out,
    TW, T, C, SX, SL, SS, prod, zs, cr, zb, zr, PS, PR, both, xs, xr, pad, tg, TT, W, acc, OUT,
    in_sem, res_sem, own_sem, a1s, a1r, b1s, b1r, s1s, s1r, s2s, s2r, a2s, a2r, b2s, b2r, cs, crs, zss, zrs,
    ps, prs, xss, xrs, ts, tr, us, ur, w2s, w2r, w3s, w3r, hs, hr, fs, fr, os, orr,
):
    f = lax.axis_index("fsdp")
    p = lax.axis_index("dp")
    x = lax.rem(f, 4)
    zl = lax.rem(lax.div(f, 4), 4)
    y = lax.div(f, 16)
    c = lax.rem(p, 2)
    z = lax.div(p, 2) * 4 + zl

    def at(dx=0, dy=0, dz=0, dc=0):
        return device(wrap(x + dx, 4), wrap(y + dy, 4), wrap(z + dz, 8), wrap(c + dc, 2))

    partners = (
        [dict(dx=d) for d in (1, 2, 3)]
        + [dict(dy=d) for d in (1, 2, 3)]
        + [dict(dz=d) for d in range(1, 8)]
        + [dict(dx=d, dc=1) for d in range(4)]
    )
    h = lax.div(z, 4)
    loads = [
        pltpu.make_async_copy(src, dst, in_sem.at[k])
        for k, (src, dst) in enumerate(
            [
                (tokens_hbm, tok), (cot_hbm, cot), (saved_hbm, saved), (tt_hbm, raw), (gain_hbm, gain),
                (master_hbm, master), (one_hbm, one), (two_hbm, two), (teacher_hbm, teacher),
            ]
        )
    ]
    for copy in loads:
        copy.start()
    barrier = pltpu.get_barrier_semaphore()
    for partner in partners:
        pl.semaphore_signal(barrier, inc=1, device_id=at(**partner), device_id_type=MESH)
    pl.semaphore_wait(barrier, len(partners))

    pending = []

    def send(copy):
        copy.start()
        pending.append(copy)

    def settle(copies):
        for copy in copies:
            copy.wait_send()

    def ring(view, to, sends, recvs):
        def spread(n):
            for k, (half, d) in enumerate([(0, 1), (1, 1), (1, -1), (0, -1)]):
                send(remote(view(n, 0, half), view(n, -d % 4, half), sends.at[n, k], recvs.at[n, k], to(d)))

        def wait(n, k):
            half, d = [(0, 3), (1, 3), (1, 1), (0, 1), (0, 2), (1, 2)][k]
            ref = view(n, d, half)
            remote(ref, ref, sends.at[n, k], recvs.at[n, k], to(1)).wait_recv()

        def relay(n):
            for k, half, d in ((0, 0, 1), (2, 1, -1)):
                wait(n, k)
                j = 4 + k // 2
                send(remote(view(n, -d % 4, half), view(n, 2, half), sends.at[n, j], recvs.at[n, j], to(d)))

        return spread, wait, relay

    halves = [pl.ds(0, 64), pl.ds(64, 64)]
    groups = [pl.ds(0, 1), pl.ds(1, 3)]
    along_x = lambda d: at(dx=d)
    along_y = lambda d: at(dy=d)
    spread_t, wait_t, relay_t = ring(lambda n, d, k: T.at[d, groups[n], halves[k]], along_x, a2s, a2r)
    spread_c, wait_c, relay_c = ring(lambda n, d, k: C.at[groups[n], d, halves[k]], along_y, b2s, b2r)
    spread_h, wait_h, relay_h = ring(lambda n, d, k: TT.at[d, c, halves[k]], along_x, ts, tr)

    def quarter(i):
        return cot_hbm.at[:, pl.ds(pl.multiple_of(512 * i, 128), 512)]

    mine = pltpu.make_async_copy(quarter(x), C.at[0, 0], own_sem.at[0])
    mine.start()
    for d in (1, 2, 3):
        send(remote(quarter(wrap(x + d, 4)), C.at[4 - d, 0], b1s.at[d - 1], b1r.at[d - 1], at(dx=d)))
    mine.wait()
    spread_c(0)
    loads[0].wait()
    for i in range(4):
        end = min(512 * i + 640, WIDTH)
        window = tok[:, 512 * i : end].astype(F32)
        if i:
            window = pltpu.roll(window, end - 512 * i - 4 * i, 1)[:, :512]
        else:
            window = window[:, :512]
        if i == 3:
            window = jnp.where(iota((128, 512), 1) < 500, window, 0.0)
        TW[i] = window.astype(BF16)
    for d in (1, 2, 3):
        send(remote(TW.at[wrap(y + d, 4)], T.at[0, 4 - d], a1s.at[d - 1], a1r.at[d - 1], at(dy=d)))
    T[0, 0] = TW[y]
    spread_t(0)
    loads[1].wait()
    loads[2].wait()
    total = jnp.zeros((1, WIDTH), F32)
    for r in range(0, 128, 16):
        total += jnp.sum(cot[r : r + 16].astype(F32) * saved[r : r + 16].astype(F32), axis=0, keepdims=True)
    top = total.astype(BF16).astype(F32)
    lane = iota((128, 128), 1)
    left = jnp.zeros((128, 128), F32)
    for i in range(3):
        tile = tok[:, 512 * (i + 1) : 512 * (i + 1) + 128].astype(F32)
        left = jnp.where(jnp.logical_and(lane >= 4 * i, lane < 4 * i + 4), tile, left)
    rows = iota((16, 512), 0)
    for i in range(4):
        side = slice(512 * i, 512 * i + 512)
        part = lax.dot_general(
            left.astype(BF16), cot[:, side], (((0,), (0,)), ((), ())), preferred_element_type=F32
        )[:16]
        part = jnp.where(rows == 12, top[:, side], jnp.where(rows == 13, total[:, side] - top[:, side], part))
        SS[i] = part.astype(BF16)
    for d in (1, 2, 3):
        send(remote(SS.at[wrap(x + d, 4)], SX.at[x], s1s.at[d - 1], s1r.at[d - 1], at(dx=d)))
    SX[x] = SS[x]

    for d in (1, 2, 3):
        ref = T.at[0, 4 - d]
        remote(ref, ref, a1s.at[d - 1], a1r.at[d - 1], at(dy=d)).wait_recv()
    spread_t(1)
    for d in (1, 2, 3):
        ref = C.at[4 - d, 0]
        remote(ref, ref, b1s.at[d - 1], b1r.at[d - 1], at(dx=d)).wait_recv()
    spread_c(1)
    relay_t(0)
    relay_c(0)

    for d in (1, 2, 3):
        ref = SX.at[wrap(x - d, 4)]
        remote(ref, ref, s1s.at[d - 1], s1r.at[d - 1], at(dx=d)).wait_recv()
    small = jnp.zeros((16, 512), F32)
    for i in range(4):
        small += SX[i].astype(F32)
    total = small[12:13] + small[13:14]
    top = total.astype(BF16).astype(F32)
    SL[y] = jnp.where(rows == 12, top, jnp.where(rows == 13, total - top, small)).astype(BF16)
    for d in (1, 2, 3):
        send(remote(SL.at[y], SL.at[y], s2s.at[d - 1], s2r.at[d - 1], at(dy=d)))

    for copy in loads[4:]:
        copy.wait()
    limit = PROJ - SHARD * f
    spots = 128 * iota((FLAT, 128), 0) + iota((FLAT, 128), 1)
    keep = jnp.where(spots < limit, 1.0 - learn_rate * decay_rate, 1.0)
    mix[...] = ema_rate * teacher[...] + (1.0 - ema_rate) * keep * master[...]
    place = jnp.full((1, 128), offsets[1] - PROJ, jnp.int32)
    row_back = lax.rem(32768 - lax.div(place, 128) * 128, 32768)
    lane_at = lax.rem(place, 128)
    lane_back = lax.rem(128 - lane_at, 128)
    lanes24 = iota((24, 128), 1)
    mine_of = lambda four: jnp.where(
        c == 0, jnp.where(h == 0, four[0], four[1]), jnp.where(h == 0, four[2], four[3])
    )
    for k, source in enumerate((mix, one, two)):
        for b in range(4):
            for m in range(4):
                four = [source[pl.ds(128 * b + 4 * m + t, 8, stride=16), :] for t in range(4)]
                PS[m, k, 8 * b : 8 * b + 8] = mine_of(four)
        tail = source[TAIL : TAIL + 256]
        moved = roll_by(tail, row_back, 0, range(7, 15))[0:24]
        rolled = roll_by(moved, lane_back, 1, range(7))
        bias = jnp.where(lanes24 < 128 - lane_at, rolled, pltpu.roll(rolled, 23, 0))
        for m in range(4):
            to = wrap(m - x, 4)
            PS[to, k, 32:33] = mine_of([source[512 + t : 513 + t] for t in range(4)])
            PS[to, k, 33:34] = mine_of([bias[4 * m + t : 4 * m + t + 1] for t in range(4)])
            PS[to, k, 34:35] = mine_of([tail[240 + 4 * m + t : 241 + 4 * m + t] for t in range(4)])
            PS[to, k, 35:40] = jnp.zeros((5, 128), F32)

    loads[3].wait()

    def arrange(g, extra):
        for k in range(2):
            j = 2 * g + k
            start = pl.multiple_of(jnp.minimum(128 * j, WIDTH - 256), 128)
            col = iota((1, 256), 1)
            lane = lax.rem(col, 128)
            source = jnp.where(col < 128, 129 * j + lane, jnp.where(lane == 16 * lax.rem(j, 8), 129 * j + 128, -1))
            pick = jnp.where(iota((256, 256), 0) == source - start, 1.0, 0.0).astype(BF16)
            part = jnp.dot(raw[:, pl.ds(start, 256)], pick, preferred_element_type=F32)
            TT[0, c, :, pl.ds(pl.multiple_of(128 * j, 128), 128)] = part[:, :128].astype(BF16)
            extra += part[:, 128:]
        return extra

    for half in range(2):
        extra = lax.fori_loop(4 * half, 4 * half + 4, arrange, jnp.zeros((128, 128), F32))
        TT[0, c, :, WIDTH + 128 * half : WIDTH + 128 * half + 128] = extra.astype(BF16)
    send(remote(TT.at[0, c], TT.at[0, c], us.at[0], ur.at[0], at(dc=1)))

    relay_t(1)
    relay_c(1)
    plane = list(pending)
    pending.clear()
    for d in (1, 2, 3):
        send(remote(PS.at[d], PR.at[4 - d], ps.at[d - 1], prs.at[d - 1], at(dx=d)))
    PR[0] = PS[0]
    spread_h(0)

    def share(n, d, arrivals):
        for k in arrivals:
            wait_h(0, k)
        ref = TT.at[d, c]
        send(remote(ref, ref, us.at[n], ur.at[n], at(dc=1)))

    def shared(n, d):
        ref = TT.at[d, 1 - c]
        remote(ref, ref, us.at[n], ur.at[n], at(dc=1)).wait_recv()

    def multiply(spots):
        left = jnp.concatenate([T[i, k].reshape(-1, 512) for i, k in spots], axis=0)
        right = jnp.concatenate([C[i, k].reshape(-1, 512) for i, k in spots], axis=0)
        part = lax.dot_general(left, right, (((0,), (0,)), ((), ())), preferred_element_type=F32)
        return part, jnp.dot(jnp.ones((16, right.shape[0]), BF16), right, preferred_element_type=F32)

    for n in range(2):
        for k in (1, 3):
            wait_t(n, k)
            wait_c(n, k)
    prod[0:512], cot_sum = multiply([(slice(0, 2), k) for k in (0, 1, 3)] + [(3, k) for k in (0, 1, 3)])
    for n in range(2):
        for k in (4, 5):
            wait_t(n, k)
            wait_c(n, k)
    part, more = multiply([(2, slice(0, 4)), (slice(0, 2), 2), (3, 2)])
    prod[0:512] += part
    cot_sum += more

    small = SL[y].astype(F32)
    for d in (1, 2, 3):
        ref = SL.at[wrap(y - d, 4)]
        remote(ref, ref, s2s.at[d - 1], s2r.at[d - 1], at(dy=d)).wait_recv()
        small += SL[wrap(y - d, 4)].astype(F32)
    rest = jnp.where(y == 0, small, jnp.where(y == 1, pltpu.roll(small, 12, 0), pltpu.roll(small, 8, 0)))
    prod[512:528] = jnp.where(rows < jnp.where(y < 3, 4, 0), rest, 0.0)
    keep_half = pl.ds(pl.multiple_of(256 * c, 128), 256)
    give_half = pl.ds(pl.multiple_of(256 * (1 - c), 128), 256)
    weight = gain[:, pl.ds(pl.multiple_of(512 * x, 128), 512)]
    for k in range(4):
        for i in range(4):
            start = 129 * k + 32 * i
            part = prod[start : start + 32]
            if i:
                part = jnp.where(x < i, prod[start + 1 : start + 33], part)
            zs[k, 32 * i : 32 * i + 32] = (part * weight).astype(BF16)
        extra = prod[129 * k + 32 : 129 * k + 33]
        for i in range(1, 4):
            extra = jnp.where(x == i, prod[129 * k + 32 * i + 32 : 129 * k + 32 * i + 33], extra)
        block = jnp.where(rows == 1, cot_sum * weight, jnp.where(rows == 2, small[12:13] + small[13:14], 0.0))
        zs[k, 128:144] = jnp.where(rows == 0, extra * weight, block).astype(BF16)
        send(remote(zs.at[k, :, give_half], cr.at[k], cs.at[k], crs.at[k], at(dc=1)))
    relay_h(0)

    for j in range(4):
        k = wrap(zl + j, 4)
        remote(zs.at[k, :, give_half], cr.at[k], cs.at[k], crs.at[k], at(dc=1)).wait_recv()
        chip = (zs[k, :, keep_half].astype(F32) + cr[k].astype(F32)).astype(BF16)
        zb[k] = chip[:, :128]
        zb[4 + k] = chip[:, 128:]
        for d in (j, j + 4):
            if d:
                to_z = wrap(z + d, 8)
                send(remote(zb.at[to_z], zr.at[z], zss.at[d - 1], zrs.at[d - 1], at(dz=d)))
    zr[z] = zb[z]

    settle(plane)
    for d in (1, 2, 3):
        ref = PR.at[4 - d]
        remote(ref, ref, ps.at[d - 1], prs.at[d - 1], at(dx=d)).wait_recv()
    for d in range(1, 8):
        ref = zr.at[wrap(z - d, 8)]
        remote(ref, ref, zss.at[d - 1], zrs.at[d - 1], at(dz=d)).wait_recv()
    group = zr[0].astype(F32)
    for k in range(1, 8):
        group += zr[k].astype(F32)

    def low_teacher(grad, mixed, old_one, old_two):
        new_one = beta_one * old_one + (1.0 - beta_one) * grad
        new_two = beta_two * old_two + (1.0 - beta_two) * grad * grad
        first = new_one / (1.0 - beta_one**STEP)
        second = new_two / (1.0 - beta_two**STEP)
        return mixed - ((1.0 - ema_rate) * learn_rate) * (first / (jnp.sqrt(second) + epsilon))

    main = [low_teacher(group[32 * i : 32 * i + 32], *[PR[wrap(i - x, 4), k, 0:32] for k in range(3)]) for i in range(4)]
    first_row = iota((8, 128), 0) == 0
    extras = [jnp.where(first_row, PR[0, k, 32:40], PR[wrap(3 - x, 4), k, 32:40]) for k in range(3)]
    block = low_teacher(group[128:136], *extras)
    nothing = jnp.zeros((8, 128), F32)
    plain = jnp.concatenate(main + [nothing, nothing], axis=0)
    moved = pltpu.roll(plain, 1, 0)
    at_row = iota((GROUP, 128), 0)
    place_row = 32 * x + 32
    plain = jnp.where(at_row < place_row, plain, jnp.where(at_row == place_row, block[0:1], moved))
    plain = jnp.where(at_row == 129, block[1:2], jnp.where(at_row == 130, block[2:3], plain))
    W[0, 0] = plain.astype(BF16)

    before_columns = list(pending)
    pending.clear()
    parts = [pl.ds(0, 80), pl.ds(80, 64)]

    def column_view(n, d, k):
        if n == 0:
            return W.at[d, 0, parts[k]]
        return W.at[d, (1 if n == 1 else 6) + k]

    spread_w, wait_w, relay_w = ring(column_view, along_y, w3s, w3r)
    for d in (4, 1, 7, 2, 6, 3, 5):
        send(remote(W.at[0, 0], W.at[0, 8 - d], w2s.at[d - 1], w2r.at[d - 1], at(dz=d)))
    spread_w(0)

    both[h] = group[0:136]
    twin = remote(both.at[h], both.at[h], hs.at[0], hr.at[0], at(dz=4))
    send(twin)

    def come(d):
        ref = W.at[0, 8 - d]
        remote(ref, ref, w2s.at[d - 1], w2r.at[d - 1], at(dz=d)).wait_recv()

    come(7)
    come(6)
    spread_w(1)
    come(1)
    come(2)
    spread_w(2)
    relay_w(0)
    share(1, 3, (1,))
    share(2, 1, (3,))
    for d in (3, 5, 4):
        come(d)
    far = W.at[0, pl.ds(3, 3)]
    for d in (1, 2, 3):
        send(remote(far, W.at[4 - d, pl.ds(3, 3)], fs.at[d - 1], fr.at[d - 1], at(dy=d)))
    relay_w(1)
    relay_w(2)

    ref = both.at[1 - h]
    remote(ref, ref, hs.at[0], hr.at[0], at(dz=4)).wait_recv()
    for i in range(4):
        for k in range(2):
            side = slice(128 * k, 128 * k + 128)
            xs[i, 0:32, side] = both[k, 32 * i : 32 * i + 32]
            xs[i, 32:40, side] = both[k, 128:136]
    slot = 2 * x + c
    others = [(dx, dc) for dx in range(4) for dc in range(2) if dx or dc]
    for n, (dx, dc) in enumerate(others):
        send(remote(xs.at[wrap(x + dx, 4)], xr.at[slot], xss.at[n], xrs.at[n], at(dx=dx, dc=dc)))
    xr[slot] = xs[x]
    share(3, 2, (4, 5))

    def block_at(i, j, n):
        return W.at[i, wrap(4 * n + j - z, 8)]

    def accumulate(i, a):
        total = jnp.zeros((256, 256), F32)
        for k in range(2):
            sides = [
                jnp.concatenate([block_at(i, 2 * k + j, n)[0:128] for j in range(2)], axis=0) for n in range(2)
            ]
            right = jnp.concatenate(sides, axis=1)
            start = pl.multiple_of(512 * wrap(y + i, 4) + 256 * k, 128)
            left = TT[a, :, :, pl.ds(start, 256)].reshape(256, 256)
            total += jnp.dot(left, right, preferred_element_type=F32)
        return total

    shared(0, 0)
    shared(1, 3)
    shared(2, 1)
    shared(3, 2)
    settle(before_columns)

    def begin(a, carry):
        acc[a] = accumulate(0, a)
        return carry

    lax.fori_loop(0, 4, begin, 0)
    for i, arrivals in ((3, (1,)), (1, (3,)), (2, (4, 5))):
        for n in range(3):
            for k in arrivals:
                wait_w(n, k)
        ref = W.at[i, pl.ds(3, 3)]
        remote(ref, ref, fs.at[0], fr.at[3 - i], at(dy=1)).wait_recv()

    ends = jnp.concatenate(
        [
            jnp.concatenate(
                [block_at(wrap(i - y, 4), j, n)[128:144] for i in range(4) for j in range(4)], axis=0
            )
            for n in range(2)
        ],
        axis=1,
    )
    tail = ends[240:256].astype(F32)
    bias_t, scale_t = tail[1:2], tail[2:3]
    columns = list(pending)
    pending.clear()
    out_cols = branch_res.at[:, pl.ds(pl.multiple_of(256 * slot, 128), 256)]
    n = 0
    for d in (2, 1, 3, 0):
        a = d
        total = acc[a] + accumulate(3, a) + accumulate(1, a) + accumulate(2, a) + jnp.dot(
            TT[a, :, :, WIDTH:].reshape(256, 256), ends, preferred_element_type=F32
        )
        OUT[a] = (scale_t * (total + bias_t)).astype(BF16).reshape(2, 128, 256)
        for dc in (1, 0):
            core = wrap(c + dc, 2)
            if d or dc:
                send(remote(OUT.at[a, core], out_cols, os.at[n], orr.at[slot], at(dx=d, dc=dc)))
                n += 1
    stay = pltpu.make_async_copy(OUT.at[0, c], out_cols, own_sem.at[1])
    stay.start()
    settle(columns)

    for n, (dx, dc) in enumerate(others):
        ref = xr.at[2 * wrap(x - dx, 4) + wrap(c - dc, 2)]
        remote(ref, ref, xss.at[n], xrs.at[n], at(dx=dx, dc=dc)).wait_recv()
    last = jnp.where(f == 63, 1.0, 0.0).astype(F32)
    pad[...] = jnp.zeros_like(pad)
    tg[...] = jnp.zeros_like(tg)
    for e in range(8):
        for t in range(2):
            n = 2 * e + t
            pad[n : n + 1] = xr[e, 33:34, 128 * t : 128 * t + 128] * last
            tg[TAIL + 240 + n : TAIL + 241 + n] = xr[e, 34:35, 128 * t : 128 * t + 128] * last
    rolled = roll_by(pad[0:24], place, 1, range(7))
    pad[0:24] = jnp.where(lanes24 >= lane_at, rolled, pltpu.roll(rolled, 1, 0))
    tg[TAIL : TAIL + 256] += roll_by(pad[...], place, 0, range(7, 15))
    lanes = iota((8, 128), 1)
    subs = iota((8, 128), 0)

    def update(where, grad, inside):
        old = master[where]
        new_one = beta_one * one[where] + (1.0 - beta_one) * grad
        new_two = beta_two * two[where] + (1.0 - beta_two) * grad * grad
        first = new_one / (1.0 - beta_one**STEP)
        second = new_two / (1.0 - beta_two**STEP)
        decay = jnp.where(inside, decay_rate, 0.0) * old
        new = old - learn_rate * (first / (jnp.sqrt(second) + epsilon) + decay)
        master_out[where] = new
        one_out[where] = new_one
        two_out[where] = new_two
        teacher_out[where] = ema_rate * teacher[where] + (1.0 - ema_rate) * new

    for b in range(4):
        for m in range(4):
            for t in range(4):
                base = 128 * b + 4 * m + t
                where = (pl.ds(base, 8, stride=16), slice(None))
                e, side = 2 * wrap(x + m, 4) + t // 2, slice(128 * (t % 2), 128 * (t % 2) + 128)
                slots = 128 * base + 2048 * subs + lanes
                update(where, xr[e, 8 * b : 8 * b + 8, side] + tg[where], slots < limit)
    for t in range(4):
        where = (slice(512 + t, 513 + t), slice(None))
        e, side = 2 * x + t // 2, slice(128 * (t % 2), 128 * (t % 2) + 128)
        inside = jnp.full((1, 128), 65536, jnp.int32) < limit
        update(where, xr[e, 32:33, side] * (1.0 - last) + tg[where], inside)
    results = [
        pltpu.make_async_copy(src, dst, res_sem.at[k])
        for k, (src, dst) in enumerate(
            [(master_out, master_res), (one_out, one_res), (two_out, two_res), (teacher_out, teacher_res)]
        )
    ]
    for copy in results:
        copy.start()

    for n, (dx, dc) in enumerate(others):
        e = 2 * wrap(x - dx, 4) + wrap(c - dc, 2)
        ref = branch_res.at[:, pl.ds(pl.multiple_of(256 * e, 128), 256)]
        remote(ref, ref, os.at[n], orr.at[e], at(dc=1)).wait_recv()
    stay.wait()
    for copy in results:
        copy.wait()
    settle(pending)


def copy_kernel(*refs):
    sems = refs[15]
    loads = [pltpu.make_async_copy(refs[k], refs[10 + k], sems.at[k]) for k in range(5)]
    stores = [pltpu.make_async_copy(refs[10 + k], refs[5 + k], sems.at[5 + k]) for k in range(5)]
    for copy in loads:
        copy.start()
    for load, store in zip(loads, stores):
        load.wait()
        store.start()
    for copy in stores:
        copy.wait()


def per_device(
    tokens, cotangent, saved_branch, layer_gain, offsets, master, moment_one, moment_two, teacher, teacher_tokens
):
    anyspace = pl.BlockSpec(memory_space=pl.ANY)
    dma = pltpu.SemaphoreType.DMA
    flat = jax.ShapeDtypeStruct((FLAT, 128), F32)
    shard = pltpu.VMEM((FLAT, 128), F32)
    rows = pltpu.VMEM((128, WIDTH), BF16)
    results = [flat] * 4 + [jax.ShapeDtypeStruct((128, WIDTH), BF16)]
    outs = pl.pallas_call(
        kernel,
        out_shape=results,
        in_specs=[pl.BlockSpec(memory_space=pltpu.SMEM)] + [anyspace] * 9,
        out_specs=[anyspace] * 5,
        scratch_shapes=[
            pltpu.VMEM((1, WIDTH), F32),
            rows, rows, rows, rows,
            shard, shard, shard, shard, shard, shard, shard, shard, shard,
            pltpu.VMEM((4, 128, 512), BF16),
            pltpu.VMEM((4, 4, 128, 512), BF16),
            pltpu.VMEM((4, 4, 128, 512), BF16),
            pltpu.VMEM((4, 16, 512), BF16),
            pltpu.VMEM((4, 16, 512), BF16),
            pltpu.VMEM((4, 16, 512), BF16),
            pltpu.VMEM((528, 512), F32),
            pltpu.VMEM((4, GROUP, 512), BF16),
            pltpu.VMEM((4, GROUP, 256), BF16),
            pltpu.VMEM((8, GROUP, 128), BF16),
            pltpu.VMEM((8, GROUP, 128), BF16),
            pltpu.VMEM((4, 3, 40, 128), F32),
            pltpu.VMEM((4, 3, 40, 128), F32),
            pltpu.VMEM((2, 136, 128), F32),
            pltpu.VMEM((4, 40, 256), F32),
            pltpu.VMEM((8, 40, 256), F32),
            pltpu.VMEM((256, 128), F32),
            pltpu.VMEM((520, 128), F32),
            pltpu.VMEM((4, 2, 128, WIDTH + 256), BF16),
            pltpu.VMEM((4, 8, GROUP, 128), BF16),
            pltpu.VMEM((4, 256, 256), F32),
            pltpu.VMEM((4, 2, 128, 256), BF16),
            dma((9,)), dma((4,)), dma((2,)),
            dma((3,)), dma((3,)), dma((3,)), dma((3,)), dma((3,)), dma((3,)), dma((3,)), dma((3,)),
            dma((2, 6)), dma((2, 6)), dma((2, 6)), dma((2, 6)),
            dma((4,)), dma((4,)), dma((7,)), dma((7,)),
            dma((3,)), dma((3,)), dma((7,)), dma((7,)),
            dma((1, 6)), dma((1, 6)), dma((4,)), dma((4,)), dma((7,)), dma((7,)), dma((3, 6)), dma((3, 6)),
            dma((1,)), dma((1,)), dma((3,)), dma((3,)),
            dma((7,)), dma((8,)),
        ],
        compiler_params=pltpu.CompilerParams(collective_id=0, has_side_effects=True, vmem_limit_bytes=56 << 20),
        name="step",
    )(
        offsets, layer_gain.reshape(1, WIDTH), tokens, cotangent, saved_branch,
        *[a.reshape(FLAT, 128) for a in (master, moment_one, moment_two, teacher)], teacher_tokens,
    )
    outs = pl.pallas_call(
        copy_kernel,
        out_shape=results,
        in_specs=[anyspace] * 5,
        out_specs=[anyspace] * 5,
        scratch_shapes=[shard, shard, shard, shard, rows, dma((10,))],
        name="place",
    )(*outs)
    return tuple(a.reshape(SHARD) for a in outs[:4]) + (outs[4],)


def solution(mesh):
    rows = P(("fsdp", "dp"), None)
    return jax.shard_map(
        per_device,
        mesh=mesh,
        in_specs=(rows, rows, rows, P(), P(), P("fsdp"), P("fsdp"), P("fsdp"), P("fsdp"), rows),
        out_specs=(P("fsdp"), P("fsdp"), P("fsdp"), P("fsdp"), rows),
        check_vma=False,
    )
```

```python
import jax
import jax.numpy as jnp
from jax import lax
from jax.experimental import pallas as pl
from jax.experimental.pallas import tpu as pltpu
from jax.sharding import PartitionSpec as P

MESH = pl.DeviceIdType.MESH
F32 = jnp.float32
BF16 = jnp.bfloat16

STEP = 1000
beta_one = 0.9
beta_two = 0.999
learn_rate = 0.001
decay_rate = 0.04
ema_rate = 0.994
epsilon = 1e-08

WIDTH = 2048
PROJ = WIDTH * WIDTH
SHARD = 66048
FLAT = SHARD // 128
TAIL = 260
GROUP = 144


def wrap(value, size):
    return lax.rem(value + size, size)


def device(x, y, z, c):
    return (y * 16 + lax.rem(z, 4) * 4 + x, lax.div(z, 4) * 2 + c)


def remote(src, dst, send, recv, to):
    return pltpu.make_async_remote_copy(
        src_ref=src, dst_ref=dst, send_sem=send, recv_sem=recv, device_id=to, device_id_type=MESH
    )


def roll_by(value, amount, axis, bits):
    for bit in bits:
        on = jnp.broadcast_to(lax.rem(lax.div(amount, 2**bit), 2) == 1, value.shape)
        value = jnp.where(on, pltpu.roll(value, 2 ** (bit - bits[0]), axis), value)
    return value


def iota(shape, axis):
    return lax.broadcasted_iota(jnp.int32, shape, axis)


def kernel(
    offsets, gain_hbm, tokens_hbm, cot_hbm, saved_hbm, master_hbm, one_hbm, two_hbm, teacher_hbm, tt_hbm,
    master_res, one_res, two_res, teacher_res, branch_res,
    gain, tok, cot, saved, raw, master, one, two, teacher, mix, master_out, one_out, two_out, teacher_out,
    TW, T, C, SX, SL, SS, prod, zs, cr, zb, zr, PS, PR, both, xs, xr, pad, tg, TT, W, acc, OUT,
    in_sem, res_sem, own_sem, a1s, a1r, b1s, b1r, s1s, s1r, s2s, s2r, a2s, a2r, b2s, b2r, cs, crs, zss, zrs,
    ps, prs, xss, xrs, ts, tr, us, ur, w2s, w2r, w3s, w3r, hs, hr, fs, fr, os, orr,
):
    f = lax.axis_index("fsdp")
    p = lax.axis_index("dp")
    x = lax.rem(f, 4)
    zl = lax.rem(lax.div(f, 4), 4)
    y = lax.div(f, 16)
    c = lax.rem(p, 2)
    z = lax.div(p, 2) * 4 + zl

    def at(dx=0, dy=0, dz=0, dc=0):
        return device(wrap(x + dx, 4), wrap(y + dy, 4), wrap(z + dz, 8), wrap(c + dc, 2))

    partners = (
        [dict(dx=d) for d in (1, 2, 3)]
        + [dict(dy=d) for d in (1, 2, 3)]
        + [dict(dz=d) for d in range(1, 8)]
        + [dict(dx=d, dc=1) for d in range(4)]
    )
    h = lax.div(z, 4)
    loads = [
        pltpu.make_async_copy(src, dst, in_sem.at[k])
        for k, (src, dst) in enumerate(
            [
                (tokens_hbm, tok), (cot_hbm, cot), (saved_hbm, saved), (tt_hbm, raw), (gain_hbm, gain),
                (master_hbm, master), (one_hbm, one), (two_hbm, two), (teacher_hbm, teacher),
            ]
        )
    ]
    for copy in loads:
        copy.start()
    barrier = pltpu.get_barrier_semaphore()
    for partner in partners:
        pl.semaphore_signal(barrier, inc=1, device_id=at(**partner), device_id_type=MESH)
    pl.semaphore_wait(barrier, len(partners))

    pending = []

    def send(copy):
        copy.start()
        pending.append(copy)

    def settle(copies):
        for copy in copies:
            copy.wait_send()

    def ring(view, to, sends, recvs):
        def spread(n):
            for k, (half, d) in enumerate([(0, 1), (1, 1), (1, -1), (0, -1)]):
                send(remote(view(n, 0, half), view(n, -d % 4, half), sends.at[n, k], recvs.at[n, k], to(d)))

        def wait(n, k):
            half, d = [(0, 3), (1, 3), (1, 1), (0, 1), (0, 2), (1, 2)][k]
            ref = view(n, d, half)
            remote(ref, ref, sends.at[n, k], recvs.at[n, k], to(1)).wait_recv()

        def relay(n):
            for k, half, d in ((0, 0, 1), (2, 1, -1)):
                wait(n, k)
                j = 4 + k // 2
                send(remote(view(n, -d % 4, half), view(n, 2, half), sends.at[n, j], recvs.at[n, j], to(d)))

        return spread, wait, relay

    halves = [pl.ds(0, 64), pl.ds(64, 64)]
    groups = [pl.ds(0, 1), pl.ds(1, 3)]
    along_x = lambda d: at(dx=d)
    along_y = lambda d: at(dy=d)
    spread_t, wait_t, relay_t = ring(lambda n, d, k: T.at[d, groups[n], halves[k]], along_x, a2s, a2r)
    spread_c, wait_c, relay_c = ring(lambda n, d, k: C.at[groups[n], d, halves[k]], along_y, b2s, b2r)
    spread_h, wait_h, relay_h = ring(lambda n, d, k: TT.at[d, c, halves[k]], along_x, ts, tr)

    def quarter(i):
        return cot_hbm.at[:, pl.ds(pl.multiple_of(512 * i, 128), 512)]

    mine = pltpu.make_async_copy(quarter(x), C.at[0, 0], own_sem.at[0])
    mine.start()
    for d in (1, 2, 3):
        send(remote(quarter(wrap(x + d, 4)), C.at[4 - d, 0], b1s.at[d - 1], b1r.at[d - 1], at(dx=d)))
    mine.wait()
    spread_c(0)
    loads[0].wait()
    for i in range(4):
        end = min(512 * i + 640, WIDTH)
        window = tok[:, 512 * i : end].astype(F32)
        if i:
            window = pltpu.roll(window, end - 512 * i - 4 * i, 1)[:, :512]
        else:
            window = window[:, :512]
        if i == 3:
            window = jnp.where(iota((128, 512), 1) < 500, window, 0.0)
        TW[i] = window.astype(BF16)
    for d in (1, 2, 3):
        send(remote(TW.at[wrap(y + d, 4)], T.at[0, 4 - d], a1s.at[d - 1], a1r.at[d - 1], at(dy=d)))
    T[0, 0] = TW[y]
    spread_t(0)
    loads[1].wait()
    loads[2].wait()
    total = jnp.zeros((1, WIDTH), F32)
    for r in range(0, 128, 16):
        total += jnp.sum(cot[r : r + 16].astype(F32) * saved[r : r + 16].astype(F32), axis=0, keepdims=True)
    top = total.astype(BF16).astype(F32)
    lane = iota((128, 128), 1)
    left = jnp.zeros((128, 128), F32)
    for i in range(3):
        tile = tok[:, 512 * (i + 1) : 512 * (i + 1) + 128].astype(F32)
        left = jnp.where(jnp.logical_and(lane >= 4 * i, lane < 4 * i + 4), tile, left)
    rows = iota((16, 512), 0)
    for i in range(4):
        side = slice(512 * i, 512 * i + 512)
        part = lax.dot_general(
            left.astype(BF16), cot[:, side], (((0,), (0,)), ((), ())), preferred_element_type=F32
        )[:16]
        part = jnp.where(rows == 12, top[:, side], jnp.where(rows == 13, total[:, side] - top[:, side], part))
        SS[i] = part.astype(BF16)
    for d in (1, 2, 3):
        send(remote(SS.at[wrap(x + d, 4)], SX.at[x], s1s.at[d - 1], s1r.at[d - 1], at(dx=d)))
    SX[x] = SS[x]

    for d in (1, 2, 3):
        ref = T.at[0, 4 - d]
        remote(ref, ref, a1s.at[d - 1], a1r.at[d - 1], at(dy=d)).wait_recv()
    spread_t(1)
    for d in (1, 2, 3):
        ref = C.at[4 - d, 0]
        remote(ref, ref, b1s.at[d - 1], b1r.at[d - 1], at(dx=d)).wait_recv()
    spread_c(1)
    relay_t(0)
    relay_c(0)

    for d in (1, 2, 3):
        ref = SX.at[wrap(x - d, 4)]
        remote(ref, ref, s1s.at[d - 1], s1r.at[d - 1], at(dx=d)).wait_recv()
    small = jnp.zeros((16, 512), F32)
    for i in range(4):
        small += SX[i].astype(F32)
    total = small[12:13] + small[13:14]
    top = total.astype(BF16).astype(F32)
    SL[y] = jnp.where(rows == 12, top, jnp.where(rows == 13, total - top, small)).astype(BF16)
    for d in (1, 2, 3):
        send(remote(SL.at[y], SL.at[y], s2s.at[d - 1], s2r.at[d - 1], at(dy=d)))

    for copy in loads[4:]:
        copy.wait()
    limit = PROJ - SHARD * f
    spots = 128 * iota((FLAT, 128), 0) + iota((FLAT, 128), 1)
    keep = jnp.where(spots < limit, 1.0 - learn_rate * decay_rate, 1.0)
    mix[...] = ema_rate * teacher[...] + (1.0 - ema_rate) * keep * master[...]
    place = jnp.full((1, 128), offsets[1] - PROJ, jnp.int32)
    row_back = lax.rem(32768 - lax.div(place, 128) * 128, 32768)
    lane_at = lax.rem(place, 128)
    lane_back = lax.rem(128 - lane_at, 128)
    lanes24 = iota((24, 128), 1)
    mine_of = lambda four: jnp.where(
        c == 0, jnp.where(h == 0, four[0], four[1]), jnp.where(h == 0, four[2], four[3])
    )
    for k, source in enumerate((mix, one, two)):
        for b in range(4):
            for m in range(4):
                four = [source[pl.ds(128 * b + 4 * m + t, 8, stride=16), :] for t in range(4)]
                PS[m, k, 8 * b : 8 * b + 8] = mine_of(four)
        tail = source[TAIL : TAIL + 256]
        moved = roll_by(tail, row_back, 0, range(7, 15))[0:24]
        rolled = roll_by(moved, lane_back, 1, range(7))
        bias = jnp.where(lanes24 < 128 - lane_at, rolled, pltpu.roll(rolled, 23, 0))
        for m in range(4):
            to = wrap(m - x, 4)
            PS[to, k, 32:33] = mine_of([source[512 + t : 513 + t] for t in range(4)])
            PS[to, k, 33:34] = mine_of([bias[4 * m + t : 4 * m + t + 1] for t in range(4)])
            PS[to, k, 34:35] = mine_of([tail[240 + 4 * m + t : 241 + 4 * m + t] for t in range(4)])
            PS[to, k, 35:40] = jnp.zeros((5, 128), F32)

    loads[3].wait()

    def arrange(g, extra):
        for k in range(2):
            j = 2 * g + k
            start = pl.multiple_of(jnp.minimum(128 * j, WIDTH - 256), 128)
            col = iota((1, 256), 1)
            lane = lax.rem(col, 128)
            source = jnp.where(col < 128, 129 * j + lane, jnp.where(lane == 16 * lax.rem(j, 8), 129 * j + 128, -1))
            pick = jnp.where(iota((256, 256), 0) == source - start, 1.0, 0.0).astype(BF16)
            part = jnp.dot(raw[:, pl.ds(start, 256)], pick, preferred_element_type=F32)
            TT[0, c, :, pl.ds(pl.multiple_of(128 * j, 128), 128)] = part[:, :128].astype(BF16)
            extra += part[:, 128:]
        return extra

    for half in range(2):
        extra = lax.fori_loop(4 * half, 4 * half + 4, arrange, jnp.zeros((128, 128), F32))
        TT[0, c, :, WIDTH + 128 * half : WIDTH + 128 * half + 128] = extra.astype(BF16)
    send(remote(TT.at[0, c], TT.at[0, c], us.at[0], ur.at[0], at(dc=1)))

    relay_t(1)
    relay_c(1)
    plane = list(pending)
    pending.clear()
    for d in (1, 2, 3):
        send(remote(PS.at[d], PR.at[4 - d], ps.at[d - 1], prs.at[d - 1], at(dx=d)))
    PR[0] = PS[0]
    spread_h(0)

    def share(n, d, arrivals):
        for k in arrivals:
            wait_h(0, k)
        ref = TT.at[d, c]
        send(remote(ref, ref, us.at[n], ur.at[n], at(dc=1)))

    def shared(n, d):
        ref = TT.at[d, 1 - c]
        remote(ref, ref, us.at[n], ur.at[n], at(dc=1)).wait_recv()

    def multiply(spots):
        left = jnp.concatenate([T[i, k].reshape(-1, 512) for i, k in spots], axis=0)
        right = jnp.concatenate([C[i, k].reshape(-1, 512) for i, k in spots], axis=0)
        part = lax.dot_general(left, right, (((0,), (0,)), ((), ())), preferred_element_type=F32)
        return part, jnp.dot(jnp.ones((16, right.shape[0]), BF16), right, preferred_element_type=F32)

    for n in range(2):
        for k in (1, 3):
            wait_t(n, k)
            wait_c(n, k)
    prod[0:512], cot_sum = multiply([(slice(0, 2), k) for k in (0, 1, 3)] + [(3, k) for k in (0, 1, 3)])
    for n in range(2):
        for k in (4, 5):
            wait_t(n, k)
            wait_c(n, k)
    part, more = multiply([(2, slice(0, 4)), (slice(0, 2), 2), (3, 2)])
    prod[0:512] += part
    cot_sum += more

    small = SL[y].astype(F32)
    for d in (1, 2, 3):
        ref = SL.at[wrap(y - d, 4)]
        remote(ref, ref, s2s.at[d - 1], s2r.at[d - 1], at(dy=d)).wait_recv()
        small += SL[wrap(y - d, 4)].astype(F32)
    rest = jnp.where(y == 0, small, jnp.where(y == 1, pltpu.roll(small, 12, 0), pltpu.roll(small, 8, 0)))
    prod[512:528] = jnp.where(rows < jnp.where(y < 3, 4, 0), rest, 0.0)
    keep_half = pl.ds(pl.multiple_of(256 * c, 128), 256)
    give_half = pl.ds(pl.multiple_of(256 * (1 - c), 128), 256)
    weight = gain[:, pl.ds(pl.multiple_of(512 * x, 128), 512)]
    for k in range(4):
        for i in range(4):
            start = 129 * k + 32 * i
            part = prod[start : start + 32]
            if i:
                part = jnp.where(x < i, prod[start + 1 : start + 33], part)
            zs[k, 32 * i : 32 * i + 32] = (part * weight).astype(BF16)
        extra = prod[129 * k + 32 : 129 * k + 33]
        for i in range(1, 4):
            extra = jnp.where(x == i, prod[129 * k + 32 * i + 32 : 129 * k + 32 * i + 33], extra)
        block = jnp.where(rows == 1, cot_sum * weight, jnp.where(rows == 2, small[12:13] + small[13:14], 0.0))
        zs[k, 128:144] = jnp.where(rows == 0, extra * weight, block).astype(BF16)
        send(remote(zs.at[k, :, give_half], cr.at[k], cs.at[k], crs.at[k], at(dc=1)))
    relay_h(0)

    for j in range(4):
        k = wrap(zl + j, 4)
        remote(zs.at[k, :, give_half], cr.at[k], cs.at[k], crs.at[k], at(dc=1)).wait_recv()
        chip = (zs[k, :, keep_half].astype(F32) + cr[k].astype(F32)).astype(BF16)
        zb[k] = chip[:, :128]
        zb[4 + k] = chip[:, 128:]
        for d in (j, j + 4):
            if d:
                to_z = wrap(z + d, 8)
                send(remote(zb.at[to_z], zr.at[z], zss.at[d - 1], zrs.at[d - 1], at(dz=d)))
    zr[z] = zb[z]

    settle(plane)
    for d in (1, 2, 3):
        ref = PR.at[4 - d]
        remote(ref, ref, ps.at[d - 1], prs.at[d - 1], at(dx=d)).wait_recv()
    for d in range(1, 8):
        ref = zr.at[wrap(z - d, 8)]
        remote(ref, ref, zss.at[d - 1], zrs.at[d - 1], at(dz=d)).wait_recv()
    group = zr[0].astype(F32)
    for k in range(1, 8):
        group += zr[k].astype(F32)

    def low_teacher(grad, mixed, old_one, old_two):
        new_one = beta_one * old_one + (1.0 - beta_one) * grad
        new_two = beta_two * old_two + (1.0 - beta_two) * grad * grad
        first = new_one / (1.0 - beta_one**STEP)
        second = new_two / (1.0 - beta_two**STEP)
        return mixed - ((1.0 - ema_rate) * learn_rate) * (first / (jnp.sqrt(second) + epsilon))

    main = [low_teacher(group[32 * i : 32 * i + 32], *[PR[wrap(i - x, 4), k, 0:32] for k in range(3)]) for i in range(4)]
    first_row = iota((8, 128), 0) == 0
    extras = [jnp.where(first_row, PR[0, k, 32:40], PR[wrap(3 - x, 4), k, 32:40]) for k in range(3)]
    block = low_teacher(group[128:136], *extras)
    nothing = jnp.zeros((8, 128), F32)
    plain = jnp.concatenate(main + [nothing, nothing], axis=0)
    moved = pltpu.roll(plain, 1, 0)
    at_row = iota((GROUP, 128), 0)
    place_row = 32 * x + 32
    plain = jnp.where(at_row < place_row, plain, jnp.where(at_row == place_row, block[0:1], moved))
    plain = jnp.where(at_row == 129, block[1:2], jnp.where(at_row == 130, block[2:3], plain))
    W[0, 0] = plain.astype(BF16)

    before_columns = list(pending)
    pending.clear()
    parts = [pl.ds(0, 80), pl.ds(80, 64)]

    def column_view(n, d, k):
        if n == 0:
            return W.at[d, 0, parts[k]]
        return W.at[d, (1 if n == 1 else 6) + k]

    spread_w, wait_w, relay_w = ring(column_view, along_y, w3s, w3r)
    for d in (4, 1, 7, 2, 6, 3, 5):
        send(remote(W.at[0, 0], W.at[0, 8 - d], w2s.at[d - 1], w2r.at[d - 1], at(dz=d)))
    spread_w(0)

    both[h] = group[0:136]
    twin = remote(both.at[h], both.at[h], hs.at[0], hr.at[0], at(dz=4))
    send(twin)

    def come(d):
        ref = W.at[0, 8 - d]
        remote(ref, ref, w2s.at[d - 1], w2r.at[d - 1], at(dz=d)).wait_recv()

    come(7)
    come(6)
    spread_w(1)
    come(1)
    come(2)
    spread_w(2)
    relay_w(0)
    share(1, 3, (1,))
    share(2, 1, (3,))
    for n, group in enumerate(((3, 5), (4,))):
        for d in group:
            come(d)
        for d in (1, 2, 3):
            for i in group:
                j = (3, 5, 4).index(i)
                send(remote(W.at[0, 8 - i], W.at[4 - d, 8 - i], fs.at[j, d - 1], fr.at[j, d - 1], at(dy=d)))
        relay_w(1 + n)

    ref = both.at[1 - h]
    remote(ref, ref, hs.at[0], hr.at[0], at(dz=4)).wait_recv()
    for i in range(4):
        for k in range(2):
            side = slice(128 * k, 128 * k + 128)
            xs[i, 0:32, side] = both[k, 32 * i : 32 * i + 32]
            xs[i, 32:40, side] = both[k, 128:136]
    slot = 2 * x + c
    others = [(dx, dc) for dx in range(4) for dc in range(2) if dx or dc]
    for n, (dx, dc) in enumerate(others):
        send(remote(xs.at[wrap(x + dx, 4)], xr.at[slot], xss.at[n], xrs.at[n], at(dx=dx, dc=dc)))
    xr[slot] = xs[x]
    share(3, 2, (4, 5))

    def block_at(i, j, n):
        return W.at[i, wrap(4 * n + j - z, 8)]

    def accumulate(i, a):
        total = jnp.zeros((256, 256), F32)
        for k in range(2):
            sides = [
                jnp.concatenate([block_at(i, 2 * k + j, n)[0:128] for j in range(2)], axis=0) for n in range(2)
            ]
            right = jnp.concatenate(sides, axis=1)
            start = pl.multiple_of(512 * wrap(y + i, 4) + 256 * k, 128)
            left = TT[a, :, :, pl.ds(start, 256)].reshape(256, 256)
            total += jnp.dot(left, right, preferred_element_type=F32)
        return total

    shared(0, 0)
    shared(1, 3)
    shared(2, 1)
    shared(3, 2)
    settle(before_columns)

    def begin(a, carry):
        acc[a] = accumulate(0, a)
        return carry

    lax.fori_loop(0, 4, begin, 0)
    for i, arrivals in ((3, (1,)), (1, (3,)), (2, (4, 5))):
        for n in range(3):
            for k in arrivals:
                wait_w(n, k)
        for j in range(3):
            ref = W.at[i, (5, 3, 4)[j]]
            remote(ref, ref, fs.at[j, 0], fr.at[j, 3 - i], at(dy=1)).wait_recv()

    ends = jnp.concatenate(
        [
            jnp.concatenate(
                [block_at(wrap(i - y, 4), j, n)[128:144] for i in range(4) for j in range(4)], axis=0
            )
            for n in range(2)
        ],
        axis=1,
    )
    tail = ends[240:256].astype(F32)
    bias_t, scale_t = tail[1:2], tail[2:3]
    columns = list(pending)
    pending.clear()
    out_cols = branch_res.at[:, pl.ds(pl.multiple_of(256 * slot, 128), 256)]
    n = 0
    for d in (2, 1, 3, 0):
        a = d
        total = acc[a] + accumulate(3, a) + accumulate(1, a) + accumulate(2, a) + jnp.dot(
            TT[a, :, :, WIDTH:].reshape(256, 256), ends, preferred_element_type=F32
        )
        OUT[a] = (scale_t * (total + bias_t)).astype(BF16).reshape(2, 128, 256)
        for dc in (1, 0):
            core = wrap(c + dc, 2)
            if d or dc:
                send(remote(OUT.at[a, core], out_cols, os.at[n], orr.at[slot], at(dx=d, dc=dc)))
                n += 1
    stay = pltpu.make_async_copy(OUT.at[0, c], out_cols, own_sem.at[1])
    stay.start()
    settle(columns)

    for n, (dx, dc) in enumerate(others):
        ref = xr.at[2 * wrap(x - dx, 4) + wrap(c - dc, 2)]
        remote(ref, ref, xss.at[n], xrs.at[n], at(dx=dx, dc=dc)).wait_recv()
    last = jnp.where(f == 63, 1.0, 0.0).astype(F32)
    pad[...] = jnp.zeros_like(pad)
    tg[...] = jnp.zeros_like(tg)
    for e in range(8):
        for t in range(2):
            n = 2 * e + t
            pad[n : n + 1] = xr[e, 33:34, 128 * t : 128 * t + 128] * last
            tg[TAIL + 240 + n : TAIL + 241 + n] = xr[e, 34:35, 128 * t : 128 * t + 128] * last
    rolled = roll_by(pad[0:24], place, 1, range(7))
    pad[0:24] = jnp.where(lanes24 >= lane_at, rolled, pltpu.roll(rolled, 1, 0))
    tg[TAIL : TAIL + 256] += roll_by(pad[...], place, 0, range(7, 15))
    lanes = iota((8, 128), 1)
    subs = iota((8, 128), 0)

    def update(where, grad, inside):
        old = master[where]
        new_one = beta_one * one[where] + (1.0 - beta_one) * grad
        new_two = beta_two * two[where] + (1.0 - beta_two) * grad * grad
        first = new_one / (1.0 - beta_one**STEP)
        second = new_two / (1.0 - beta_two**STEP)
        decay = jnp.where(inside, decay_rate, 0.0) * old
        new = old - learn_rate * (first / (jnp.sqrt(second) + epsilon) + decay)
        master_out[where] = new
        one_out[where] = new_one
        two_out[where] = new_two
        teacher_out[where] = ema_rate * teacher[where] + (1.0 - ema_rate) * new

    for b in range(4):
        for m in range(4):
            for t in range(4):
                base = 128 * b + 4 * m + t
                where = (pl.ds(base, 8, stride=16), slice(None))
                e, side = 2 * wrap(x + m, 4) + t // 2, slice(128 * (t % 2), 128 * (t % 2) + 128)
                slots = 128 * base + 2048 * subs + lanes
                update(where, xr[e, 8 * b : 8 * b + 8, side] + tg[where], slots < limit)
    for t in range(4):
        where = (slice(512 + t, 513 + t), slice(None))
        e, side = 2 * x + t // 2, slice(128 * (t % 2), 128 * (t % 2) + 128)
        inside = jnp.full((1, 128), 65536, jnp.int32) < limit
        update(where, xr[e, 32:33, side] * (1.0 - last) + tg[where], inside)
    results = [
        pltpu.make_async_copy(src, dst, res_sem.at[k])
        for k, (src, dst) in enumerate(
            [(master_out, master_res), (one_out, one_res), (two_out, two_res), (teacher_out, teacher_res)]
        )
    ]
    for copy in results:
        copy.start()

    for n, (dx, dc) in enumerate(others):
        e = 2 * wrap(x - dx, 4) + wrap(c - dc, 2)
        ref = branch_res.at[:, pl.ds(pl.multiple_of(256 * e, 128), 256)]
        remote(ref, ref, os.at[n], orr.at[e], at(dc=1)).wait_recv()
    stay.wait()
    for copy in results:
        copy.wait()
    settle(pending)


def copy_kernel(*refs):
    sems = refs[15]
    loads = [pltpu.make_async_copy(refs[k], refs[10 + k], sems.at[k]) for k in range(5)]
    stores = [pltpu.make_async_copy(refs[10 + k], refs[5 + k], sems.at[5 + k]) for k in range(5)]
    for copy in loads:
        copy.start()
    for load, store in zip(loads, stores):
        load.wait()
        store.start()
    for copy in stores:
        copy.wait()


def per_device(
    tokens, cotangent, saved_branch, layer_gain, offsets, master, moment_one, moment_two, teacher, teacher_tokens
):
    anyspace = pl.BlockSpec(memory_space=pl.ANY)
    dma = pltpu.SemaphoreType.DMA
    flat = jax.ShapeDtypeStruct((FLAT, 128), F32)
    shard = pltpu.VMEM((FLAT, 128), F32)
    rows = pltpu.VMEM((128, WIDTH), BF16)
    results = [flat] * 4 + [jax.ShapeDtypeStruct((128, WIDTH), BF16)]
    outs = pl.pallas_call(
        kernel,
        out_shape=results,
        in_specs=[pl.BlockSpec(memory_space=pltpu.SMEM)] + [anyspace] * 9,
        out_specs=[anyspace] * 5,
        scratch_shapes=[
            pltpu.VMEM((1, WIDTH), F32),
            rows, rows, rows, rows,
            shard, shard, shard, shard, shard, shard, shard, shard, shard,
            pltpu.VMEM((4, 128, 512), BF16),
            pltpu.VMEM((4, 4, 128, 512), BF16),
            pltpu.VMEM((4, 4, 128, 512), BF16),
            pltpu.VMEM((4, 16, 512), BF16),
            pltpu.VMEM((4, 16, 512), BF16),
            pltpu.VMEM((4, 16, 512), BF16),
            pltpu.VMEM((528, 512), F32),
            pltpu.VMEM((4, GROUP, 512), BF16),
            pltpu.VMEM((4, GROUP, 256), BF16),
            pltpu.VMEM((8, GROUP, 128), BF16),
            pltpu.VMEM((8, GROUP, 128), BF16),
            pltpu.VMEM((4, 3, 40, 128), F32),
            pltpu.VMEM((4, 3, 40, 128), F32),
            pltpu.VMEM((2, 136, 128), F32),
            pltpu.VMEM((4, 40, 256), F32),
            pltpu.VMEM((8, 40, 256), F32),
            pltpu.VMEM((256, 128), F32),
            pltpu.VMEM((520, 128), F32),
            pltpu.VMEM((4, 2, 128, WIDTH + 256), BF16),
            pltpu.VMEM((4, 8, GROUP, 128), BF16),
            pltpu.VMEM((4, 256, 256), F32),
            pltpu.VMEM((4, 2, 128, 256), BF16),
            dma((9,)), dma((4,)), dma((2,)),
            dma((3,)), dma((3,)), dma((3,)), dma((3,)), dma((3,)), dma((3,)), dma((3,)), dma((3,)),
            dma((2, 6)), dma((2, 6)), dma((2, 6)), dma((2, 6)),
            dma((4,)), dma((4,)), dma((7,)), dma((7,)),
            dma((3,)), dma((3,)), dma((7,)), dma((7,)),
            dma((1, 6)), dma((1, 6)), dma((4,)), dma((4,)), dma((7,)), dma((7,)), dma((3, 6)), dma((3, 6)),
            dma((1,)), dma((1,)), dma((3, 3)), dma((3, 3)),
            dma((7,)), dma((8,)),
        ],
        compiler_params=pltpu.CompilerParams(collective_id=0, has_side_effects=True, vmem_limit_bytes=56 << 20),
        name="step",
    )(
        offsets, layer_gain.reshape(1, WIDTH), tokens, cotangent, saved_branch,
        *[a.reshape(FLAT, 128) for a in (master, moment_one, moment_two, teacher)], teacher_tokens,
    )
    outs = pl.pallas_call(
        copy_kernel,
        out_shape=results,
        in_specs=[anyspace] * 5,
        out_specs=[anyspace] * 5,
        scratch_shapes=[shard, shard, shard, shard, rows, dma((10,))],
        name="place",
    )(*outs)
    return tuple(a.reshape(SHARD) for a in outs[:4]) + (outs[4],)


def solution(mesh):
    rows = P(("fsdp", "dp"), None)
    return jax.shard_map(
        per_device,
        mesh=mesh,
        in_specs=(rows, rows, rows, P(), P(), P("fsdp"), P("fsdp"), P("fsdp"), P("fsdp"), rows),
        out_specs=(P("fsdp"), P("fsdp"), P("fsdp"), P("fsdp"), rows),
        check_vma=False,
    )
```
